32 devices in a mesh: band: 4 (over x, core), span: 8 (over z, y).
Axes of the slice: x: 2, y: 2, z: 4, core: 2. Of those that a mesh axis runs over, the one named last changes fastest.
Arguments:
- gases: bfloat16 [7, 32, 16384], P(None, None, ('band', 'span')), may hold values from 0 to 1
- pressure_bin: int32 [32, 16384], P(None, ('band', 'span')), may hold values from 0 to 59
- layer_mass: bfloat16 [32, 16384], P(None, ('band', 'span')), may hold values from 0.5 to 2
- cos_zenith: bfloat16 [16384], P(('band', 'span')), may hold values from 0.19921875 to 1
- surface_albedo: bfloat16 [16384], P(('band', 'span')), may hold values from 0.049804688 to 0.8984375
- column_order: int32 [16384], P(('band', 'span')), may hold values from 0 to 511, as said below
- sunlit: int32 [128], P(('band', 'span')), may hold values from 0 to 1, as said below
- absorption: bfloat16 [112, 7, 60], replicated, may hold values from 9.9658966e-05 to 0.099609375
- scattering: bfloat16 [112, 60], replicated, may hold values from 0.19921875 to 0.94921875
Outputs:
- heating: float32 [32, 16384], P(None, ('band', 'span'))
The draws below stay inside these ranges and needn't reach their ends.
Inputs may be any that keep to these rules, and one draw needn't show every extreme that they name: `column_order`: the 512 entries of each device's slice are a permutation of 0 to 511. The 4 devices with the same index along the second mesh axis hold 8 sunlit blocks together; among them one device has all 4 blocks sunlit and one has none.
All inputs are finite; a program needn't handle non-finite values.
Results may differ from the reference program's by a relative error of at most 0.0003.
Values may be sent and summed in bfloat16 or wider, within the bound.
No kernel may reach another device: no remote copies, remote signals or barrier semaphores. Data moves between devices by JAX's collectives and lax.ppermute only.
A program may use at most 64 MiB of HBM per device.

```python
import math
import jax
import jax.numpy as jnp
from jax import lax

G = 112
NGAS = 7
K = 60
L = 32
BLK = 128
NB = 4
C_DEV = 512
COLS = 16384
N_BAND = 4
N_SPAN = 8


def draw_column_order(key, part):
    device_count = COLS // C_DEV
    device_keys = jax.random.split(key, device_count)
    orders = jax.vmap(lambda device_key: jax.random.permutation(device_key, C_DEV))(device_keys)
    return orders.reshape(-1).astype(jnp.int32)


def draw_sunlit(key, part):

    def one_group(group_key):
        keys = jax.random.split(group_key, 4)
        counts = jnp.zeros((N_BAND,), jnp.int32).at[0].set(NB)
        if N_BAND > 2:
            values = jax.random.randint(keys[0], ((N_BAND - 2) // 2,), 0, NB + 1).astype(jnp.int32)
            middle = jnp.concatenate([values, NB - values])
            counts = counts.at[1:N_BAND - 1].set(middle)
            unit_moves = jax.random.randint(keys[1], (2 * N_BAND, 2), 1, N_BAND - 1)
            for move_index in range(2 * N_BAND):
                giver_slot = unit_moves[move_index, 0]
                taker_slot = unit_moves[move_index, 1]
                allowed = ((counts[giver_slot] > 0) & (counts[taker_slot] < NB) & (giver_slot != taker_slot)).astype(jnp.int32)
                counts = counts.at[giver_slot].add(-allowed).at[taker_slot].add(allowed)
        placed = jnp.zeros_like(counts).at[jax.random.permutation(keys[2], N_BAND)].set(counts)
        block_keys = jax.random.split(keys[3], N_BAND)
        shuffled = jax.vmap(lambda block_key: jax.random.permutation(block_key, NB))(block_keys)
        return (shuffled < placed[:, None]).astype(jnp.int32)
    group_keys = jax.random.split(key, N_SPAN)
    flags = jax.vmap(one_group)(group_keys)
    return jnp.transpose(flags, (1, 0, 2)).reshape(-1).astype(jnp.int32)


def plant(values, stream_key, smallest, largest):
    extent = values.shape
    place = [jax.random.randint(jax.random.fold_in(stream_key, axis), (), 0, extent[axis]) for axis in range(len(extent))]
    values = values.at[tuple(place)].set(smallest)
    longest = extent.index(max(extent))
    place[longest] = (place[longest] + 1) % extent[longest]
    return values.at[tuple(place)].set(largest)


def level_of(own_key, shape, cuts, smallest, top_value):
    def one(axis_at, shards_of):
        heights = jax.random.uniform(jax.random.fold_in(jax.random.fold_in(own_key, 6), axis_at), (shards_of,), jnp.float32, smallest / len(cuts), top_value / len(cuts))
        return jnp.repeat(jnp.exp(heights), shape[axis_at] // shards_of).reshape((-1,) + (1,) * (len(shape) - axis_at - 1))

    factor_of = one(*cuts[0])
    for cut in cuts[1:]:
        factor_of = factor_of * one(*cut)
    return factor_of


def setup_inputs(seed: int = 0) -> dict:
    key_of = jax.random.split(jax.random.key(seed), 10)
    return {
        "gases": jnp.clip(1.0 * jax.random.uniform(key_of[0], (NGAS, L, COLS), jnp.float32) ** level_of(key_of[0], (NGAS, L, COLS), ((2, 32),), -0.2, 0.2), 0.0, 1.0).astype(jnp.bfloat16),
        "pressure_bin": plant(jax.random.randint(key_of[1], (L, COLS), 0, K), jax.random.fold_in(key_of[1], 1), 0, K - 1).astype(jnp.int32),
        "layer_mass": jnp.clip(jnp.exp(math.log(2.0) - 1.3862944 * jax.random.uniform(key_of[2], (L, COLS), jnp.float32) ** level_of(key_of[2], (L, COLS), ((1, 32),), -0.2, 0.2)), 0.5, 2.0).astype(jnp.bfloat16),
        "cos_zenith": jnp.clip(0.19921875 + 0.80078125 * jax.random.uniform(key_of[3], (COLS,), jnp.float32) ** level_of(key_of[3], (COLS,), ((0, 32),), -0.2, 0.2), 0.19921875, 1.0).astype(jnp.bfloat16),
        "surface_albedo": jnp.clip(0.049804688 + 0.8486328 * jax.random.uniform(key_of[4], (COLS,), jnp.float32) ** level_of(key_of[4], (COLS,), ((0, 32),), -0.2, 0.2), 0.049804688, 0.8984375).astype(jnp.bfloat16),
        "column_order": draw_column_order(jax.random.fold_in(key_of[9], 71), 0),
        "sunlit": draw_sunlit(jax.random.fold_in(key_of[9], 71), 0),
        "absorption": jnp.clip(jnp.exp(jax.random.uniform(key_of[7], (G, NGAS, K), jnp.float32, math.log(9.965896606445312e-05), math.log(0.099609375))), 9.965896606445312e-05, 0.099609375).astype(jnp.bfloat16),
        "scattering": jnp.clip(jax.random.uniform(key_of[8], (G, K), jnp.float32, 0.19921875, 0.94921875), 0.19921875, 0.94921875).astype(jnp.bfloat16),
    }


def column_heating(amounts, bin_index, thickness, cosine, ground, absorption, scattering):
    selector = (bin_index[None] == jnp.arange(K, dtype=jnp.int32)[:, None, None]).astype(jnp.bfloat16)
    weighted = amounts[:, None] * selector[None]
    optical_depth = jnp.einsum("gak,akln->lgn", absorption.astype(jnp.float32), weighted.astype(jnp.float32))
    albedo = jnp.einsum("gk,kln->lgn", scattering.astype(jnp.float32), selector.astype(jnp.float32))
    column_path = jnp.cumsum(optical_depth, axis=0)
    column_path = jnp.concatenate([jnp.zeros_like(column_path[:1]), column_path], axis=0)
    direct = cosine * jnp.exp(-column_path / cosine)
    fading = jnp.exp(-1.66 * optical_depth)
    reflect = 0.5 * albedo * (1.0 - fading)
    transmit = fading + reflect
    source = 0.5 * albedo * (direct[:-1] - direct[1:])

    def upward(state_pair, layer):
        refl_below, source_below = state_pair
        layer_reflect, layer_transmit, layer_source = layer
        denominator = 1.0 - layer_reflect * refl_below
        refl_top = layer_reflect + layer_transmit * layer_transmit * refl_below / denominator
        source_top = layer_source + layer_transmit * (source_below + refl_below * layer_source) / denominator
        return (refl_top, source_top), (refl_top, source_top)

    floor_refl = jnp.broadcast_to(ground, reflect.shape[1:])
    floor_source = ground * direct[-1]
    final_pair, tops = lax.scan(upward, (floor_refl, floor_source), (reflect, transmit, source), reverse=True)
    refl_all = jnp.concatenate([tops[0], floor_refl[None]], axis=0)
    source_all = jnp.concatenate([tops[1], floor_source[None]], axis=0)

    def downward(diffuse, layer):
        layer_reflect, layer_transmit, layer_source, refl_low, source_low = layer
        denominator = 1.0 - layer_reflect * refl_low
        diffuse = (layer_transmit * diffuse + layer_reflect * source_low + layer_source) / denominator
        return diffuse, diffuse

    start_diffuse = jnp.zeros_like(floor_refl)
    final_diffuse, lower = lax.scan(downward, start_diffuse, (reflect, transmit, source, refl_all[1:], source_all[1:]))
    diffuse_all = jnp.concatenate([start_diffuse[None], lower], axis=0)
    net = direct + diffuse_all - (refl_all * diffuse_all + source_all)
    return jnp.sum(net[:-1] - net[1:], axis=1) / thickness


def reference(gases, pressure_bin, layer_mass, cos_zenith, surface_albedo, column_order, sunlit, absorption, scattering):
    device_count = N_BAND * N_SPAN
    per_peer = C_DEV // N_SPAN

    def split(array):
        return jnp.moveaxis(array.reshape(array.shape[:-1] + (device_count, C_DEV)), -2, 0)

    def per_device(inputs):
        amounts, bin_index, thickness, cosine, ground = inputs
        return column_heating(amounts, bin_index, thickness.astype(jnp.float32), cosine.astype(jnp.float32), ground.astype(jnp.float32), absorption, scattering)

    heating = lax.map(per_device, (split(gases), split(pressure_bin), split(layer_mass), split(cos_zenith), split(surface_albedo)))
    block_flag = jnp.repeat(sunlit, BLK).reshape(N_BAND, N_SPAN, N_SPAN, per_peer)
    at_order = jnp.transpose(block_flag, (0, 2, 1, 3)).reshape(device_count, C_DEV)
    ordering = column_order.reshape(device_count, C_DEV)
    dyn_flag = jax.vmap(lambda order_row, flag_row: jnp.zeros((C_DEV,), jnp.int32).at[order_row].set(flag_row))(ordering, at_order)
    heating = heating * dyn_flag[:, None, :].astype(jnp.float32)
    return jnp.moveaxis(heating, 0, 1).reshape(L, device_count * C_DEV)
```

```python
import functools
import math

import jax
import jax.numpy as jnp
from jax import lax
from jax.experimental import pallas as pl
from jax.experimental.pallas import tpu as pltpu
from jax.sharding import PartitionSpec as P

LANES = 128
ROWS = 8
TILE = 256
STEP = 4
HALVES = 2
BIN_ROWS = 64
LOG2E = math.log2(math.e)


def invert(x):
    guess = pl.reciprocal(x, approx=True)
    return guess * (2.0 - x * guess)


def heating_kernel(
    per_peer,
    gases_ref,
    bins_ref,
    mass_ref,
    cosine_ref,
    ground_ref,
    order_ref,
    table_ref,
    scatter_ref,
    heat_ref,
    owner_ref,
    gas_buf,
    slope_buf,
    tau_even,
    tau_odd,
    half_even,
    half_odd,
    up_buf,
    rise_buf,
    pass_buf,
    refl_buf,
    fall_buf,
    direct_buf,
    gain_buf,
    net_buf,
):
    gas_count, levels, columns = gases_ref.shape
    points = table_ref.shape[0]
    half = points // HALVES
    vregs = half // ROWS
    groups = levels // STEP
    blocks = columns // LANES
    tiles = columns // TILE

    for gas in range(gas_count):
        gas_buf[gas] = gases_ref[gas].astype(jnp.float32)
    cosine = jnp.broadcast_to(cosine_ref[...].astype(jnp.float32), (ROWS, columns))
    slope_buf[...] = (-LOG2E) / cosine

    def optical(layer, tile, tau_ref, half_ref, slot):
        cols = slice(tile * TILE, (tile + 1) * TILE)
        spread = (BIN_ROWS, TILE)
        bins = jnp.broadcast_to(bins_ref[pl.ds(layer, 1), cols], spread)
        hit = bins == lax.broadcasted_iota(jnp.int32, spread, 0)
        selector = jnp.where(hit, 1.0, 0.0).astype(jnp.bfloat16)
        parts = []
        for gas in range(gas_count):
            amount = jnp.broadcast_to(gas_buf[gas, pl.ds(layer, 1), cols], (16, TILE)).astype(jnp.bfloat16)
            amount = jnp.concatenate([amount] * (BIN_ROWS // 16), axis=0)
            parts.append(amount * selector)
        weighted = jnp.concatenate(parts, axis=0)
        tau_ref[slot, :, cols] = jnp.dot(table_ref[...], weighted, preferred_element_type=jnp.float32)
        half_ref[slot, :, cols] = jnp.dot(scatter_ref[...], selector, preferred_element_type=jnp.float32)

    def advance(first, slots, chunk, tau_ref, half_ref):
        block, part = divmod(chunk, HALVES)
        cols = slice(block * LANES, (block + 1) * LANES)
        rows = slice(part * half, (part + 1) * half)
        shape = (vregs, ROWS, LANES)
        slope = slope_buf[:, cols]
        refl = refl_buf[rows, cols].reshape(shape)
        fall = fall_buf[rows, cols].reshape(shape)
        direct = direct_buf[rows, cols].reshape(shape)
        for slot in range(slots):
            layer = first + slot
            tau = tau_ref[slot, rows, cols].reshape(shape)
            half_albedo = half_ref[slot, rows, cols].reshape(shape)
            fading = jnp.exp2(tau * (-1.66 * LOG2E))
            passed = jnp.exp2(tau * slope)
            reflect = half_albedo * (1.0 - fading)
            transmit = fading + reflect
            below = direct * passed
            source = half_albedo * (direct - below)
            pass_buf[layer, rows, cols] = (1.0 - refl).reshape(half, LANES)
            inverse = invert(1.0 - reflect * refl)
            up = transmit * inverse
            rise = (reflect * fall + source) * inverse
            up_buf[layer, rows, cols] = up.reshape(half, LANES)
            rise_buf[layer, rows, cols] = rise.reshape(half, LANES)
            fall = source + transmit * (fall + refl * rise)
            refl = reflect + transmit * (refl * up)
            direct = below
            gain_buf[part, layer + 1, :, cols] = jnp.sum(direct + fall, axis=0)
        refl_buf[rows, cols] = refl.reshape(half, LANES)
        fall_buf[rows, cols] = fall.reshape(half, LANES)
        direct_buf[rows, cols] = direct.reshape(half, LANES)

    refl_buf[...] = jnp.zeros_like(refl_buf)
    fall_buf[...] = jnp.zeros_like(fall_buf)
    direct_buf[...] = jnp.broadcast_to(cosine[:1], direct_buf.shape)
    for part in range(HALVES):
        gain_buf[part, 0] = cosine * float(vregs)

    work = [(slot, tile) for slot in range(STEP) for tile in range(tiles)]
    for slot, tile in work:
        optical(slot, tile, tau_even, half_even, slot)

    chunks = blocks * HALVES

    def down_pair(pair, carry):
        first = pair * (2 * STEP)
        following = jnp.minimum(first + 2 * STEP, levels - STEP)
        for chunk in range(chunks):
            for slot, tile in work[chunk * len(work) // chunks:(chunk + 1) * len(work) // chunks]:
                optical(first + STEP + slot, tile, tau_odd, half_odd, slot)
            advance(first, STEP, chunk, tau_even, half_even)
        for chunk in range(chunks):
            for slot, tile in work[chunk * len(work) // chunks:(chunk + 1) * len(work) // chunks]:
                optical(following + slot, tile, tau_even, half_even, slot)
            advance(first + STEP, STEP, chunk, tau_odd, half_odd)
        return carry

    lax.fori_loop(0, groups // 2, down_pair, 0)

    ground = jnp.broadcast_to(ground_ref[...].astype(jnp.float32), (ROWS, columns))
    for block in range(blocks):
        cols = slice(block * LANES, (block + 1) * LANES)
        shape = (points // ROWS, ROWS, LANES)
        albedo = ground[:, cols]
        refl = refl_buf[:, cols].reshape(shape)
        arriving = (fall_buf[:, cols] + direct_buf[:, cols]).reshape(shape)
        rising = albedo * arriving / (1.0 - albedo * refl)
        fall_buf[:, cols] = rising.reshape(points, LANES)
        taken = jnp.sum(rising * (1.0 - refl), axis=0)
        total = gain_buf[0, levels, :, cols]
        for part in range(1, HALVES):
            total = total + gain_buf[part, levels, :, cols]
        net_buf[levels, :, cols] = total - taken

    def up_group(index, carry):
        last = levels - 1 - index * STEP
        for block in range(blocks):
            cols = slice(block * LANES, (block + 1) * LANES)
            shape = (points // ROWS, ROWS, LANES)
            rising = fall_buf[:, cols].reshape(shape)
            for slot in range(STEP):
                layer = last - slot
                rising = up_buf[layer, :, cols].reshape(shape) * rising + rise_buf[layer, :, cols].reshape(shape)
                taken = jnp.sum(rising * pass_buf[layer, :, cols].reshape(shape), axis=0)
                total = gain_buf[0, layer, :, cols]
                for part in range(1, HALVES):
                    total = total + gain_buf[part, layer, :, cols]
                net_buf[layer, :, cols] = total - taken
            fall_buf[:, cols] = rising.reshape(points, LANES)
        return carry

    lax.fori_loop(0, groups, up_group, 0)

    heat = jnp.sum(net_buf[:levels] - net_buf[1:], axis=1)
    heat_ref[...] = heat / mass_ref[...].astype(jnp.float32)

    spread = (columns, columns)
    order = jnp.broadcast_to(order_ref[...], spread)
    match = jnp.where(order == lax.broadcasted_iota(jnp.int32, spread, 0), 1.0, 0.0).astype(jnp.bfloat16)
    place = lax.broadcasted_iota(jnp.int32, (ROWS, columns), 1)
    group = (place // per_peer).astype(jnp.float32).astype(jnp.bfloat16)
    owner = lax.dot_general(group, match, (((1,), (1,)), ((), ())), preferred_element_type=jnp.float32)
    owner_ref[...] = owner.astype(jnp.int32)


def local(
    gases,
    pressure_bin,
    layer_mass,
    cos_zenith,
    surface_albedo,
    column_order,
    sunlit,
    absorption,
    scattering,
):
    group_size = lax.axis_size("span")
    me = lax.axis_index("span")
    gas_count, levels, columns = gases.shape
    points, _, bins = absorption.shape
    table = jnp.pad(absorption, ((0, 0), (0, 0), (0, BIN_ROWS - bins))).reshape(points, gas_count * BIN_ROWS)
    scatter = jnp.pad(0.5 * scattering, ((0, 0), (0, BIN_ROWS - bins)))
    flags = lax.all_gather(sunlit, "span", axis=0, tiled=False)
    field = pltpu.VMEM((levels, points, columns), jnp.float32)
    staged = pltpu.VMEM((STEP, points, columns), jnp.float32)
    state = pltpu.VMEM((points, columns), jnp.float32)
    heat, owner = pl.pallas_call(
        functools.partial(heating_kernel, columns // group_size),
        out_shape=(
            jax.ShapeDtypeStruct((levels, columns), jnp.float32),
            jax.ShapeDtypeStruct((ROWS, columns), jnp.int32),
        ),
        in_specs=[pl.BlockSpec(memory_space=pltpu.VMEM)] * 8,
        out_specs=(pl.BlockSpec(memory_space=pltpu.VMEM),) * 2,
        scratch_shapes=[
            pltpu.VMEM(gases.shape, jnp.float32),
            pltpu.VMEM((ROWS, columns), jnp.float32),
            staged,
            staged,
            staged,
            staged,
            field,
            field,
            field,
            state,
            state,
            state,
            pltpu.VMEM((HALVES, levels + 1, ROWS, columns), jnp.float32),
            pltpu.VMEM((levels + 1, ROWS, columns), jnp.float32),
        ],
        compiler_params=pltpu.CompilerParams(vmem_limit_bytes=48 * 1024 * 1024),
    )(
        gases,
        pressure_bin,
        layer_mass,
        cos_zenith.reshape(1, columns),
        surface_albedo.reshape(1, columns),
        column_order.reshape(1, columns),
        table,
        scatter,
    )
    per_peer = columns // group_size
    block_cols = columns // sunlit.shape[0]
    mine = lax.dynamic_index_in_dim(flags, me * per_peer // block_cols, axis=1, keepdims=False)
    lit = jnp.sum(jnp.where(owner[0][None] == jnp.arange(group_size, dtype=jnp.int32)[:, None], mine[:, None], 0), axis=0)
    return heat * lit.astype(jnp.float32)


def solution(mesh):
    placed = (
        P(None, None, ("band", "span")),
        P(None, ("band", "span")),
        P(None, ("band", "span")),
        P(("band", "span")),
        P(("band", "span")),
        P(("band", "span")),
        P(("band", "span")),
        P(),
        P(),
    )
    return jax.shard_map(
        local, mesh=mesh, in_specs=placed, out_specs=P(None, ("band", "span")), check_vma=False
    )
```

```python
import functools
import math

import jax
import jax.numpy as jnp
from jax import lax
from jax.experimental import pallas as pl
from jax.experimental.pallas import tpu as pltpu
from jax.sharding import PartitionSpec as P

LANES = 128
ROWS = 8
TILE = 256
STEP = 4
HALVES = 2
BIN_ROWS = 64
LOG2E = math.log2(math.e)


def invert(x):
    return pl.reciprocal(x, approx=True)


def heating_kernel(
    per_peer,
    gases_hbm,
    bins_hbm,
    mass_hbm,
    cosine_hbm,
    ground_hbm,
    order_hbm,
    absorb_hbm,
    scatter_hbm,
    heat_ref,
    owner_ref,
    gases_ref,
    bins_ref,
    mass_ref,
    cosine_ref,
    ground_ref,
    order_ref,
    absorb_ref,
    albedo_ref,
    copied,
    wide_buf,
    table_ref,
    scatter_ref,
    gas_buf,
    slope_buf,
    tau_even,
    tau_odd,
    half_even,
    half_odd,
    up_buf,
    rise_buf,
    pass_buf,
    refl_buf,
    fall_buf,
    direct_buf,
    gain_buf,
    net_buf,
):
    gas_count, levels, columns = gases_ref.shape
    points = table_ref.shape[0]
    half = points // HALVES
    vregs = half // ROWS
    groups = levels // STEP
    blocks = columns // LANES
    tiles = columns // TILE

    copies = [
        pltpu.make_async_copy(source, target, copied.at[place])
        for place, (source, target) in enumerate(
            (
                (absorb_hbm, absorb_ref),
                (scatter_hbm, albedo_ref),
                (cosine_hbm, cosine_ref),
                (bins_hbm, bins_ref),
                (gases_hbm, gases_ref),
                (ground_hbm, ground_ref),
                (order_hbm, order_ref),
                (mass_hbm, mass_ref),
            )
        )
    ]
    for copy in copies:
        copy.start()
    refl_buf[...] = jnp.zeros_like(refl_buf)
    fall_buf[...] = jnp.zeros_like(fall_buf)
    wide_buf[...] = jnp.zeros_like(wide_buf)
    for copy in copies:
        copy.wait()

    for gas in range(gas_count):
        wide_buf[gas * BIN_ROWS : gas * BIN_ROWS + absorb_ref.shape[1], :points] = absorb_ref[gas].astype(jnp.float32)
    first_row = gas_count * BIN_ROWS
    wide_buf[first_row : first_row + absorb_ref.shape[1], :points] = 0.5 * albedo_ref[...].astype(jnp.float32)
    turned = [
        jnp.transpose(wide_buf[i * LANES : (i + 1) * LANES])[:points].astype(jnp.bfloat16)
        for i in range(wide_buf.shape[0] // LANES)
    ]
    whole = jnp.concatenate(turned, axis=1)
    table_ref[...] = whole[:, :first_row]
    scatter_ref[...] = whole[:, first_row : first_row + BIN_ROWS]
    for gas in range(gas_count):
        gas_buf[gas] = gases_ref[gas].astype(jnp.float32)
    cosine = jnp.broadcast_to(cosine_ref[...].astype(jnp.float32).reshape(1, columns), (ROWS, columns))
    slope_buf[...] = (-LOG2E) / cosine

    def optical(layer, tile, tau_ref, half_ref, slot):
        cols = slice(tile * TILE, (tile + 1) * TILE)
        spread = (BIN_ROWS, TILE)
        bins = jnp.broadcast_to(bins_ref[pl.ds(layer, 1), cols], spread)
        hit = bins == lax.broadcasted_iota(jnp.int32, spread, 0)
        selector = jnp.where(hit, 1.0, 0.0).astype(jnp.bfloat16)
        parts = []
        for gas in range(gas_count):
            amount = jnp.broadcast_to(gas_buf[gas, pl.ds(layer, 1), cols], (16, TILE)).astype(jnp.bfloat16)
            amount = jnp.concatenate([amount] * (BIN_ROWS // 16), axis=0)
            parts.append(amount * selector)
        weighted = jnp.concatenate(parts, axis=0)
        tau_ref[slot, :, cols] = jnp.dot(table_ref[...], weighted, preferred_element_type=jnp.float32)
        half_ref[slot, :, cols] = jnp.dot(scatter_ref[...], selector, preferred_element_type=jnp.float32)

    def advance(first, slots, chunk, tau_ref, half_ref):
        block, part = divmod(chunk, HALVES)
        cols = slice(block * LANES, (block + 1) * LANES)
        rows = slice(part * half, (part + 1) * half)
        shape = (vregs, ROWS, LANES)
        slope = slope_buf[:, cols]
        refl = refl_buf[rows, cols].reshape(shape)
        fall = fall_buf[rows, cols].reshape(shape)
        direct = direct_buf[rows, cols].reshape(shape)
        for slot in range(slots):
            layer = first + slot
            tau = tau_ref[slot, rows, cols].reshape(shape)
            half_albedo = half_ref[slot, rows, cols].reshape(shape)
            fading = jnp.exp2(tau * (-1.66 * LOG2E))
            passed = jnp.exp2(tau * slope)
            reflect = half_albedo * (1.0 - fading)
            transmit = fading + reflect
            below = direct * passed
            source = half_albedo * (direct - below)
            pass_buf[layer, rows, cols] = (1.0 - refl).reshape(half, LANES)
            inverse = invert(1.0 - reflect * refl)
            up = transmit * inverse
            rise = (reflect * fall + source) * inverse
            up_buf[layer, rows, cols] = up.reshape(half, LANES)
            rise_buf[layer, rows, cols] = rise.reshape(half, LANES)
            fall = source + transmit * (fall + refl * rise)
            refl = reflect + transmit * (refl * up)
            direct = below
            gain_buf[part, layer + 1, :, cols] = jnp.sum(direct + fall, axis=0)
        refl_buf[rows, cols] = refl.reshape(half, LANES)
        fall_buf[rows, cols] = fall.reshape(half, LANES)
        direct_buf[rows, cols] = direct.reshape(half, LANES)

    direct_buf[...] = jnp.broadcast_to(cosine[:1], direct_buf.shape)
    for part in range(HALVES):
        gain_buf[part, 0] = cosine * float(vregs)

    work = [(slot, tile) for slot in range(STEP) for tile in range(tiles)]
    for slot, tile in work:
        optical(slot, tile, tau_even, half_even, slot)

    chunks = blocks * HALVES

    def down_pair(pair, carry):
        first = pair * (2 * STEP)
        following = jnp.minimum(first + 2 * STEP, levels - STEP)
        for chunk in range(chunks):
            for slot, tile in work[chunk * len(work) // chunks:(chunk + 1) * len(work) // chunks]:
                optical(first + STEP + slot, tile, tau_odd, half_odd, slot)
            advance(first, STEP, chunk, tau_even, half_even)
        for chunk in range(chunks):
            for slot, tile in work[chunk * len(work) // chunks:(chunk + 1) * len(work) // chunks]:
                optical(following + slot, tile, tau_even, half_even, slot)
            advance(first + STEP, STEP, chunk, tau_odd, half_odd)
        return carry

    lax.fori_loop(0, groups // 2, down_pair, 0)

    ground = jnp.broadcast_to(ground_ref[...].astype(jnp.float32).reshape(1, columns), (ROWS, columns))
    for block in range(blocks):
        cols = slice(block * LANES, (block + 1) * LANES)
        shape = (points // ROWS, ROWS, LANES)
        albedo = ground[:, cols]
        refl = refl_buf[:, cols].reshape(shape)
        arriving = (fall_buf[:, cols] + direct_buf[:, cols]).reshape(shape)
        rising = albedo * arriving / (1.0 - albedo * refl)
        fall_buf[:, cols] = rising.reshape(points, LANES)
        taken = jnp.sum(rising * (1.0 - refl), axis=0)
        total = gain_buf[0, levels, :, cols]
        for part in range(1, HALVES):
            total = total + gain_buf[part, levels, :, cols]
        net_buf[levels, :, cols] = total - taken

    def up_group(index, carry):
        last = levels - 1 - index * STEP
        for block in range(blocks):
            cols = slice(block * LANES, (block + 1) * LANES)
            shape = (points // ROWS, ROWS, LANES)
            rising = fall_buf[:, cols].reshape(shape)
            for slot in range(STEP):
                layer = last - slot
                rising = up_buf[layer, :, cols].reshape(shape) * rising + rise_buf[layer, :, cols].reshape(shape)
                taken = jnp.sum(rising * pass_buf[layer, :, cols].reshape(shape), axis=0)
                total = gain_buf[0, layer, :, cols]
                for part in range(1, HALVES):
                    total = total + gain_buf[part, layer, :, cols]
                net_buf[layer, :, cols] = total - taken
            fall_buf[:, cols] = rising.reshape(points, LANES)
        return carry

    lax.fori_loop(0, groups, up_group, 0)

    heat = jnp.sum(net_buf[:levels] - net_buf[1:], axis=1)
    heat_ref[...] = heat / mass_ref[...].astype(jnp.float32)

    spread = (columns, columns)
    order = jnp.broadcast_to(order_ref[...], spread)
    match = jnp.where(order == lax.broadcasted_iota(jnp.int32, spread, 0), 1.0, 0.0).astype(jnp.bfloat16)
    place = lax.broadcasted_iota(jnp.int32, (ROWS, columns), 1)
    group = (place // per_peer).astype(jnp.float32).astype(jnp.bfloat16)
    owner = lax.dot_general(group, match, (((1,), (1,)), ((), ())), preferred_element_type=jnp.float32)
    owner_ref[...] = owner.astype(jnp.int32)


def local(
    gases,
    pressure_bin,
    layer_mass,
    cos_zenith,
    surface_albedo,
    column_order,
    sunlit,
    absorption,
    scattering,
):
    group_size = lax.axis_size("span")
    me = lax.axis_index("span")
    gas_count, levels, columns = gases.shape
    points, _, bins = absorption.shape
    ring = [
        lax.ppermute(sunlit, "span", [(i, (i + hop) % group_size) for i in range(group_size)])
        for hop in range(1, group_size)
    ]
    field = pltpu.VMEM((levels, points, columns), jnp.float32)
    staged = pltpu.VMEM((STEP, points, columns), jnp.float32)
    state = pltpu.VMEM((points, columns), jnp.float32)
    heat, owner = pl.pallas_call(
        functools.partial(heating_kernel, columns // group_size),
        out_shape=(
            jax.ShapeDtypeStruct((levels, columns), jnp.float32),
            jax.ShapeDtypeStruct((ROWS, columns), jnp.int32),
        ),
        in_specs=[pl.BlockSpec(memory_space=pltpu.HBM)] * 8,
        out_specs=(pl.BlockSpec(memory_space=pltpu.VMEM),) * 2,
        scratch_shapes=[
            pltpu.VMEM(gases.shape, gases.dtype),
            pltpu.VMEM(pressure_bin.shape, pressure_bin.dtype),
            pltpu.VMEM(layer_mass.shape, layer_mass.dtype),
            pltpu.VMEM(cos_zenith.shape, cos_zenith.dtype),
            pltpu.VMEM(surface_albedo.shape, surface_albedo.dtype),
            pltpu.VMEM((1, columns), column_order.dtype),
            pltpu.VMEM((gas_count, bins, points), absorption.dtype),
            pltpu.VMEM((bins, points), scattering.dtype),
            pltpu.SemaphoreType.DMA((8,)),
            pltpu.VMEM((-(-(gas_count + 1) * BIN_ROWS // LANES) * LANES, LANES), jnp.float32),
            pltpu.VMEM((points, gas_count * BIN_ROWS), jnp.bfloat16),
            pltpu.VMEM((points, BIN_ROWS), jnp.bfloat16),
            pltpu.VMEM(gases.shape, jnp.float32),
            pltpu.VMEM((ROWS, columns), jnp.float32),
            staged,
            staged,
            staged,
            staged,
            field,
            field,
            field,
            state,
            state,
            state,
            pltpu.VMEM((HALVES, levels + 1, ROWS, columns), jnp.float32),
            pltpu.VMEM((levels + 1, ROWS, columns), jnp.float32),
        ],
        compiler_params=pltpu.CompilerParams(vmem_limit_bytes=48 * 1024 * 1024),
        cost_estimate=pl.CostEstimate(
            flops=40 * levels * points * columns, bytes_accessed=1 << 20, transcendentals=3 * levels * points * columns
        ),
    )(
        gases,
        pressure_bin,
        layer_mass,
        cos_zenith,
        surface_albedo,
        column_order.reshape(1, columns),
        jnp.transpose(absorption, (1, 2, 0)),
        jnp.transpose(scattering),
    )
    place = me * (columns // group_size) // (columns // sunlit.shape[0])
    flags = lax.dynamic_index_in_dim(jnp.stack([sunlit] + ring), place, axis=1, keepdims=False)
    hops = lax.rem(me - owner[0] + group_size, group_size)
    lit = jnp.sum(jnp.where(hops[None] == jnp.arange(group_size, dtype=jnp.int32)[:, None], flags[:, None], 0), axis=0)
    return heat * lit.astype(jnp.float32)


def solution(mesh):
    placed = (
        P(None, None, ("band", "span")),
        P(None, ("band", "span")),
        P(None, ("band", "span")),
        P(("band", "span")),
        P(("band", "span")),
        P(("band", "span")),
        P(("band", "span")),
        P(),
        P(),
    )
    return jax.shard_map(
        local, mesh=mesh, in_specs=placed, out_specs=P(None, ("band", "span")), check_vma=False
    )
```

```python
import functools
import math

import jax
import jax.numpy as jnp
from jax import lax
from jax.experimental import pallas as pl
from jax.experimental.pallas import tpu as pltpu
from jax.sharding import PartitionSpec as P

LANES = 128
ROWS = 8
TILE = 256
STEP = 4
HALVES = 2
BIN_ROWS = 64
VMEM_BYTES = 63 * 1024 * 1024
LOG2E = math.log2(math.e)


def invert(x):
    return pl.reciprocal(x, approx=True)


def heating_kernel(
    per_peer,
    gases_hbm,
    bins_hbm,
    mass_hbm,
    cosine_hbm,
    ground_hbm,
    order_hbm,
    absorb_hbm,
    scatter_hbm,
    heat_ref,
    owner_ref,
    gases_ref,
    bins_ref,
    mass_ref,
    cosine_ref,
    ground_ref,
    order_ref,
    absorb_ref,
    albedo_ref,
    copied,
    wide_buf,
    table_ref,
    gas_buf,
    slope_buf,
    weight_even,
    weight_odd,
    optic_even,
    optic_odd,
    up_buf,
    rise_buf,
    pass_buf,
    refl_buf,
    fall_buf,
    direct_buf,
    gain_buf,
    net_buf,
):
    gas_count, levels, columns = gases_ref.shape
    points = table_ref.shape[0] // 2
    half = points // HALVES
    vregs = half // ROWS
    groups = levels // STEP
    blocks = columns // LANES
    tiles = columns // TILE

    copies = [
        pltpu.make_async_copy(source, target, copied.at[place])
        for place, (source, target) in enumerate(
            (
                (absorb_hbm, absorb_ref),
                (scatter_hbm, albedo_ref),
                (cosine_hbm, cosine_ref),
                (bins_hbm, bins_ref),
                (gases_hbm, gases_ref),
                (ground_hbm, ground_ref),
                (order_hbm, order_ref),
                (mass_hbm, mass_ref),
            )
        )
    ]
    for copy in copies:
        copy.start()
    refl_buf[...] = jnp.zeros_like(refl_buf)
    fall_buf[...] = jnp.zeros_like(fall_buf)
    wide_buf[...] = jnp.zeros_like(wide_buf)
    for copy in copies:
        copy.wait()

    for gas in range(gas_count):
        wide_buf[gas * BIN_ROWS : gas * BIN_ROWS + absorb_ref.shape[1], :points] = absorb_ref[gas].astype(jnp.float32)
    first_row = gas_count * BIN_ROWS
    wide_buf[first_row : first_row + absorb_ref.shape[1], :points] = 0.5 * albedo_ref[...].astype(jnp.float32)
    turned = [
        jnp.transpose(wide_buf[i * LANES : (i + 1) * LANES])[:points]
        for i in range(wide_buf.shape[0] // LANES)
    ]
    whole = jnp.concatenate(turned, axis=1)
    gas_lane = lax.broadcasted_iota(jnp.int32, whole.shape, 1) < first_row
    table_ref[:points] = jnp.where(gas_lane, whole, 0.0).astype(jnp.bfloat16)
    table_ref[points:] = jnp.where(gas_lane, 0.0, whole).astype(jnp.bfloat16)
    for gas in range(gas_count):
        gas_buf[gas] = gases_ref[gas].astype(jnp.float32)
    cosine = jnp.broadcast_to(cosine_ref[...].astype(jnp.float32).reshape(1, columns), (ROWS, columns))
    slope_buf[...] = (-LOG2E) / cosine

    def weigh(layer, tile, weight_ref):
        cols = slice(tile * TILE, (tile + 1) * TILE)
        spread = (BIN_ROWS, TILE)
        bins = jnp.broadcast_to(bins_ref[pl.ds(layer, 1), cols], spread)
        hit = bins == lax.broadcasted_iota(jnp.int32, spread, 0)
        selector = jnp.where(hit, 1.0, 0.0).astype(jnp.bfloat16)
        for gas in range(gas_count):
            amount = jnp.broadcast_to(gas_buf[gas, pl.ds(layer, 1), cols], (16, TILE)).astype(jnp.bfloat16)
            amount = jnp.concatenate([amount] * (BIN_ROWS // 16), axis=0)
            weight_ref[gas * BIN_ROWS : (gas + 1) * BIN_ROWS] = amount * selector
        weight_ref[gas_count * BIN_ROWS : (gas_count + 1) * BIN_ROWS] = selector

    def optical(slot, tile, weight_ref, optic_ref):
        cols = slice(tile * TILE, (tile + 1) * TILE)
        optic_ref[slot, :, cols] = jnp.dot(table_ref[...], weight_ref[...], preferred_element_type=jnp.float32)

    def advance(first, slots, chunk, optic_ref):
        block, part = divmod(chunk, HALVES)
        cols = slice(block * LANES, (block + 1) * LANES)
        rows = slice(part * half, (part + 1) * half)
        half_rows = slice(points + part * half, points + (part + 1) * half)
        shape = (vregs, ROWS, LANES)
        slope = slope_buf[:, cols]
        refl = refl_buf[rows, cols].reshape(shape)
        fall = fall_buf[rows, cols].reshape(shape)
        direct = direct_buf[rows, cols].reshape(shape)
        for slot in range(slots):
            layer = first + slot
            tau = optic_ref[slot, rows, cols].reshape(shape)
            half_albedo = optic_ref[slot, half_rows, cols].reshape(shape)
            fading = jnp.exp2(tau * (-1.66 * LOG2E))
            passed = jnp.exp2(tau * slope)
            reflect = half_albedo * (1.0 - fading)
            transmit = fading + reflect
            below = direct * passed
            source = half_albedo * (direct - below)
            pass_buf[layer, rows, cols] = (1.0 - refl).reshape(half, LANES)
            inverse = invert(1.0 - reflect * refl)
            up = transmit * inverse
            rise = (reflect * fall + source) * inverse
            up_buf[layer, rows, cols] = up.reshape(half, LANES)
            rise_buf[layer, rows, cols] = rise.reshape(half, LANES)
            fall = source + transmit * (fall + refl * rise)
            refl = reflect + transmit * (refl * up)
            direct = below
            gain_buf[part, layer + 1, :, cols] = jnp.sum(direct + fall, axis=0)
        refl_buf[rows, cols] = refl.reshape(half, LANES)
        fall_buf[rows, cols] = fall.reshape(half, LANES)
        direct_buf[rows, cols] = direct.reshape(half, LANES)

    direct_buf[...] = jnp.broadcast_to(cosine[:1], direct_buf.shape)
    for part in range(HALVES):
        gain_buf[part, 0] = cosine * float(vregs)

    chunks = blocks * HALVES
    work = [(slot, tile) for slot in range(STEP) for tile in range(tiles)]
    count = len(work)
    weights = (weight_even, weight_odd)

    weigh(0, 0, weights[0])
    for place, (slot, tile) in enumerate(work):
        after_slot, after_tile = (work + [(STEP, 0)])[place + 1]
        weigh(after_slot, after_tile, weights[(place + 1) % 2])
        optical(slot, tile, weights[place % 2], optic_even)

    def down_pair(pair, carry):
        first = pair * (2 * STEP)
        tasks = []
        for back in range(2):
            tasks += [(first + (back + 1) * STEP, slot, tile, (optic_odd, optic_even)[back]) for slot, tile in work]
        tasks.append((first + 3 * STEP, 0, 0, None))
        done = 0
        for step in range(2 * chunks):
            while done < (step + 1) * count // chunks:
                _, slot, tile, optic_ref = tasks[done]
                after, after_slot, after_tile, _ = tasks[done + 1]
                weigh(jnp.minimum(after + after_slot, levels - 1), after_tile, weights[(done + 1) % 2])
                optical(slot, tile, weights[done % 2], optic_ref)
                done += 1
            back, chunk = divmod(step, chunks)
            advance(first + back * STEP, STEP, chunk, (optic_even, optic_odd)[back])
        return carry

    lax.fori_loop(0, groups // 2, down_pair, 0)

    ground = jnp.broadcast_to(ground_ref[...].astype(jnp.float32).reshape(1, columns), (ROWS, columns))
    for block in range(blocks):
        cols = slice(block * LANES, (block + 1) * LANES)
        shape = (points // ROWS, ROWS, LANES)
        albedo = ground[:, cols]
        refl = refl_buf[:, cols].reshape(shape)
        arriving = (fall_buf[:, cols] + direct_buf[:, cols]).reshape(shape)
        rising = albedo * arriving / (1.0 - albedo * refl)
        fall_buf[:, cols] = rising.reshape(points, LANES)
        taken = jnp.sum(rising * (1.0 - refl), axis=0)
        total = gain_buf[0, levels, :, cols]
        for part in range(1, HALVES):
            total = total + gain_buf[part, levels, :, cols]
        net_buf[levels, :, cols] = total - taken

    def up_group(index, carry):
        last = levels - 1 - index * STEP
        for block in range(blocks):
            cols = slice(block * LANES, (block + 1) * LANES)
            shape = (points // ROWS, ROWS, LANES)
            rising = fall_buf[:, cols].reshape(shape)
            for slot in range(STEP):
                layer = last - slot
                rising = up_buf[layer, :, cols].reshape(shape) * rising + rise_buf[layer, :, cols].reshape(shape)
                taken = jnp.sum(rising * pass_buf[layer, :, cols].reshape(shape), axis=0)
                total = gain_buf[0, layer, :, cols]
                for part in range(1, HALVES):
                    total = total + gain_buf[part, layer, :, cols]
                net_buf[layer, :, cols] = total - taken
            fall_buf[:, cols] = rising.reshape(points, LANES)
        return carry

    lax.fori_loop(0, groups, up_group, 0)

    heat = jnp.sum(net_buf[:levels] - net_buf[1:], axis=1)
    heat_ref[...] = heat / mass_ref[...].astype(jnp.float32)

    spread = (columns, columns)
    order = jnp.broadcast_to(order_ref[...], spread)
    match = jnp.where(order == lax.broadcasted_iota(jnp.int32, spread, 0), 1.0, 0.0).astype(jnp.bfloat16)
    place = lax.broadcasted_iota(jnp.int32, (ROWS, columns), 1)
    group = (place // per_peer).astype(jnp.float32).astype(jnp.bfloat16)
    owner = lax.dot_general(group, match, (((1,), (1,)), ((), ())), preferred_element_type=jnp.float32)
    owner_ref[...] = owner.astype(jnp.int32)


def local(
    gases,
    pressure_bin,
    layer_mass,
    cos_zenith,
    surface_albedo,
    column_order,
    sunlit,
    absorption,
    scattering,
):
    group_size = lax.axis_size("span")
    me = lax.axis_index("span")
    gas_count, levels, columns = gases.shape
    points, _, bins = absorption.shape
    tile = jnp.broadcast_to(jnp.pad(sunlit, (0, LANES - sunlit.shape[0]))[None], (ROWS, LANES))
    gathered = lax.all_gather(tile, "span", axis=0, tiled=True).reshape(group_size, ROWS, LANES)
    field = pltpu.VMEM((levels, points, columns), jnp.float32)
    staged = pltpu.VMEM((STEP, 2 * points, columns), jnp.float32)
    weight = pltpu.VMEM(((gas_count + 1) * BIN_ROWS, TILE), jnp.bfloat16)
    state = pltpu.VMEM((points, columns), jnp.float32)
    heat, owner = pl.pallas_call(
        functools.partial(heating_kernel, columns // group_size),
        out_shape=(
            jax.ShapeDtypeStruct((levels, columns), jnp.float32),
            jax.ShapeDtypeStruct((ROWS, columns), jnp.int32),
        ),
        in_specs=[pl.BlockSpec(memory_space=pltpu.HBM)] * 8,
        out_specs=(pl.BlockSpec(memory_space=pltpu.VMEM),) * 2,
        scratch_shapes=[
            pltpu.VMEM(gases.shape, gases.dtype),
            pltpu.VMEM(pressure_bin.shape, pressure_bin.dtype),
            pltpu.VMEM(layer_mass.shape, layer_mass.dtype),
            pltpu.VMEM(cos_zenith.shape, cos_zenith.dtype),
            pltpu.VMEM(surface_albedo.shape, surface_albedo.dtype),
            pltpu.VMEM((1, columns), column_order.dtype),
            pltpu.VMEM((gas_count, bins, points), absorption.dtype),
            pltpu.VMEM((bins, points), scattering.dtype),
            pltpu.SemaphoreType.DMA((8,)),
            pltpu.VMEM((-(-(gas_count + 1) * BIN_ROWS // LANES) * LANES, LANES), jnp.float32),
            pltpu.VMEM((2 * points, (gas_count + 1) * BIN_ROWS), jnp.bfloat16),
            pltpu.VMEM(gases.shape, jnp.float32),
            pltpu.VMEM((ROWS, columns), jnp.float32),
            weight,
            weight,
            staged,
            staged,
            field,
            field,
            field,
            state,
            state,
            state,
            pltpu.VMEM((HALVES, levels + 1, ROWS, columns), jnp.float32),
            pltpu.VMEM((levels + 1, ROWS, columns), jnp.float32),
        ],
        compiler_params=pltpu.CompilerParams(vmem_limit_bytes=VMEM_BYTES),
        cost_estimate=pl.CostEstimate(
            flops=40 * levels * points * columns, bytes_accessed=1 << 20, transcendentals=3 * levels * points * columns
        ),
    )(
        gases,
        pressure_bin,
        layer_mass,
        cos_zenith,
        surface_albedo,
        column_order.reshape(1, columns),
        jnp.transpose(absorption, (1, 2, 0)),
        jnp.transpose(scattering),
    )
    place = me * (columns // group_size) // (columns // sunlit.shape[0])
    flags = lax.dynamic_index_in_dim(gathered[:, 0], place, axis=1, keepdims=False)
    peers = jnp.arange(group_size, dtype=jnp.int32)[:, None]
    lit = jnp.sum(jnp.where(owner[0][None] == peers, flags[:, None], 0), axis=0)
    return heat * lit.astype(jnp.float32)


def solution(mesh):
    placed = (
        P(None, None, ("band", "span")),
        P(None, ("band", "span")),
        P(None, ("band", "span")),
        P(("band", "span")),
        P(("band", "span")),
        P(("band", "span")),
        P(("band", "span")),
        P(),
        P(),
    )
    return jax.shard_map(
        local, mesh=mesh, in_specs=placed, out_specs=P(None, ("band", "span")), check_vma=False
    )
```

```python
import functools
import math

import jax
import jax.numpy as jnp
from jax import lax
from jax.experimental import pallas as pl
from jax.experimental.pallas import tpu as pltpu
from jax.sharding import PartitionSpec as P

LANES = 128
ROWS = 8
TILE = 256
STEP = 4
HALVES = 2
BIN_ROWS = 64
SHARE = 256
VMEM_BYTES = 63 * 1024 * 1024
LOG2E = math.log2(math.e)


def invert(x):
    return pl.reciprocal(x, approx=True)


def heating_kernel(
    per_peer,
    gases_hbm,
    bins_hbm,
    mass_hbm,
    cosine_hbm,
    ground_hbm,
    order_hbm,
    absorb_hbm,
    scatter_hbm,
    heat_ref,
    owner_ref,
    gases_ref,
    bins_ref,
    mass_ref,
    cosine_ref,
    ground_ref,
    order_ref,
    absorb_ref,
    albedo_ref,
    copied,
    wide_buf,
    table_ref,
    scatter_ref,
    gas_buf,
    slope_buf,
    tau_even,
    tau_odd,
    half_even,
    half_odd,
    up_buf,
    rise_buf,
    pass_buf,
    refl_buf,
    fall_buf,
    direct_buf,
    gain_buf,
    net_buf,
):
    gas_count, levels, columns = gases_ref.shape
    points = table_ref.shape[0]
    half = points // HALVES
    vregs = half // ROWS
    groups = levels // STEP
    blocks = columns // LANES
    tiles = columns // TILE

    copies = [
        pltpu.make_async_copy(source, target, copied.at[place])
        for place, (source, target) in enumerate(
            (
                (absorb_hbm, absorb_ref),
                (scatter_hbm, albedo_ref),
                (cosine_hbm, cosine_ref),
                (bins_hbm, bins_ref),
                (gases_hbm, gases_ref),
                (ground_hbm, ground_ref),
                (order_hbm, order_ref),
                (mass_hbm, mass_ref),
            )
        )
    ]
    for copy in copies:
        copy.start()
    refl_buf[...] = jnp.zeros_like(refl_buf)
    fall_buf[...] = jnp.zeros_like(fall_buf)
    wide_buf[...] = jnp.zeros_like(wide_buf)
    for copy in copies:
        copy.wait()

    for gas in range(gas_count):
        wide_buf[gas * BIN_ROWS : gas * BIN_ROWS + absorb_ref.shape[1], :points] = absorb_ref[gas].astype(jnp.float32)
    first_row = gas_count * BIN_ROWS
    wide_buf[first_row : first_row + absorb_ref.shape[1], :points] = 0.5 * albedo_ref[...].astype(jnp.float32)
    turned = [
        jnp.transpose(wide_buf[i * LANES : (i + 1) * LANES])[:points].astype(jnp.bfloat16)
        for i in range(wide_buf.shape[0] // LANES)
    ]
    whole = jnp.concatenate(turned, axis=1)
    table_ref[...] = whole[:, :first_row]
    scatter_ref[...] = whole[:, first_row : first_row + BIN_ROWS]
    for gas in range(gas_count):
        gas_buf[gas] = gases_ref[gas].astype(jnp.float32)
    cosine = jnp.broadcast_to(cosine_ref[...].astype(jnp.float32).reshape(1, columns), (ROWS, columns))
    slope_buf[...] = (-LOG2E) / cosine

    def optical(layer, tile, tau_ref, half_ref, slot):
        cols = slice(tile * TILE, (tile + 1) * TILE)
        spread = (BIN_ROWS, TILE)
        bins = jnp.broadcast_to(bins_ref[pl.ds(layer, 1), cols], spread)
        hit = bins == lax.broadcasted_iota(jnp.int32, spread, 0)
        selector = jnp.where(hit, 1.0, 0.0).astype(jnp.bfloat16)
        parts = []
        for gas in range(gas_count):
            amount = jnp.broadcast_to(gas_buf[gas, pl.ds(layer, 1), cols], (16, TILE)).astype(jnp.bfloat16)
            amount = jnp.concatenate([amount] * (BIN_ROWS // 16), axis=0)
            parts.append(amount * selector)
        weighted = jnp.concatenate(parts, axis=0)
        tau_ref[slot, :, cols] = jnp.dot(table_ref[...], weighted, preferred_element_type=jnp.float32)
        half_ref[slot, :, cols] = jnp.dot(scatter_ref[...], selector, preferred_element_type=jnp.float32)

    def advance(first, slots, chunk, tau_ref, half_ref):
        block, part = divmod(chunk, HALVES)
        cols = slice(block * LANES, (block + 1) * LANES)
        rows = slice(part * half, (part + 1) * half)
        shape = (vregs, ROWS, LANES)
        slope = slope_buf[:, cols]
        refl = refl_buf[rows, cols].reshape(shape)
        fall = fall_buf[rows, cols].reshape(shape)
        direct = direct_buf[rows, cols].reshape(shape)
        for slot in range(slots):
            layer = first + slot
            tau = tau_ref[slot, rows, cols].reshape(shape)
            half_albedo = half_ref[slot, rows, cols].reshape(shape)
            fading = jnp.exp2(tau * (-1.66 * LOG2E))
            passed = jnp.exp2(tau * slope)
            reflect = half_albedo * (1.0 - fading)
            transmit = fading + reflect
            below = direct * passed
            source = half_albedo * (direct - below)
            pass_buf[layer, rows, cols] = (1.0 - refl).reshape(half, LANES)
            inverse = invert(1.0 - reflect * refl)
            up = transmit * inverse
            rise = (reflect * fall + source) * inverse
            up_buf[layer, rows, cols] = up.reshape(half, LANES)
            rise_buf[layer, rows, cols] = rise.reshape(half, LANES)
            fall = source + transmit * (fall + refl * rise)
            refl = reflect + transmit * (refl * up)
            direct = below
            gain_buf[part, layer + 1, :, cols] = jnp.sum(direct + fall, axis=0)
        refl_buf[rows, cols] = refl.reshape(half, LANES)
        fall_buf[rows, cols] = fall.reshape(half, LANES)
        direct_buf[rows, cols] = direct.reshape(half, LANES)

    direct_buf[...] = jnp.broadcast_to(cosine[:1], direct_buf.shape)
    for part in range(HALVES):
        gain_buf[part, 0] = cosine * float(vregs)

    work = [(slot, tile) for slot in range(STEP) for tile in range(tiles)]
    for slot, tile in work:
        optical(slot, tile, tau_even, half_even, slot)

    chunks = blocks * HALVES

    def down_pair(pair, carry):
        first = pair * (2 * STEP)
        following = jnp.minimum(first + 2 * STEP, levels - STEP)
        for chunk in range(chunks):
            for slot, tile in work[chunk * len(work) // chunks:(chunk + 1) * len(work) // chunks]:
                optical(first + STEP + slot, tile, tau_odd, half_odd, slot)
            advance(first, STEP, chunk, tau_even, half_even)
        for chunk in range(chunks):
            for slot, tile in work[chunk * len(work) // chunks:(chunk + 1) * len(work) // chunks]:
                optical(following + slot, tile, tau_even, half_even, slot)
            advance(first + STEP, STEP, chunk, tau_odd, half_odd)
        return carry

    lax.fori_loop(0, groups // 2, down_pair, 0)

    ground = jnp.broadcast_to(ground_ref[...].astype(jnp.float32).reshape(1, columns), (ROWS, columns))
    for block in range(blocks):
        cols = slice(block * LANES, (block + 1) * LANES)
        shape = (points // ROWS, ROWS, LANES)
        albedo = ground[:, cols]
        refl = refl_buf[:, cols].reshape(shape)
        arriving = (fall_buf[:, cols] + direct_buf[:, cols]).reshape(shape)
        rising = albedo * arriving / (1.0 - albedo * refl)
        fall_buf[:, cols] = rising.reshape(points, LANES)
        taken = jnp.sum(rising * (1.0 - refl), axis=0)
        total = gain_buf[0, levels, :, cols]
        for part in range(1, HALVES):
            total = total + gain_buf[part, levels, :, cols]
        net_buf[levels, :, cols] = total - taken

    def up_group(index, carry):
        last = levels - 1 - index * STEP
        for block in range(blocks):
            cols = slice(block * LANES, (block + 1) * LANES)
            shape = (points // ROWS, ROWS, LANES)
            rising = fall_buf[:, cols].reshape(shape)
            for slot in range(STEP):
                layer = last - slot
                rising = up_buf[layer, :, cols].reshape(shape) * rising + rise_buf[layer, :, cols].reshape(shape)
                taken = jnp.sum(rising * pass_buf[layer, :, cols].reshape(shape), axis=0)
                total = gain_buf[0, layer, :, cols]
                for part in range(1, HALVES):
                    total = total + gain_buf[part, layer, :, cols]
                net_buf[layer, :, cols] = total - taken
            fall_buf[:, cols] = rising.reshape(points, LANES)
        return carry

    lax.fori_loop(0, groups, up_group, 0)

    heat = jnp.sum(net_buf[:levels] - net_buf[1:], axis=1)
    heat_ref[...] = heat / mass_ref[...].astype(jnp.float32)

    spread = (columns, columns)
    order = jnp.broadcast_to(order_ref[...], spread)
    match = jnp.where(order == lax.broadcasted_iota(jnp.int32, spread, 0), 1.0, 0.0).astype(jnp.bfloat16)
    place = lax.broadcasted_iota(jnp.int32, (ROWS, columns), 1)
    group = (place // per_peer).astype(jnp.float32).astype(jnp.bfloat16)
    owner = lax.dot_general(group, match, (((1,), (1,)), ((), ())), preferred_element_type=jnp.float32)
    owner_ref[...] = owner.astype(jnp.int32)


def local(
    gases,
    pressure_bin,
    layer_mass,
    cos_zenith,
    surface_albedo,
    column_order,
    sunlit,
    absorption,
    scattering,
):
    group_size = lax.axis_size("span")
    me = lax.axis_index("span")
    gas_count, levels, columns = gases.shape
    points, _, bins = absorption.shape
    padded = jnp.pad(sunlit.astype(jnp.float32), (0, LANES - sunlit.shape[0]))
    tile = jnp.broadcast_to(padded[None], (SHARE, LANES))
    gathered = lax.all_gather(tile, "span", axis=0, tiled=True).reshape(group_size, SHARE, LANES)
    field = pltpu.VMEM((levels, points, columns), jnp.float32)
    staged = pltpu.VMEM((STEP, points, columns), jnp.float32)
    state = pltpu.VMEM((points, columns), jnp.float32)
    heat, owner = pl.pallas_call(
        functools.partial(heating_kernel, columns // group_size),
        out_shape=(
            jax.ShapeDtypeStruct((levels, columns), jnp.float32),
            jax.ShapeDtypeStruct((ROWS, columns), jnp.int32),
        ),
        in_specs=[pl.BlockSpec(memory_space=pltpu.HBM)] * 8,
        out_specs=(pl.BlockSpec(memory_space=pltpu.VMEM),) * 2,
        scratch_shapes=[
            pltpu.VMEM(gases.shape, gases.dtype),
            pltpu.VMEM(pressure_bin.shape, pressure_bin.dtype),
            pltpu.VMEM(layer_mass.shape, layer_mass.dtype),
            pltpu.VMEM(cos_zenith.shape, cos_zenith.dtype),
            pltpu.VMEM(surface_albedo.shape, surface_albedo.dtype),
            pltpu.VMEM((1, columns), column_order.dtype),
            pltpu.VMEM((gas_count, bins, points), absorption.dtype),
            pltpu.VMEM((bins, points), scattering.dtype),
            pltpu.SemaphoreType.DMA((8,)),
            pltpu.VMEM((-(-(gas_count + 1) * BIN_ROWS // LANES) * LANES, LANES), jnp.float32),
            pltpu.VMEM((points, gas_count * BIN_ROWS), jnp.bfloat16),
            pltpu.VMEM((points, BIN_ROWS), jnp.bfloat16),
            pltpu.VMEM(gases.shape, jnp.float32),
            pltpu.VMEM((ROWS, columns), jnp.float32),
            staged,
            staged,
            staged,
            staged,
            field,
            field,
            field,
            state,
            state,
            state,
            pltpu.VMEM((HALVES, levels + 1, ROWS, columns), jnp.float32),
            pltpu.VMEM((levels + 1, ROWS, columns), jnp.float32),
        ],
        compiler_params=pltpu.CompilerParams(vmem_limit_bytes=VMEM_BYTES),
        cost_estimate=pl.CostEstimate(
            flops=40 * levels * points * columns, bytes_accessed=1 << 20, transcendentals=3 * levels * points * columns
        ),
    )(
        gases,
        pressure_bin,
        layer_mass,
        cos_zenith,
        surface_albedo,
        column_order.reshape(1, columns),
        jnp.transpose(absorption, (1, 2, 0)),
        jnp.transpose(scattering),
    )
    place = me * (columns // group_size) // (columns // sunlit.shape[0])
    flags = lax.dynamic_index_in_dim(gathered[:, 0], place, axis=1, keepdims=False)
    peers = jnp.arange(group_size, dtype=jnp.int32)[:, None]
    lit = jnp.sum(jnp.where(owner[0][None] == peers, flags[:, None], 0.0), axis=0)
    return heat * lit


def solution(mesh):
    placed = (
        P(None, None, ("band", "span")),
        P(None, ("band", "span")),
        P(None, ("band", "span")),
        P(("band", "span")),
        P(("band", "span")),
        P(("band", "span")),
        P(("band", "span")),
        P(),
        P(),
    )
    return jax.shard_map(
        local, mesh=mesh, in_specs=placed, out_specs=P(None, ("band", "span")), check_vma=False
    )
```

```python
import functools
import math

import jax
import jax.numpy as jnp
from jax import lax
from jax.experimental import pallas as pl
from jax.experimental.pallas import tpu as pltpu
from jax.sharding import PartitionSpec as P

LANES = 128
ROWS = 8
PACK = 16
STEP = 4
HALVES = 2
BIN_ROWS = 64
LOG2E = math.log2(math.e)
VMEM_BYTES = 63 * 1024 * 1024


def one_hot(hit):
    return jnp.where(hit, 1.0, 0.0).astype(jnp.bfloat16)


def heating_kernel(
    groups,
    flags_ref,
    gases_hbm,
    bins_hbm,
    mass_hbm,
    cosine_hbm,
    ground_hbm,
    order_hbm,
    absorb_hbm,
    scatter_hbm,
    heat_ref,
    gases_ref,
    bins_ref,
    mass_ref,
    cosine_ref,
    ground_ref,
    order_ref,
    absorb_ref,
    albedo_ref,
    copied,
    listed,
    wide_buf,
    table_ref,
    scatter_ref,
    match_ref,
    dealt_ref,
    block_ref,
    optic_ref,
    up_buf,
    rise_buf,
    pass_buf,
    refl_buf,
    fall_buf,
    direct_buf,
    gain_buf,
    net_buf,
    warm_buf,
):
    gas_count, levels, columns = gases_ref.shape
    points = table_ref.shape[0]
    bin_count = absorb_ref.shape[1]
    half = points // HALVES
    vregs = half // ROWS
    blocks = columns // LANES
    per_peer = columns // groups
    in_block = LANES // per_peer
    bin_row = gas_count * levels
    ray_row = bin_row + levels
    first_row = gas_count * BIN_ROWS

    copies = [
        pltpu.make_async_copy(source, target, copied.at[place])
        for place, (source, target) in enumerate(
            (
                (absorb_hbm, absorb_ref),
                (scatter_hbm, albedo_ref),
                (order_hbm, order_ref),
                (cosine_hbm, cosine_ref),
                (ground_hbm, ground_ref),
                (bins_hbm, bins_ref),
                (gases_hbm, gases_ref),
                (mass_hbm, mass_ref),
            )
        )
    ]
    for copy in copies:
        copy.start()

    lit_count = jnp.int32(0)
    listed[0] = 0
    for group in range(groups):
        lit_flag = flags_ref[group]
        listed[lit_count] = group
        lit_count = lit_count + lit_flag
    last = listed[jnp.maximum(lit_count - 1, 0)]
    for spot in range(groups):
        listed[spot] = jnp.where(spot < lit_count, listed[spot], last)
    active = (lit_count + in_block - 1) // in_block

    wide_buf[...] = jnp.zeros_like(wide_buf)
    warm_buf[...] = jnp.zeros_like(warm_buf)
    for copy in copies:
        copy.wait()

    for gas in range(gas_count):
        wide_buf[gas * BIN_ROWS : gas * BIN_ROWS + bin_count, :points] = absorb_ref[gas].astype(jnp.float32)
    wide_buf[first_row : first_row + bin_count, :points] = 0.5 * albedo_ref[...].astype(jnp.float32)
    turned = [
        jnp.transpose(wide_buf[i * LANES : (i + 1) * LANES])[:points].astype(jnp.bfloat16)
        for i in range(wide_buf.shape[0] // LANES)
    ]
    whole = jnp.concatenate(turned, axis=1)
    table_ref[...] = whole[:, :first_row]
    scatter_ref[...] = whole[:, first_row : first_row + BIN_ROWS]

    square = (columns, columns)
    order = jnp.broadcast_to(order_ref[...], square)
    match_ref[...] = one_hot(order == lax.broadcasted_iota(jnp.int32, square, 0))
    spread = (PACK, columns)
    ray = jnp.where(
        lax.broadcasted_iota(jnp.int32, spread, 0) == 0,
        jnp.broadcast_to(cosine_ref[...].astype(jnp.float32).reshape(1, columns), spread),
        jnp.broadcast_to(ground_ref[...].astype(jnp.float32).reshape(1, columns), spread),
    ).astype(jnp.bfloat16)
    fields = jnp.concatenate(
        [gases_ref[...].reshape(bin_row, columns), bins_ref[...].astype(jnp.float32).astype(jnp.bfloat16), ray], axis=0
    )
    for block in range(blocks):
        dealt_ref[block] = jnp.dot(
            fields, match_ref[:, block * LANES : (block + 1) * LANES], preferred_element_type=jnp.float32
        )

    def shift_of(target, source):
        return lax.rem((target - source) * per_peer + LANES, LANES)

    lane = lax.broadcasted_iota(jnp.int32, (1, LANES), 1) // per_peer

    def pack(block, slot):
        packed = None
        for spot in range(in_block):
            group = listed[block * in_block + spot]
            moved = pltpu.roll(dealt_ref[group // in_block], shift_of(spot, group % in_block), 1)
            packed = moved if packed is None else jnp.where(lane == spot, moved, packed)
        block_ref[slot] = packed

    def optical(slot, layer):
        parts = []
        shape = (BIN_ROWS, LANES)
        rows = lax.broadcasted_iota(jnp.int32, shape, 0).astype(jnp.float32)
        selectors = []
        for near in (layer, layer + 1):
            place = bin_row + near
            bins = jnp.broadcast_to(block_ref[slot, place : place + 1, :], shape)
            selectors.append(one_hot(bins == rows))
        for gas in range(gas_count):
            pair = []
            for near, selector in zip((layer, layer + 1), selectors):
                place = gas * levels + near
                amount = jnp.broadcast_to(block_ref[slot, place : place + 1, :], (PACK, LANES)).astype(jnp.bfloat16)
                pair.append(jnp.concatenate([amount] * (BIN_ROWS // PACK), axis=0) * selector)
            parts.append(jnp.concatenate(pair, axis=1))
        weighted = jnp.concatenate(parts, axis=0)
        selected = jnp.concatenate(selectors, axis=1)
        tau = jnp.dot(table_ref[...], weighted, preferred_element_type=jnp.float32)
        albedo = jnp.dot(scatter_ref[...], selected, preferred_element_type=jnp.float32)
        for near in range(2):
            cols = slice(near * LANES, (near + 1) * LANES)
            optic_ref[layer + near, :points] = tau[:, cols]
            optic_ref[layer + near, points:] = albedo[:, cols]

    def advance(first, part, slope):
        rows = slice(part * half, (part + 1) * half)
        half_rows = slice(points + part * half, points + (part + 1) * half)
        shape = (vregs, ROWS, LANES)
        refl = refl_buf[rows].reshape(shape)
        fall = fall_buf[rows].reshape(shape)
        direct = direct_buf[rows].reshape(shape)
        for layer in range(first, first + STEP):
            tau = optic_ref[layer, rows].reshape(shape)
            half_albedo = optic_ref[layer, half_rows].reshape(shape)
            fading = jnp.exp2(tau * (-1.66 * LOG2E))
            passed = jnp.exp2(tau * slope)
            reflect = half_albedo * (1.0 - fading)
            transmit = fading + reflect
            below = direct * passed
            source = half_albedo * (direct - below)
            pass_buf[layer, rows] = (1.0 - refl).reshape(half, LANES)
            inverse = pl.reciprocal(1.0 - reflect * refl, approx=True)
            up = transmit * inverse
            rise = (reflect * fall + source) * inverse
            up_buf[layer, rows] = up.reshape(half, LANES)
            rise_buf[layer, rows] = rise.reshape(half, LANES)
            fall = source + transmit * (fall + refl * rise)
            refl = reflect + transmit * (refl * up)
            direct = below
            gain_buf[part, layer + 1] = jnp.sum(direct + fall, axis=0)
        refl_buf[rows] = refl.reshape(half, LANES)
        fall_buf[rows] = fall.reshape(half, LANES)
        direct_buf[rows] = direct.reshape(half, LANES)

    lead = range(0, STEP, 2)

    def column_block(block, carry):
        here = lax.rem(block, 2)
        cosine = jnp.broadcast_to(block_ref[here, ray_row : ray_row + 1, :], (ROWS, LANES))
        slope = (-LOG2E) / cosine
        refl_buf[...] = jnp.zeros_like(refl_buf)
        fall_buf[...] = jnp.zeros_like(fall_buf)
        direct_buf[...] = jnp.broadcast_to(cosine[:1], direct_buf.shape)
        for part in range(HALVES):
            gain_buf[part, 0] = cosine * float(vregs)
        for first in range(0, levels, STEP):
            coming = [layer for layer in range(first + STEP, first + 2 * STEP, 2) if layer < levels]
            for part in range(HALVES):
                for layer in coming[part * len(coming) // HALVES : (part + 1) * len(coming) // HALVES]:
                    optical(here, layer)
                advance(first, part, slope)

        pack(jnp.minimum(block + 1, blocks - 1), 1 - here)
        for layer in lead:
            optical(1 - here, layer)

        albedo = jnp.broadcast_to(block_ref[here, ray_row + 1 : ray_row + 2, :], (ROWS, LANES))
        shape = (points // ROWS, ROWS, LANES)
        refl = refl_buf[...].reshape(shape)
        arriving = (fall_buf[...] + direct_buf[...]).reshape(shape)
        rising = albedo * arriving * pl.reciprocal(1.0 - albedo * refl, approx=True)

        def total(level):
            summed = gain_buf[0, level]
            for part in range(1, HALVES):
                summed = summed + gain_buf[part, level]
            return summed

        net_buf[levels] = total(levels) - jnp.sum(rising * (1.0 - refl), axis=0)
        for layer in range(levels - 1, -1, -1):
            rising = up_buf[layer].reshape(shape) * rising + rise_buf[layer].reshape(shape)
            net_buf[layer] = total(layer) - jnp.sum(rising * pass_buf[layer].reshape(shape), axis=0)
        warm = jnp.sum(net_buf[:levels] - net_buf[1:], axis=1)
        for spot in range(in_block):
            group = listed[block * in_block + spot]
            own = group % in_block
            home = group // in_block
            moved = pltpu.roll(warm, shift_of(own, spot), 1)
            warm_buf[home] = jnp.where(lane == own, moved, warm_buf[home])
        return carry

    pack(0, 0)
    for layer in lead:
        optical(0, layer)
    lax.fori_loop(0, active, column_block, 0)

    warm = jnp.concatenate([warm_buf[block] for block in range(blocks)], axis=1)
    pieces = []
    for _ in range(3):
        piece = warm.astype(jnp.bfloat16)
        warm = warm - piece.astype(jnp.float32)
        pieces.append(piece)
    spread_out = lax.dot_general(
        jnp.concatenate(pieces, axis=0), match_ref[...], (((1,), (1,)), ((), ())), preferred_element_type=jnp.float32
    )
    heat = spread_out[:levels] + spread_out[levels : 2 * levels] + spread_out[2 * levels :]
    heat_ref[...] = heat / mass_ref[...].astype(jnp.float32)


def local(
    gases,
    pressure_bin,
    layer_mass,
    cos_zenith,
    surface_albedo,
    column_order,
    sunlit,
    absorption,
    scattering,
):
    group_size = lax.axis_size("span")
    gas_count, levels, columns = gases.shape
    points, _, bins = absorption.shape
    block_count = sunlit.shape[0]
    wanted = jnp.broadcast_to(sunlit[:, None], (block_count, group_size // block_count)).reshape(group_size)
    flags = lax.all_to_all(wanted, "span", split_axis=0, concat_axis=0, tiled=True)
    field = pltpu.VMEM((levels, points, LANES), jnp.float32)
    state = pltpu.VMEM((points, LANES), jnp.float32)
    rows = gas_count * levels + levels + PACK
    blocks = columns // LANES
    return pl.pallas_call(
        functools.partial(heating_kernel, group_size),
        out_shape=jax.ShapeDtypeStruct((levels, columns), jnp.float32),
        in_specs=[pl.BlockSpec(memory_space=pltpu.SMEM)] + [pl.BlockSpec(memory_space=pltpu.HBM)] * 8,
        out_specs=pl.BlockSpec(memory_space=pltpu.VMEM),
        scratch_shapes=[
            pltpu.VMEM(gases.shape, gases.dtype),
            pltpu.VMEM(pressure_bin.shape, pressure_bin.dtype),
            pltpu.VMEM(layer_mass.shape, layer_mass.dtype),
            pltpu.VMEM(cos_zenith.shape, cos_zenith.dtype),
            pltpu.VMEM(surface_albedo.shape, surface_albedo.dtype),
            pltpu.VMEM((1, columns), column_order.dtype),
            pltpu.VMEM((gas_count, bins, points), absorption.dtype),
            pltpu.VMEM((bins, points), scattering.dtype),
            pltpu.SemaphoreType.DMA((8,)),
            pltpu.SMEM((group_size + 1,), jnp.int32),
            pltpu.VMEM((-(-(gas_count + 1) * BIN_ROWS // LANES) * LANES, LANES), jnp.float32),
            pltpu.VMEM((points, gas_count * BIN_ROWS), jnp.bfloat16),
            pltpu.VMEM((points, BIN_ROWS), jnp.bfloat16),
            pltpu.VMEM((columns, columns), jnp.bfloat16),
            pltpu.VMEM((blocks, rows, LANES), jnp.float32),
            pltpu.VMEM((2, rows, LANES), jnp.float32),
            pltpu.VMEM((levels, 2 * points, LANES), jnp.float32),
            field,
            field,
            field,
            state,
            state,
            state,
            pltpu.VMEM((HALVES, levels + 1, ROWS, LANES), jnp.float32),
            pltpu.VMEM((levels + 1, ROWS, LANES), jnp.float32),
            pltpu.VMEM((blocks, levels, LANES), jnp.float32),
        ],
        compiler_params=pltpu.CompilerParams(vmem_limit_bytes=VMEM_BYTES),
        cost_estimate=pl.CostEstimate(
            flops=40 * levels * points * columns, bytes_accessed=1 << 20, transcendentals=3 * levels * points * columns
        ),
    )(
        flags,
        gases,
        pressure_bin,
        layer_mass,
        cos_zenith,
        surface_albedo,
        column_order.reshape(1, columns),
        jnp.transpose(absorption, (1, 2, 0)),
        jnp.transpose(scattering),
    )


def solution(mesh):
    placed = (
        P(None, None, ("band", "span")),
        P(None, ("band", "span")),
        P(None, ("band", "span")),
        P(("band", "span")),
        P(("band", "span")),
        P(("band", "span")),
        P(("band", "span")),
        P(),
        P(),
    )
    return jax.shard_map(
        local, mesh=mesh, in_specs=placed, out_specs=P(None, ("band", "span")), check_vma=False
    )
```

```python
import functools
import math

import jax
import jax.numpy as jnp
from jax import lax
from jax.experimental import pallas as pl
from jax.experimental.pallas import tpu as pltpu
from jax.sharding import PartitionSpec as P

LANES = 128
ROWS = 8
PACK = 16
STEP = 4
HALVES = 2
BIN_ROWS = 64
LOG2E = math.log2(math.e)
PREPARE_BYTES = 63 * 1024 * 1024
VMEM_BYTES = 63 * 1024 * 1024


def one_hot(hit):
    return jnp.where(hit, 1.0, 0.0).astype(jnp.bfloat16)


def prepare_kernel(
    gases_hbm,
    bins_hbm,
    cosine_hbm,
    ground_hbm,
    order_hbm,
    absorb_hbm,
    scatter_hbm,
    table_ref,
    scatter_ref,
    match_ref,
    dealt_ref,
    gases_ref,
    bins_ref,
    cosine_ref,
    ground_ref,
    order_ref,
    absorb_ref,
    albedo_ref,
    copied,
    wide_buf,
):
    gas_count, levels, columns = gases_ref.shape
    points = table_ref.shape[0]
    bin_count = absorb_ref.shape[1]
    blocks = columns // LANES
    bin_row = gas_count * levels
    first_row = gas_count * BIN_ROWS

    copies = [
        pltpu.make_async_copy(source, target, copied.at[place])
        for place, (source, target) in enumerate(
            (
                (absorb_hbm, absorb_ref),
                (scatter_hbm, albedo_ref),
                (order_hbm, order_ref),
                (cosine_hbm, cosine_ref),
                (ground_hbm, ground_ref),
                (bins_hbm, bins_ref),
                (gases_hbm, gases_ref),
            )
        )
    ]
    for copy in copies:
        copy.start()
    wide_buf[...] = jnp.zeros_like(wide_buf)
    for copy in copies:
        copy.wait()

    for gas in range(gas_count):
        wide_buf[gas * BIN_ROWS : gas * BIN_ROWS + bin_count, :points] = absorb_ref[gas].astype(jnp.float32)
    wide_buf[first_row : first_row + bin_count, :points] = 0.5 * albedo_ref[...].astype(jnp.float32)
    turned = [
        jnp.transpose(wide_buf[i * LANES : (i + 1) * LANES])[:points].astype(jnp.bfloat16)
        for i in range(wide_buf.shape[0] // LANES)
    ]
    whole = jnp.concatenate(turned, axis=1)
    table_ref[...] = whole[:, :first_row]
    scatter_ref[...] = whole[:, first_row : first_row + BIN_ROWS]

    square = (columns, columns)
    order = jnp.broadcast_to(order_ref[...], square)
    match_ref[...] = one_hot(order == lax.broadcasted_iota(jnp.int32, square, 0))
    spread = (PACK, columns)
    ray = jnp.where(
        lax.broadcasted_iota(jnp.int32, spread, 0) == 0,
        jnp.broadcast_to(cosine_ref[...].astype(jnp.float32).reshape(1, columns), spread),
        jnp.broadcast_to(ground_ref[...].astype(jnp.float32).reshape(1, columns), spread),
    ).astype(jnp.bfloat16)
    fields = jnp.concatenate(
        [gases_ref[...].reshape(bin_row, columns), bins_ref[...].astype(jnp.float32).astype(jnp.bfloat16), ray], axis=0
    )
    for block in range(blocks):
        dealt_ref[block] = jnp.dot(
            fields, match_ref[:, block * LANES : (block + 1) * LANES], preferred_element_type=jnp.float32
        )


def heating_kernel(
    groups,
    flags_hbm,
    mass_hbm,
    table_hbm,
    scatter_hbm,
    match_hbm,
    dealt_hbm,
    heat_ref,
    flags_ref,
    mass_ref,
    table_ref,
    scatter_ref,
    match_ref,
    dealt_ref,
    copied,
    listed,
    block_ref,
    optic_ref,
    up_buf,
    rise_buf,
    pass_buf,
    refl_buf,
    fall_buf,
    direct_buf,
    gain_buf,
    net_buf,
    warm_buf,
):
    levels, columns = heat_ref.shape
    points, gas_rows = table_ref.shape
    gas_count = gas_rows // BIN_ROWS
    half = points // HALVES
    vregs = half // ROWS
    blocks = columns // LANES
    per_peer = columns // groups
    in_block = LANES // per_peer
    bin_row = gas_count * levels
    ray_row = bin_row + levels

    early = [
        pltpu.make_async_copy(source, target, copied.at[place])
        for place, (source, target) in enumerate(
            (
                (flags_hbm, flags_ref),
                (dealt_hbm, dealt_ref),
                (table_hbm, table_ref),
                (scatter_hbm, scatter_ref),
            )
        )
    ]
    late = [
        pltpu.make_async_copy(source, target, copied.at[len(early) + place])
        for place, (source, target) in enumerate(((match_hbm, match_ref), (mass_hbm, mass_ref)))
    ]
    for copy in early + late:
        copy.start()
    warm_buf[...] = jnp.zeros_like(warm_buf)
    for copy in early:
        copy.wait()

    lit_count = jnp.int32(0)
    for group in range(groups):
        lit_flag = flags_ref[group, 0]
        listed[lit_count] = group
        lit_count = lit_count + lit_flag
    last = listed[jnp.maximum(lit_count - 1, 0)]
    for spot in range(groups):
        listed[spot] = jnp.where(spot < lit_count, listed[spot], last)
    active = (lit_count + in_block - 1) // in_block

    def shift_of(target, source):
        return lax.rem((target - source) * per_peer + LANES, LANES)

    lane = lax.broadcasted_iota(jnp.int32, (1, LANES), 1) // per_peer

    def pack(block, slot):
        packed = None
        for spot in range(in_block):
            group = listed[block * in_block + spot]
            moved = pltpu.roll(dealt_ref[group // in_block], shift_of(spot, group % in_block), 1)
            packed = moved if packed is None else jnp.where(lane == spot, moved, packed)
        block_ref[slot] = packed

    def optical(slot, layer):
        parts = []
        shape = (BIN_ROWS, LANES)
        rows = lax.broadcasted_iota(jnp.int32, shape, 0).astype(jnp.float32)
        selectors = []
        for near in (layer, layer + 1):
            place = bin_row + near
            bins = jnp.broadcast_to(block_ref[slot, place : place + 1, :], shape)
            selectors.append(one_hot(bins == rows))
        for gas in range(gas_count):
            pair = []
            for near, selector in zip((layer, layer + 1), selectors):
                place = gas * levels + near
                amount = jnp.broadcast_to(block_ref[slot, place : place + 1, :], (PACK, LANES)).astype(jnp.bfloat16)
                pair.append(jnp.concatenate([amount] * (BIN_ROWS // PACK), axis=0) * selector)
            parts.append(jnp.concatenate(pair, axis=1))
        weighted = jnp.concatenate(parts, axis=0)
        selected = jnp.concatenate(selectors, axis=1)
        tau = jnp.dot(table_ref[...], weighted, preferred_element_type=jnp.float32)
        albedo = jnp.dot(scatter_ref[...], selected, preferred_element_type=jnp.float32)
        for near in range(2):
            cols = slice(near * LANES, (near + 1) * LANES)
            optic_ref[layer + near, :points] = tau[:, cols]
            optic_ref[layer + near, points:] = albedo[:, cols]

    def advance(first, part, slope):
        rows = slice(part * half, (part + 1) * half)
        half_rows = slice(points + part * half, points + (part + 1) * half)
        shape = (vregs, ROWS, LANES)
        refl = refl_buf[rows].reshape(shape)
        fall = fall_buf[rows].reshape(shape)
        direct = direct_buf[rows].reshape(shape)
        for layer in range(first, first + STEP):
            tau = optic_ref[layer, rows].reshape(shape)
            half_albedo = optic_ref[layer, half_rows].reshape(shape)
            fading = jnp.exp2(tau * (-1.66 * LOG2E))
            passed = jnp.exp2(tau * slope)
            reflect = half_albedo * (1.0 - fading)
            transmit = fading + reflect
            below = direct * passed
            source = half_albedo * (direct - below)
            pass_buf[layer, rows] = (1.0 - refl).reshape(half, LANES)
            inverse = pl.reciprocal(1.0 - reflect * refl, approx=True)
            up = transmit * inverse
            rise = (reflect * fall + source) * inverse
            up_buf[layer, rows] = up.reshape(half, LANES)
            rise_buf[layer, rows] = rise.reshape(half, LANES)
            fall = source + transmit * (fall + refl * rise)
            refl = reflect + transmit * (refl * up)
            direct = below
            gain_buf[part, layer + 1] = jnp.sum(direct + fall, axis=0)
        refl_buf[rows] = refl.reshape(half, LANES)
        fall_buf[rows] = fall.reshape(half, LANES)
        direct_buf[rows] = direct.reshape(half, LANES)

    lead = range(0, STEP, 2)

    def column_block(block, carry):
        here = lax.rem(block, 2)
        cosine = jnp.broadcast_to(block_ref[here, ray_row : ray_row + 1, :], (ROWS, LANES))
        slope = (-LOG2E) / cosine
        refl_buf[...] = jnp.zeros_like(refl_buf)
        fall_buf[...] = jnp.zeros_like(fall_buf)
        direct_buf[...] = jnp.broadcast_to(cosine[:1], direct_buf.shape)
        for part in range(HALVES):
            gain_buf[part, 0] = cosine * float(vregs)
        for first in range(0, levels, STEP):
            coming = [layer for layer in range(first + STEP, first + 2 * STEP, 2) if layer < levels]
            for part in range(HALVES):
                for layer in coming[part * len(coming) // HALVES : (part + 1) * len(coming) // HALVES]:
                    optical(here, layer)
                advance(first, part, slope)

        pack(jnp.minimum(block + 1, blocks - 1), 1 - here)
        for layer in lead:
            optical(1 - here, layer)

        albedo = jnp.broadcast_to(block_ref[here, ray_row + 1 : ray_row + 2, :], (ROWS, LANES))
        shape = (points // ROWS, ROWS, LANES)
        refl = refl_buf[...].reshape(shape)
        arriving = (fall_buf[...] + direct_buf[...]).reshape(shape)
        rising = albedo * arriving * pl.reciprocal(1.0 - albedo * refl, approx=True)

        def total(level):
            summed = gain_buf[0, level]
            for part in range(1, HALVES):
                summed = summed + gain_buf[part, level]
            return summed

        net_buf[levels] = total(levels) - jnp.sum(rising * (1.0 - refl), axis=0)
        for layer in range(levels - 1, -1, -1):
            rising = up_buf[layer].reshape(shape) * rising + rise_buf[layer].reshape(shape)
            net_buf[layer] = total(layer) - jnp.sum(rising * pass_buf[layer].reshape(shape), axis=0)
        warm = jnp.sum(net_buf[:levels] - net_buf[1:], axis=1)
        for spot in range(in_block):
            group = listed[block * in_block + spot]
            own = group % in_block
            home = group // in_block
            moved = pltpu.roll(warm, shift_of(own, spot), 1)
            warm_buf[home] = jnp.where(lane == own, moved, warm_buf[home])
        return carry

    pack(0, 0)
    for layer in lead:
        optical(0, layer)
    lax.fori_loop(0, active, column_block, 0)

    for copy in late:
        copy.wait()
    warm = jnp.concatenate([warm_buf[block] for block in range(blocks)], axis=1)
    pieces = []
    for _ in range(3):
        piece = warm.astype(jnp.bfloat16)
        warm = warm - piece.astype(jnp.float32)
        pieces.append(piece)
    spread_out = lax.dot_general(
        jnp.concatenate(pieces, axis=0), match_ref[...], (((1,), (1,)), ((), ())), preferred_element_type=jnp.float32
    )
    heat = spread_out[:levels] + spread_out[levels : 2 * levels] + spread_out[2 * levels :]
    heat_ref[...] = heat / mass_ref[...].astype(jnp.float32)


def local(
    gases,
    pressure_bin,
    layer_mass,
    cos_zenith,
    surface_albedo,
    column_order,
    sunlit,
    absorption,
    scattering,
):
    group_size = lax.axis_size("span")
    gas_count, levels, columns = gases.shape
    points, _, bins = absorption.shape
    block_count = sunlit.shape[0]
    wanted = jnp.broadcast_to(sunlit[:, None, None], (block_count, group_size // block_count, LANES))
    flags = lax.all_to_all(wanted.reshape(group_size, LANES), "span", split_axis=0, concat_axis=0, tiled=True)
    rows = gas_count * levels + levels + PACK
    blocks = columns // LANES
    gas_rows = gas_count * BIN_ROWS
    hbm = pl.BlockSpec(memory_space=pltpu.HBM)
    made = (
        jax.ShapeDtypeStruct((points, gas_rows), jnp.bfloat16),
        jax.ShapeDtypeStruct((points, BIN_ROWS), jnp.bfloat16),
        jax.ShapeDtypeStruct((columns, columns), jnp.bfloat16),
        jax.ShapeDtypeStruct((blocks, rows, LANES), jnp.float32),
    )
    table, scatter, match, dealt = pl.pallas_call(
        prepare_kernel,
        out_shape=made,
        in_specs=[hbm] * 7,
        out_specs=(pl.BlockSpec(memory_space=pltpu.VMEM),) * 4,
        scratch_shapes=[
            pltpu.VMEM(gases.shape, gases.dtype),
            pltpu.VMEM(pressure_bin.shape, pressure_bin.dtype),
            pltpu.VMEM(cos_zenith.shape, cos_zenith.dtype),
            pltpu.VMEM(surface_albedo.shape, surface_albedo.dtype),
            pltpu.VMEM((1, columns), column_order.dtype),
            pltpu.VMEM((gas_count, bins, points), absorption.dtype),
            pltpu.VMEM((bins, points), scattering.dtype),
            pltpu.SemaphoreType.DMA((7,)),
            pltpu.VMEM((-(-(gas_count + 1) * BIN_ROWS // LANES) * LANES, LANES), jnp.float32),
        ],
        compiler_params=pltpu.CompilerParams(vmem_limit_bytes=PREPARE_BYTES),
        cost_estimate=pl.CostEstimate(
            flops=8 * rows * columns * columns, bytes_accessed=4 << 20, transcendentals=0
        ),
    )(
        gases,
        pressure_bin,
        cos_zenith,
        surface_albedo,
        column_order.reshape(1, columns),
        jnp.transpose(absorption, (1, 2, 0)),
        jnp.transpose(scattering),
    )
    field = pltpu.VMEM((levels, points, LANES), jnp.float32)
    state = pltpu.VMEM((points, LANES), jnp.float32)
    return pl.pallas_call(
        functools.partial(heating_kernel, group_size),
        out_shape=jax.ShapeDtypeStruct((levels, columns), jnp.float32),
        in_specs=[hbm] * 6,
        out_specs=pl.BlockSpec(memory_space=pltpu.VMEM),
        scratch_shapes=[
            pltpu.SMEM((group_size, LANES), sunlit.dtype),
            pltpu.VMEM(layer_mass.shape, layer_mass.dtype),
            *[pltpu.VMEM(each.shape, each.dtype) for each in made],
            pltpu.SemaphoreType.DMA((6,)),
            pltpu.SMEM((group_size + 1,), jnp.int32),
            pltpu.VMEM((2, rows, LANES), jnp.float32),
            pltpu.VMEM((levels, 2 * points, LANES), jnp.float32),
            field,
            field,
            field,
            state,
            state,
            state,
            pltpu.VMEM((HALVES, levels + 1, ROWS, LANES), jnp.float32),
            pltpu.VMEM((levels + 1, ROWS, LANES), jnp.float32),
            pltpu.VMEM((blocks, levels, LANES), jnp.float32),
        ],
        compiler_params=pltpu.CompilerParams(vmem_limit_bytes=VMEM_BYTES),
        cost_estimate=pl.CostEstimate(
            flops=40 * levels * points * columns, bytes_accessed=1 << 20, transcendentals=3 * levels * points * columns
        ),
    )(flags, layer_mass, table, scatter, match, dealt)


def solution(mesh):
    placed = (
        P(None, None, ("band", "span")),
        P(None, ("band", "span")),
        P(None, ("band", "span")),
        P(("band", "span")),
        P(("band", "span")),
        P(("band", "span")),
        P(("band", "span")),
        P(),
        P(),
    )
    return jax.shard_map(
        local, mesh=mesh, in_specs=placed, out_specs=P(None, ("band", "span")), check_vma=False
    )
```

```python
import functools
import math

import jax
import jax.numpy as jnp
from jax import lax
from jax.experimental import pallas as pl
from jax.experimental.pallas import tpu as pltpu
from jax.sharding import PartitionSpec as P

LANES = 128
ROWS = 8
PACK = 16
STEP = 4
HALVES = 2
BIN_ROWS = 64
LOG2E = math.log2(math.e)
VMEM_BYTES = 63 * 1024 * 1024


def one_hot(hit):
    return jnp.where(hit, 1.0, 0.0).astype(jnp.bfloat16)


def heating_kernel(
    per_peer,
    gases_hbm,
    bins_hbm,
    mass_hbm,
    cosine_hbm,
    ground_hbm,
    order_hbm,
    absorb_hbm,
    scatter_hbm,
    heat_ref,
    owner_ref,
    gases_ref,
    bins_ref,
    mass_ref,
    cosine_ref,
    ground_ref,
    order_ref,
    absorb_ref,
    albedo_ref,
    copied,
    wide_buf,
    table_ref,
    scatter_ref,
    block_ref,
    optic_ref,
    up_buf,
    rise_buf,
    pass_buf,
    refl_buf,
    fall_buf,
    direct_buf,
    gain_buf,
    net_buf,
    warm_ref,
):
    gas_count, levels, columns = gases_ref.shape
    points = table_ref.shape[0]
    bin_count = absorb_ref.shape[1]
    half = points // HALVES
    vregs = half // ROWS
    blocks = columns // LANES
    bin_row = gas_count * levels
    ray_row = bin_row + levels
    first_row = gas_count * BIN_ROWS

    copies = [
        pltpu.make_async_copy(source, target, copied.at[place])
        for place, (source, target) in enumerate(
            (
                (absorb_hbm, absorb_ref),
                (scatter_hbm, albedo_ref),
                (order_hbm, order_ref),
                (cosine_hbm, cosine_ref),
                (ground_hbm, ground_ref),
                (bins_hbm, bins_ref),
                (gases_hbm, gases_ref),
                (mass_hbm, mass_ref),
            )
        )
    ]
    for copy in copies:
        copy.start()

    wide_buf[...] = jnp.zeros_like(wide_buf)
    for copy in copies[:3]:
        copy.wait()

    square = (columns, columns)
    order = jnp.broadcast_to(order_ref[...], square)
    match = one_hot(order == lax.broadcasted_iota(jnp.int32, square, 0))
    place = lax.broadcasted_iota(jnp.int32, (ROWS, columns), 1)
    group = (place // per_peer).astype(jnp.float32).astype(jnp.bfloat16)
    owner_ref[...] = lax.dot_general(group, match, (((1,), (1,)), ((), ())), preferred_element_type=jnp.float32)

    for gas in range(gas_count):
        wide_buf[gas * BIN_ROWS : gas * BIN_ROWS + bin_count, :points] = absorb_ref[gas].astype(jnp.float32)
    wide_buf[first_row : first_row + bin_count, :points] = 0.5 * albedo_ref[...].astype(jnp.float32)
    turned = [
        jnp.transpose(wide_buf[i * LANES : (i + 1) * LANES])[:points].astype(jnp.bfloat16)
        for i in range(wide_buf.shape[0] // LANES)
    ]
    whole = jnp.concatenate(turned, axis=1)
    table_ref[...] = whole[:, :first_row]
    scatter_ref[...] = whole[:, first_row : first_row + BIN_ROWS]
    for copy in copies[3:]:
        copy.wait()

    for block in range(blocks):
        cols = slice(block * LANES, (block + 1) * LANES)
        for gas in range(gas_count):
            block_ref[block, gas * levels : (gas + 1) * levels] = gases_ref[gas, :, cols].astype(jnp.float32)
        block_ref[block, bin_row:ray_row] = bins_ref[:, cols].astype(jnp.float32)
    wide = (1, columns)
    cosines = cosine_ref[...].astype(jnp.float32).reshape(wide)
    grounds = ground_ref[...].astype(jnp.float32).reshape(wide)
    for block in range(blocks):
        cols = slice(block * LANES, (block + 1) * LANES)
        block_ref[block, ray_row : ray_row + ROWS] = jnp.broadcast_to(cosines[:, cols], (ROWS, LANES))
        block_ref[block, ray_row + ROWS : ray_row + 2 * ROWS] = jnp.broadcast_to(grounds[:, cols], (ROWS, LANES))

    def optical(slot, layer):
        parts = []
        shape = (BIN_ROWS, LANES)
        rows = lax.broadcasted_iota(jnp.int32, shape, 0).astype(jnp.float32)
        selectors = []
        for near in (layer, layer + 1):
            place = bin_row + near
            bins = jnp.broadcast_to(block_ref[slot, place : place + 1, :], shape)
            selectors.append(one_hot(bins == rows))
        for gas in range(gas_count):
            pair = []
            for near, selector in zip((layer, layer + 1), selectors):
                place = gas * levels + near
                amount = jnp.broadcast_to(block_ref[slot, place : place + 1, :], (PACK, LANES)).astype(jnp.bfloat16)
                pair.append(jnp.concatenate([amount] * (BIN_ROWS // PACK), axis=0) * selector)
            parts.append(jnp.concatenate(pair, axis=1))
        weighted = jnp.concatenate(parts, axis=0)
        selected = jnp.concatenate(selectors, axis=1)
        tau = jnp.dot(table_ref[...], weighted, preferred_element_type=jnp.float32)
        albedo = jnp.dot(scatter_ref[...], selected, preferred_element_type=jnp.float32)
        for near in range(2):
            cols = slice(near * LANES, (near + 1) * LANES)
            optic_ref[layer + near, :points] = tau[:, cols]
            optic_ref[layer + near, points:] = albedo[:, cols]

    def advance(first, part, slope):
        rows = slice(part * half, (part + 1) * half)
        half_rows = slice(points + part * half, points + (part + 1) * half)
        shape = (vregs, ROWS, LANES)
        refl = refl_buf[rows].reshape(shape)
        fall = fall_buf[rows].reshape(shape)
        direct = direct_buf[rows].reshape(shape)
        for layer in range(first, first + STEP):
            tau = optic_ref[layer, rows].reshape(shape)
            half_albedo = optic_ref[layer, half_rows].reshape(shape)
            fading = jnp.exp2(tau * (-1.66 * LOG2E))
            passed = jnp.exp2(tau * slope)
            reflect = half_albedo * (1.0 - fading)
            transmit = fading + reflect
            below = direct * passed
            source = half_albedo * (direct - below)
            pass_buf[layer, rows] = (1.0 - refl).reshape(half, LANES)
            inverse = pl.reciprocal(1.0 - reflect * refl, approx=True)
            up = transmit * inverse
            rise = (reflect * fall + source) * inverse
            up_buf[layer, rows] = up.reshape(half, LANES)
            rise_buf[layer, rows] = rise.reshape(half, LANES)
            fall = source + transmit * (fall + refl * rise)
            refl = reflect + transmit * (refl * up)
            direct = below
            gain_buf[part, layer + 1] = jnp.sum(direct + fall, axis=0)
        refl_buf[rows] = refl.reshape(half, LANES)
        fall_buf[rows] = fall.reshape(half, LANES)
        direct_buf[rows] = direct.reshape(half, LANES)

    lead = range(0, STEP, 2)

    def column_block(block, carry):
        cosine = block_ref[block, ray_row : ray_row + ROWS]
        slope = (-LOG2E) / cosine
        refl_buf[...] = jnp.zeros_like(refl_buf)
        fall_buf[...] = jnp.zeros_like(fall_buf)
        direct_buf[...] = jnp.broadcast_to(cosine[:1], direct_buf.shape)
        for part in range(HALVES):
            gain_buf[part, 0] = cosine * float(vregs)
        for first in range(0, levels, STEP):
            coming = [layer for layer in range(first + STEP, first + 2 * STEP, 2) if layer < levels]
            for part in range(HALVES):
                for layer in coming[part * len(coming) // HALVES : (part + 1) * len(coming) // HALVES]:
                    optical(block, layer)
                advance(first, part, slope)

        following = jnp.minimum(block + 1, blocks - 1)
        for layer in lead:
            optical(following, layer)

        albedo = block_ref[block, ray_row + ROWS : ray_row + 2 * ROWS]
        shape = (points // ROWS, ROWS, LANES)
        refl = refl_buf[...].reshape(shape)
        arriving = (fall_buf[...] + direct_buf[...]).reshape(shape)
        rising = albedo * arriving * pl.reciprocal(1.0 - albedo * refl, approx=True)

        def total(level):
            summed = gain_buf[0, level]
            for part in range(1, HALVES):
                summed = summed + gain_buf[part, level]
            return summed

        net_buf[levels] = total(levels) - jnp.sum(rising * (1.0 - refl), axis=0)
        for layer in range(levels - 1, -1, -1):
            rising = up_buf[layer].reshape(shape) * rising + rise_buf[layer].reshape(shape)
            net_buf[layer] = total(layer) - jnp.sum(rising * pass_buf[layer].reshape(shape), axis=0)
        warm_ref[block] = jnp.sum(net_buf[:levels] - net_buf[1:], axis=1)
        return carry

    for layer in lead:
        optical(0, layer)
    lax.fori_loop(0, blocks, column_block, 0)

    for block in range(blocks):
        cols = slice(block * LANES, (block + 1) * LANES)
        heat_ref[:, cols] = warm_ref[block] / mass_ref[:, cols].astype(jnp.float32)


def shade_kernel(heat_hbm, owner_hbm, flags_hbm, out_ref, heat_ref, owner_ref, flags_ref, copied):
    copies = [
        pltpu.make_async_copy(source, target, copied.at[place])
        for place, (source, target) in enumerate(
            ((heat_hbm, heat_ref), (owner_hbm, owner_ref), (flags_hbm, flags_ref))
        )
    ]
    for copy in copies:
        copy.start()
    for copy in copies:
        copy.wait()
    owner = owner_ref[...]
    lit = jnp.zeros_like(owner)
    for group in range(flags_ref.shape[0]):
        flag = jnp.broadcast_to(flags_ref[group].astype(jnp.float32), owner.shape)
        lit = jnp.where(owner == float(group), flag, lit)
    out_ref[...] = heat_ref[...] * lit[:1]


def local(
    gases,
    pressure_bin,
    layer_mass,
    cos_zenith,
    surface_albedo,
    column_order,
    sunlit,
    absorption,
    scattering,
):
    group_size = lax.axis_size("span")
    gas_count, levels, columns = gases.shape
    points, _, bins = absorption.shape
    block_count = sunlit.shape[0]
    wanted = jnp.broadcast_to(sunlit[:, None], (block_count, group_size // block_count)).reshape(group_size, 1, 1)
    flags = lax.all_to_all(wanted, "span", split_axis=0, concat_axis=0, tiled=True)
    field = pltpu.VMEM((levels, points, LANES), jnp.float32)
    state = pltpu.VMEM((points, LANES), jnp.float32)
    rows = gas_count * levels + levels + PACK
    blocks = columns // LANES
    heat, owner = pl.pallas_call(
        functools.partial(heating_kernel, columns // group_size),
        out_shape=(
            jax.ShapeDtypeStruct((levels, columns), jnp.float32),
            jax.ShapeDtypeStruct((ROWS, columns), jnp.float32),
        ),
        in_specs=[pl.BlockSpec(memory_space=pltpu.HBM)] * 8,
        out_specs=(pl.BlockSpec(memory_space=pltpu.VMEM),) * 2,
        scratch_shapes=[
            pltpu.VMEM(gases.shape, gases.dtype),
            pltpu.VMEM(pressure_bin.shape, pressure_bin.dtype),
            pltpu.VMEM(layer_mass.shape, layer_mass.dtype),
            pltpu.VMEM(cos_zenith.shape, cos_zenith.dtype),
            pltpu.VMEM(surface_albedo.shape, surface_albedo.dtype),
            pltpu.VMEM((1, columns), column_order.dtype),
            pltpu.VMEM((gas_count, bins, points), absorption.dtype),
            pltpu.VMEM((bins, points), scattering.dtype),
            pltpu.SemaphoreType.DMA((8,)),
            pltpu.VMEM((-(-(gas_count + 1) * BIN_ROWS // LANES) * LANES, LANES), jnp.float32),
            pltpu.VMEM((points, gas_count * BIN_ROWS), jnp.bfloat16),
            pltpu.VMEM((points, BIN_ROWS), jnp.bfloat16),
            pltpu.VMEM((blocks, rows, LANES), jnp.float32),
            pltpu.VMEM((levels, 2 * points, LANES), jnp.float32),
            field,
            field,
            field,
            state,
            state,
            state,
            pltpu.VMEM((HALVES, levels + 1, ROWS, LANES), jnp.float32),
            pltpu.VMEM((levels + 1, ROWS, LANES), jnp.float32),
            pltpu.VMEM((blocks, levels, LANES), jnp.float32),
        ],
        compiler_params=pltpu.CompilerParams(vmem_limit_bytes=VMEM_BYTES),
        cost_estimate=pl.CostEstimate(
            flops=40 * levels * points * columns, bytes_accessed=1 << 20, transcendentals=3 * levels * points * columns
        ),
    )(
        gases,
        pressure_bin,
        layer_mass,
        cos_zenith,
        surface_albedo,
        column_order.reshape(1, columns),
        jnp.transpose(absorption, (1, 2, 0)),
        jnp.transpose(scattering),
    )
    return pl.pallas_call(
        shade_kernel,
        out_shape=jax.ShapeDtypeStruct(heat.shape, heat.dtype),
        in_specs=[pl.BlockSpec(memory_space=pltpu.HBM)] * 3,
        out_specs=pl.BlockSpec(memory_space=pltpu.VMEM),
        scratch_shapes=[
            pltpu.VMEM(heat.shape, heat.dtype),
            pltpu.VMEM(owner.shape, owner.dtype),
            pltpu.VMEM(flags.shape, flags.dtype),
            pltpu.SemaphoreType.DMA((3,)),
        ],
        compiler_params=pltpu.CompilerParams(vmem_limit_bytes=VMEM_BYTES),
    )(heat, owner, flags)


def solution(mesh):
    placed = (
        P(None, None, ("band", "span")),
        P(None, ("band", "span")),
        P(None, ("band", "span")),
        P(("band", "span")),
        P(("band", "span")),
        P(("band", "span")),
        P(("band", "span")),
        P(),
        P(),
    )
    return jax.shard_map(
        local, mesh=mesh, in_specs=placed, out_specs=P(None, ("band", "span")), check_vma=False
    )
```

```python
import functools
import math

import jax
import jax.numpy as jnp
from jax import lax
from jax.experimental import pallas as pl
from jax.experimental.pallas import tpu as pltpu
from jax.sharding import PartitionSpec as P

LANES = 128
ROWS = 8
PACK = 16
STEP = 8
HALVES = 2
BIN_ROWS = 64
LOG2E = math.log2(math.e)
VMEM_BYTES = 63 * 1024 * 1024
SHADE_BYTES = 55200 * 1024


def one_hot(hit):
    return jnp.where(hit, 1.0, 0.0).astype(jnp.bfloat16)


def heating_kernel(
    per_peer,
    gases_hbm,
    bins_hbm,
    mass_hbm,
    cosine_hbm,
    ground_hbm,
    order_hbm,
    absorb_hbm,
    scatter_hbm,
    heat_ref,
    gases_ref,
    bins_ref,
    mass_ref,
    cosine_ref,
    ground_ref,
    order_ref,
    absorb_ref,
    albedo_ref,
    copied,
    wide_buf,
    table_ref,
    scatter_ref,
    block_ref,
    optic_ref,
    up_buf,
    rise_buf,
    pass_buf,
    refl_buf,
    fall_buf,
    direct_buf,
    gain_buf,
    net_buf,
    warm_ref,
):
    gas_count, levels, columns = gases_ref.shape
    points = table_ref.shape[0]
    bin_count = absorb_ref.shape[1]
    half = points // HALVES
    vregs = half // ROWS
    blocks = columns // LANES
    bin_row = gas_count * levels
    ray_row = bin_row + levels
    first_row = gas_count * BIN_ROWS

    copies = [
        pltpu.make_async_copy(source, target, copied.at[place])
        for place, (source, target) in enumerate(
            (
                (absorb_hbm, absorb_ref),
                (scatter_hbm, albedo_ref),
                (order_hbm, order_ref),
                (cosine_hbm, cosine_ref),
                (ground_hbm, ground_ref),
                (bins_hbm, bins_ref),
                (gases_hbm, gases_ref),
                (mass_hbm, mass_ref),
            )
        )
    ]
    for copy in copies:
        copy.start()

    wide_buf[...] = jnp.zeros_like(wide_buf)
    for copy in copies[:3]:
        copy.wait()

    square = (columns, columns)
    order = jnp.broadcast_to(order_ref[...], square)
    match = one_hot(order == lax.broadcasted_iota(jnp.int32, square, 0))
    place = lax.broadcasted_iota(jnp.int32, (ROWS, columns), 1)
    group = (place // per_peer).astype(jnp.float32).astype(jnp.bfloat16)
    heat_ref[levels:] = lax.dot_general(group, match, (((1,), (1,)), ((), ())), preferred_element_type=jnp.float32)

    for gas in range(gas_count):
        wide_buf[gas * BIN_ROWS : gas * BIN_ROWS + bin_count, :points] = absorb_ref[gas].astype(jnp.float32)
    wide_buf[first_row : first_row + bin_count, :points] = 0.5 * albedo_ref[...].astype(jnp.float32)
    turned = [
        jnp.transpose(wide_buf[i * LANES : (i + 1) * LANES])[:points].astype(jnp.bfloat16)
        for i in range(wide_buf.shape[0] // LANES)
    ]
    whole = jnp.concatenate(turned, axis=1)
    table_ref[...] = whole[:, :first_row]
    scatter_ref[...] = whole[:, first_row : first_row + BIN_ROWS]
    for copy in copies[3:]:
        copy.wait()

    for block in range(blocks):
        cols = slice(block * LANES, (block + 1) * LANES)
        for gas in range(gas_count):
            block_ref[block, gas * levels : (gas + 1) * levels] = gases_ref[gas, :, cols].astype(jnp.float32)
        block_ref[block, bin_row:ray_row] = bins_ref[:, cols].astype(jnp.float32)
    wide = (1, columns)
    cosines = cosine_ref[...].astype(jnp.float32).reshape(wide)
    grounds = ground_ref[...].astype(jnp.float32).reshape(wide)
    for block in range(blocks):
        cols = slice(block * LANES, (block + 1) * LANES)
        block_ref[block, ray_row : ray_row + ROWS] = jnp.broadcast_to(cosines[:, cols], (ROWS, LANES))
        block_ref[block, ray_row + ROWS : ray_row + 2 * ROWS] = jnp.broadcast_to(grounds[:, cols], (ROWS, LANES))

    def optical(slot, layer):
        parts = []
        shape = (BIN_ROWS, LANES)
        rows = lax.broadcasted_iota(jnp.int32, shape, 0).astype(jnp.float32).astype(jnp.bfloat16)
        one = jnp.ones(shape, jnp.bfloat16)
        zero = jnp.zeros(shape, jnp.bfloat16)
        selectors = []
        for near in (layer, layer + 1):
            place = bin_row + near
            bins = jnp.broadcast_to(block_ref[slot, place : place + 1, :], (PACK, LANES)).astype(jnp.bfloat16)
            bins = jnp.concatenate([bins] * (BIN_ROWS // PACK), axis=0)
            selectors.append(jnp.where(bins == rows, one, zero))
        for gas in range(gas_count):
            pair = []
            for near, selector in zip((layer, layer + 1), selectors):
                place = gas * levels + near
                amount = jnp.broadcast_to(block_ref[slot, place : place + 1, :], (PACK, LANES)).astype(jnp.bfloat16)
                pair.append(jnp.concatenate([amount] * (BIN_ROWS // PACK), axis=0) * selector)
            parts.append(jnp.concatenate(pair, axis=1))
        weighted = jnp.concatenate(parts, axis=0)
        selected = jnp.concatenate(selectors, axis=1)
        tau = jnp.dot(table_ref[...], weighted, preferred_element_type=jnp.float32)
        albedo = jnp.dot(scatter_ref[...], selected, preferred_element_type=jnp.float32)
        for near in range(2):
            cols = slice(near * LANES, (near + 1) * LANES)
            optic_ref[layer + near, :points] = tau[:, cols]
            optic_ref[layer + near, points:] = albedo[:, cols]

    def advance(first, part, cosine, slope):
        rows = slice(part * half, (part + 1) * half)
        half_rows = slice(points + part * half, points + (part + 1) * half)
        shape = (vregs, ROWS, LANES)
        if first > 0:
            refl = refl_buf[rows].reshape(shape)
            fall = fall_buf[rows].reshape(shape)
            direct = direct_buf[rows].reshape(shape)
        else:
            direct = jnp.broadcast_to(cosine[None], shape)
        for layer in range(first, first + STEP):
            tau = optic_ref[layer, rows].reshape(shape)
            half_albedo = optic_ref[layer, half_rows].reshape(shape)
            fading = jnp.exp2(tau * (-1.66 * LOG2E))
            passed = jnp.exp2(tau * slope)
            reflect = half_albedo * (1.0 - fading)
            transmit = fading + reflect
            below = direct * passed
            source = half_albedo * (direct - below)
            if layer == 0:
                up_buf[layer, rows] = transmit.reshape(half, LANES)
                rise_buf[layer, rows] = source.reshape(half, LANES)
                fall = source
                refl = reflect
            else:
                pass_buf[layer, rows] = (1.0 - refl).reshape(half, LANES)
                inverse = pl.reciprocal(1.0 - reflect * refl, approx=True)
                up = transmit * inverse
                rise = (reflect * fall + source) * inverse
                up_buf[layer, rows] = up.reshape(half, LANES)
                rise_buf[layer, rows] = rise.reshape(half, LANES)
                fall = source + transmit * (fall + refl * rise)
                refl = reflect + transmit * (refl * up)
            direct = below
            gain_buf[part, layer + 1] = jnp.sum(direct + fall, axis=0)
        refl_buf[rows] = refl.reshape(half, LANES)
        fall_buf[rows] = fall.reshape(half, LANES)
        direct_buf[rows] = direct.reshape(half, LANES)

    lead = range(0, STEP, 2)

    def column_block(block, carry):
        cosine = block_ref[block, ray_row : ray_row + ROWS]
        slope = (-LOG2E) / cosine
        for part in range(HALVES):
            gain_buf[part, 0] = cosine * float(vregs)
        for first in range(0, levels, STEP):
            coming = [layer for layer in range(first + STEP, first + 2 * STEP, 2) if layer < levels]
            for part in range(HALVES):
                for layer in coming[part * len(coming) // HALVES : (part + 1) * len(coming) // HALVES]:
                    optical(block, layer)
                advance(first, part, cosine, slope)

        following = jnp.minimum(block + 1, blocks - 1)
        for layer in lead:
            optical(following, layer)

        albedo = block_ref[block, ray_row + ROWS : ray_row + 2 * ROWS]
        shape = (points // ROWS, ROWS, LANES)
        refl = refl_buf[...].reshape(shape)
        arriving = (fall_buf[...] + direct_buf[...]).reshape(shape)
        rising = albedo * arriving * pl.reciprocal(1.0 - albedo * refl, approx=True)

        def total(level):
            summed = gain_buf[0, level]
            for part in range(1, HALVES):
                summed = summed + gain_buf[part, level]
            return summed

        net_buf[levels] = total(levels) - jnp.sum(rising * (1.0 - refl), axis=0)
        for layer in range(levels - 1, -1, -1):
            rising = up_buf[layer].reshape(shape) * rising + rise_buf[layer].reshape(shape)
            taken = rising if layer == 0 else rising * pass_buf[layer].reshape(shape)
            net_buf[layer] = total(layer) - jnp.sum(taken, axis=0)
        warm_ref[block] = jnp.sum(net_buf[:levels] - net_buf[1:], axis=1)
        return carry

    for layer in lead:
        optical(0, layer)
    lax.fori_loop(0, blocks, column_block, 0)

    for block in range(blocks):
        cols = slice(block * LANES, (block + 1) * LANES)
        heat_ref[:levels, cols] = warm_ref[block] / mass_ref[:, cols].astype(jnp.float32)


def shade_kernel(heat_hbm, flags_ref, out_ref, heat_ref, copied):
    copy = pltpu.make_async_copy(heat_hbm, heat_ref, copied)
    copy.start()
    copy.wait()
    levels = out_ref.shape[0]
    owner = heat_ref[levels:]
    lit = jnp.zeros_like(owner)
    for group in range(flags_ref.shape[0]):
        flag = jnp.broadcast_to(flags_ref[group].astype(jnp.float32), owner.shape)
        lit = jnp.where(owner == float(group), flag, lit)
    out_ref[...] = heat_ref[:levels] * lit[:1]


def local(
    gases,
    pressure_bin,
    layer_mass,
    cos_zenith,
    surface_albedo,
    column_order,
    sunlit,
    absorption,
    scattering,
):
    group_size = lax.axis_size("span")
    gas_count, levels, columns = gases.shape
    points, _, bins = absorption.shape
    block_count = sunlit.shape[0]
    wanted = jnp.broadcast_to(sunlit[:, None], (block_count, group_size // block_count)).reshape(group_size, 1, 1)
    flags = lax.all_to_all(wanted, "span", split_axis=0, concat_axis=0, tiled=True)
    field = pltpu.VMEM((levels, points, LANES), jnp.float32)
    state = pltpu.VMEM((points, LANES), jnp.float32)
    rows = gas_count * levels + levels + PACK
    blocks = columns // LANES
    heat = pl.pallas_call(
        functools.partial(heating_kernel, columns // group_size),
        out_shape=jax.ShapeDtypeStruct((levels + ROWS, columns), jnp.float32),
        in_specs=[pl.BlockSpec(memory_space=pltpu.HBM)] * 8,
        out_specs=pl.BlockSpec(memory_space=pltpu.VMEM),
        scratch_shapes=[
            pltpu.VMEM(gases.shape, gases.dtype),
            pltpu.VMEM(pressure_bin.shape, pressure_bin.dtype),
            pltpu.VMEM(layer_mass.shape, layer_mass.dtype),
            pltpu.VMEM(cos_zenith.shape, cos_zenith.dtype),
            pltpu.VMEM(surface_albedo.shape, surface_albedo.dtype),
            pltpu.VMEM((1, columns), column_order.dtype),
            pltpu.VMEM((gas_count, bins, points), absorption.dtype),
            pltpu.VMEM((bins, points), scattering.dtype),
            pltpu.SemaphoreType.DMA((8,)),
            pltpu.VMEM((-(-(gas_count + 1) * BIN_ROWS // LANES) * LANES, LANES), jnp.float32),
            pltpu.VMEM((points, gas_count * BIN_ROWS), jnp.bfloat16),
            pltpu.VMEM((points, BIN_ROWS), jnp.bfloat16),
            pltpu.VMEM((blocks, rows, LANES), jnp.float32),
            pltpu.VMEM((levels, 2 * points, LANES), jnp.float32),
            field,
            field,
            field,
            state,
            state,
            state,
            pltpu.VMEM((HALVES, levels + 1, ROWS, LANES), jnp.float32),
            pltpu.VMEM((levels + 1, ROWS, LANES), jnp.float32),
            pltpu.VMEM((blocks, levels, LANES), jnp.float32),
        ],
        compiler_params=pltpu.CompilerParams(vmem_limit_bytes=VMEM_BYTES),
        cost_estimate=pl.CostEstimate(
            flops=40 * levels * points * columns, bytes_accessed=1 << 20, transcendentals=3 * levels * points * columns
        ),
    )(
        gases,
        pressure_bin,
        layer_mass,
        cos_zenith,
        surface_albedo,
        column_order.reshape(1, columns),
        jnp.transpose(absorption, (1, 2, 0)),
        jnp.transpose(scattering),
    )
    return pl.pallas_call(
        shade_kernel,
        out_shape=jax.ShapeDtypeStruct((levels, columns), heat.dtype),
        in_specs=[pl.BlockSpec(memory_space=pltpu.HBM), pl.BlockSpec(memory_space=pltpu.VMEM)],
        out_specs=pl.BlockSpec(memory_space=pltpu.VMEM),
        scratch_shapes=[
            pltpu.VMEM(heat.shape, heat.dtype),
            pltpu.SemaphoreType.DMA(()),
        ],
        compiler_params=pltpu.CompilerParams(vmem_limit_bytes=SHADE_BYTES),
    )(heat, flags)


def solution(mesh):
    placed = (
        P(None, None, ("band", "span")),
        P(None, ("band", "span")),
        P(None, ("band", "span")),
        P(("band", "span")),
        P(("band", "span")),
        P(("band", "span")),
        P(("band", "span")),
        P(),
        P(),
    )
    return jax.shard_map(
        local, mesh=mesh, in_specs=placed, out_specs=P(None, ("band", "span")), check_vma=False
    )
```

```python
import functools
import math

import jax
import jax.numpy as jnp
from jax import lax
from jax.experimental import pallas as pl
from jax.experimental.pallas import tpu as pltpu
from jax.sharding import PartitionSpec as P

LANES = 128
ROWS = 8
PACK = 16
STEP = 8
HALVES = 2
BIN_ROWS = 64
LOG2E = math.log2(math.e)
VMEM_BYTES = 63 * 1024 * 1024
SHADE_BYTES = 55200 * 1024


def one_hot(hit):
    return jnp.where(hit, 1.0, 0.0).astype(jnp.bfloat16)


def heating_kernel(
    per_peer,
    gases_hbm,
    bins_hbm,
    mass_hbm,
    cosine_hbm,
    ground_hbm,
    order_hbm,
    absorb_hbm,
    scatter_hbm,
    heat_ref,
    gases_ref,
    bins_ref,
    mass_ref,
    cosine_ref,
    ground_ref,
    order_ref,
    absorb_ref,
    albedo_ref,
    copied,
    wide_buf,
    table_ref,
    mixed_ref,
    block_ref,
    optic_ref,
    up_buf,
    rise_buf,
    pass_buf,
    refl_buf,
    fall_buf,
    direct_buf,
    gain_buf,
    net_buf,
    warm_ref,
):
    gas_count, levels, columns = gases_ref.shape
    points, split = table_ref.shape
    bin_count = absorb_ref.shape[1]
    half = points // HALVES
    vregs = half // ROWS
    blocks = columns // LANES
    bin_row = gas_count * levels
    ray_row = bin_row + levels
    first_row = gas_count * BIN_ROWS

    copies = [
        pltpu.make_async_copy(source, target, copied.at[place])
        for place, (source, target) in enumerate(
            (
                (absorb_hbm, absorb_ref),
                (scatter_hbm, albedo_ref),
                (order_hbm, order_ref),
                (cosine_hbm, cosine_ref),
                (ground_hbm, ground_ref),
                (bins_hbm, bins_ref),
                (gases_hbm, gases_ref),
                (mass_hbm, mass_ref),
            )
        )
    ]
    for copy in copies:
        copy.start()

    wide_buf[...] = jnp.zeros_like(wide_buf)
    for copy in copies[:3]:
        copy.wait()

    square = (columns, columns)
    order = jnp.broadcast_to(order_ref[...], square)
    match = one_hot(order == lax.broadcasted_iota(jnp.int32, square, 0))
    place = lax.broadcasted_iota(jnp.int32, (ROWS, columns), 1)
    group = (place // per_peer).astype(jnp.float32).astype(jnp.bfloat16)
    heat_ref[levels:] = lax.dot_general(group, match, (((1,), (1,)), ((), ())), preferred_element_type=jnp.float32)

    for gas in range(gas_count):
        wide_buf[gas * BIN_ROWS : gas * BIN_ROWS + bin_count, :points] = absorb_ref[gas].astype(jnp.float32)
    wide_buf[first_row : first_row + bin_count, :points] = 0.5 * albedo_ref[...].astype(jnp.float32)
    turned = [
        jnp.transpose(wide_buf[i * LANES : (i + 1) * LANES])[:points]
        for i in range(wide_buf.shape[0] // LANES)
    ]
    whole = jnp.concatenate(turned, axis=1)
    table_ref[...] = whole[:, :split].astype(jnp.bfloat16)
    rest = whole[:, split:]
    gas_lane = lax.broadcasted_iota(jnp.int32, rest.shape, 1) < first_row - split
    mixed_ref[:points] = jnp.where(gas_lane, rest, 0.0).astype(jnp.bfloat16)
    mixed_ref[points:] = jnp.where(gas_lane, 0.0, rest).astype(jnp.bfloat16)
    for copy in copies[3:]:
        copy.wait()

    for block in range(blocks):
        cols = slice(block * LANES, (block + 1) * LANES)
        for gas in range(gas_count):
            block_ref[block, gas * levels : (gas + 1) * levels] = gases_ref[gas, :, cols].astype(jnp.float32)
        block_ref[block, bin_row:ray_row] = bins_ref[:, cols].astype(jnp.float32)
    wide = (1, columns)
    cosines = cosine_ref[...].astype(jnp.float32).reshape(wide)
    grounds = ground_ref[...].astype(jnp.float32).reshape(wide)
    for block in range(blocks):
        cols = slice(block * LANES, (block + 1) * LANES)
        block_ref[block, ray_row : ray_row + ROWS] = jnp.broadcast_to(cosines[:, cols], (ROWS, LANES))
        block_ref[block, ray_row + ROWS : ray_row + 2 * ROWS] = jnp.broadcast_to(grounds[:, cols], (ROWS, LANES))

    def optical(slot, layer):
        parts = []
        shape = (BIN_ROWS, LANES)
        rows = lax.broadcasted_iota(jnp.int32, shape, 0).astype(jnp.float32).astype(jnp.bfloat16)
        one = jnp.ones(shape, jnp.bfloat16)
        zero = jnp.zeros(shape, jnp.bfloat16)
        selectors = []
        for near in (layer, layer + 1):
            place = bin_row + near
            bins = jnp.broadcast_to(block_ref[slot, place : place + 1, :], (PACK, LANES)).astype(jnp.bfloat16)
            bins = jnp.concatenate([bins] * (BIN_ROWS // PACK), axis=0)
            selectors.append(jnp.where(bins == rows, one, zero))
        for gas in range(gas_count):
            pair = []
            for near, selector in zip((layer, layer + 1), selectors):
                place = gas * levels + near
                amount = jnp.broadcast_to(block_ref[slot, place : place + 1, :], (PACK, LANES)).astype(jnp.bfloat16)
                pair.append(jnp.concatenate([amount] * (BIN_ROWS // PACK), axis=0) * selector)
            parts.append(jnp.concatenate(pair, axis=1))
        parts.append(jnp.concatenate(selectors, axis=1))
        weighted = jnp.concatenate(parts, axis=0)
        tau = jnp.dot(table_ref[...], weighted[:split], preferred_element_type=jnp.float32)
        mixed = jnp.dot(mixed_ref[...], weighted[split:], preferred_element_type=jnp.float32)
        for near in range(2):
            cols = slice(near * LANES, (near + 1) * LANES)
            optic_ref[layer + near, :points] = tau[:, cols] + mixed[:points, cols]
            optic_ref[layer + near, points:] = mixed[points:, cols]

    def advance(first, part, cosine, slope):
        rows = slice(part * half, (part + 1) * half)
        half_rows = slice(points + part * half, points + (part + 1) * half)
        shape = (vregs, ROWS, LANES)
        if first > 0:
            refl = refl_buf[rows].reshape(shape)
            fall = fall_buf[rows].reshape(shape)
            direct = direct_buf[rows].reshape(shape)
        else:
            direct = jnp.broadcast_to(cosine[None], shape)
        for layer in range(first, first + STEP):
            tau = optic_ref[layer, rows].reshape(shape)
            half_albedo = optic_ref[layer, half_rows].reshape(shape)
            fading = jnp.exp2(tau * (-1.66 * LOG2E))
            passed = jnp.exp2(tau * slope)
            reflect = half_albedo * (1.0 - fading)
            transmit = fading + reflect
            below = direct * passed
            source = half_albedo * (direct - below)
            if layer == 0:
                up_buf[layer, rows] = transmit.reshape(half, LANES)
                rise_buf[layer, rows] = source.reshape(half, LANES)
                fall = source
                refl = reflect
            else:
                pass_buf[layer, rows] = (1.0 - refl).reshape(half, LANES)
                inverse = pl.reciprocal(1.0 - reflect * refl, approx=True)
                up = transmit * inverse
                rise = (reflect * fall + source) * inverse
                up_buf[layer, rows] = up.reshape(half, LANES)
                rise_buf[layer, rows] = rise.reshape(half, LANES)
                fall = source + transmit * (fall + refl * rise)
                refl = reflect + transmit * (refl * up)
            direct = below
            gain_buf[part, layer + 1] = jnp.sum(direct + fall, axis=0)
        refl_buf[rows] = refl.reshape(half, LANES)
        fall_buf[rows] = fall.reshape(half, LANES)
        direct_buf[rows] = direct.reshape(half, LANES)

    lead = range(0, STEP, 2)

    def column_block(block, carry):
        cosine = block_ref[block, ray_row : ray_row + ROWS]
        slope = (-LOG2E) / cosine
        for part in range(HALVES):
            gain_buf[part, 0] = cosine * float(vregs)
        for first in range(0, levels, STEP):
            coming = [layer for layer in range(first + STEP, first + 2 * STEP, 2) if layer < levels]
            for part in range(HALVES):
                for layer in coming[part * len(coming) // HALVES : (part + 1) * len(coming) // HALVES]:
                    optical(block, layer)
                advance(first, part, cosine, slope)

        following = jnp.minimum(block + 1, blocks - 1)
        for layer in lead:
            optical(following, layer)

        albedo = block_ref[block, ray_row + ROWS : ray_row + 2 * ROWS]
        shape = (points // ROWS, ROWS, LANES)
        refl = refl_buf[...].reshape(shape)
        arriving = (fall_buf[...] + direct_buf[...]).reshape(shape)
        rising = albedo * arriving * pl.reciprocal(1.0 - albedo * refl, approx=True)

        def total(level):
            summed = gain_buf[0, level]
            for part in range(1, HALVES):
                summed = summed + gain_buf[part, level]
            return summed

        net_buf[levels] = total(levels) - jnp.sum(rising * (1.0 - refl), axis=0)
        for layer in range(levels - 1, -1, -1):
            rising = up_buf[layer].reshape(shape) * rising + rise_buf[layer].reshape(shape)
            taken = rising if layer == 0 else rising * pass_buf[layer].reshape(shape)
            net_buf[layer] = total(layer) - jnp.sum(taken, axis=0)
        warm_ref[block] = jnp.sum(net_buf[:levels] - net_buf[1:], axis=1)
        return carry

    for layer in lead:
        optical(0, layer)
    lax.fori_loop(0, blocks, column_block, 0)

    for block in range(blocks):
        cols = slice(block * LANES, (block + 1) * LANES)
        heat_ref[:levels, cols] = warm_ref[block] / mass_ref[:, cols].astype(jnp.float32)


def shade_kernel(heat_hbm, flags_ref, out_ref, heat_ref, copied):
    copy = pltpu.make_async_copy(heat_hbm, heat_ref, copied)
    copy.start()
    copy.wait()
    levels = out_ref.shape[0]
    owner = heat_ref[levels:]
    lit = jnp.zeros_like(owner)
    for group in range(flags_ref.shape[0]):
        flag = jnp.broadcast_to(flags_ref[group].astype(jnp.float32), owner.shape)
        lit = jnp.where(owner == float(group), flag, lit)
    out_ref[...] = heat_ref[:levels] * lit[:1]


def local(
    gases,
    pressure_bin,
    layer_mass,
    cos_zenith,
    surface_albedo,
    column_order,
    sunlit,
    absorption,
    scattering,
):
    group_size = lax.axis_size("span")
    gas_count, levels, columns = gases.shape
    points, _, bins = absorption.shape
    block_count = sunlit.shape[0]
    wanted = jnp.broadcast_to(sunlit[:, None], (block_count, group_size // block_count)).reshape(group_size, 1, 1)
    flags = lax.all_to_all(wanted, "span", split_axis=0, concat_axis=0, tiled=True)
    field = pltpu.VMEM((levels, points, LANES), jnp.float32)
    state = pltpu.VMEM((points, LANES), jnp.float32)
    rows = gas_count * levels + levels + PACK
    split = (gas_count + 1) * BIN_ROWS // 2 // LANES * LANES
    blocks = columns // LANES
    heat = pl.pallas_call(
        functools.partial(heating_kernel, columns // group_size),
        out_shape=jax.ShapeDtypeStruct((levels + ROWS, columns), jnp.float32),
        in_specs=[pl.BlockSpec(memory_space=pltpu.HBM)] * 8,
        out_specs=pl.BlockSpec(memory_space=pltpu.VMEM),
        scratch_shapes=[
            pltpu.VMEM(gases.shape, gases.dtype),
            pltpu.VMEM(pressure_bin.shape, pressure_bin.dtype),
            pltpu.VMEM(layer_mass.shape, layer_mass.dtype),
            pltpu.VMEM(cos_zenith.shape, cos_zenith.dtype),
            pltpu.VMEM(surface_albedo.shape, surface_albedo.dtype),
            pltpu.VMEM((1, columns), column_order.dtype),
            pltpu.VMEM((gas_count, bins, points), absorption.dtype),
            pltpu.VMEM((bins, points), scattering.dtype),
            pltpu.SemaphoreType.DMA((8,)),
            pltpu.VMEM((-(-(gas_count + 1) * BIN_ROWS // LANES) * LANES, LANES), jnp.float32),
            pltpu.VMEM((points, split), jnp.bfloat16),
            pltpu.VMEM((2 * points, (gas_count + 1) * BIN_ROWS - split), jnp.bfloat16),
            pltpu.VMEM((blocks, rows, LANES), jnp.float32),
            pltpu.VMEM((levels, 2 * points, LANES), jnp.float32),
            field,
            field,
            field,
            state,
            state,
            state,
            pltpu.VMEM((HALVES, levels + 1, ROWS, LANES), jnp.float32),
            pltpu.VMEM((levels + 1, ROWS, LANES), jnp.float32),
            pltpu.VMEM((blocks, levels, LANES), jnp.float32),
        ],
        compiler_params=pltpu.CompilerParams(vmem_limit_bytes=VMEM_BYTES),
        cost_estimate=pl.CostEstimate(
            flops=40 * levels * points * columns, bytes_accessed=1 << 20, transcendentals=3 * levels * points * columns
        ),
    )(
        gases,
        pressure_bin,
        layer_mass,
        cos_zenith,
        surface_albedo,
        column_order.reshape(1, columns),
        jnp.transpose(absorption, (1, 2, 0)),
        jnp.transpose(scattering),
    )
    return pl.pallas_call(
        shade_kernel,
        out_shape=jax.ShapeDtypeStruct((levels, columns), heat.dtype),
        in_specs=[pl.BlockSpec(memory_space=pltpu.HBM), pl.BlockSpec(memory_space=pltpu.VMEM)],
        out_specs=pl.BlockSpec(memory_space=pltpu.VMEM),
        scratch_shapes=[
            pltpu.VMEM(heat.shape, heat.dtype),
            pltpu.SemaphoreType.DMA(()),
        ],
        compiler_params=pltpu.CompilerParams(vmem_limit_bytes=SHADE_BYTES),
    )(heat, flags)


def solution(mesh):
    placed = (
        P(None, None, ("band", "span")),
        P(None, ("band", "span")),
        P(None, ("band", "span")),
        P(("band", "span")),
        P(("band", "span")),
        P(("band", "span")),
        P(("band", "span")),
        P(),
        P(),
    )
    return jax.shard_map(
        local, mesh=mesh, in_specs=placed, out_specs=P(None, ("band", "span")), check_vma=False
    )
```

```python
import functools
import math

import jax
import jax.numpy as jnp
from jax import lax
from jax.experimental import pallas as pl
from jax.experimental.pallas import tpu as pltpu
from jax.sharding import PartitionSpec as P

LANES = 128
ROWS = 8
PACK = 16
STEP = 8
PARTS = 4
BIN_ROWS = 64
LOG2E = math.log2(math.e)
VMEM_BYTES = 63 * 1024 * 1024
SHADE_BYTES = 55200 * 1024


def one_hot(hit):
    return jnp.where(hit, 1.0, 0.0).astype(jnp.bfloat16)


def heating_kernel(
    per_peer,
    gases_hbm,
    bins_hbm,
    mass_hbm,
    cosine_hbm,
    ground_hbm,
    order_hbm,
    absorb_hbm,
    scatter_hbm,
    heat_ref,
    gases_ref,
    bins_ref,
    mass_ref,
    cosine_ref,
    ground_ref,
    order_ref,
    absorb_ref,
    albedo_ref,
    copied,
    wide_buf,
    table_ref,
    scatter_ref,
    block_ref,
    optic_ref,
    up_buf,
    rise_buf,
    pass_buf,
    refl_buf,
    fall_buf,
    direct_buf,
    gain_buf,
    net_buf,
    warm_ref,
):
    gas_count, levels, columns = gases_ref.shape
    points = table_ref.shape[0]
    bin_count = absorb_ref.shape[1]
    edges = [part * (points // ROWS) // PARTS * ROWS for part in range(PARTS + 1)]
    blocks = columns // LANES
    bin_row = gas_count * levels
    ray_row = bin_row + levels
    first_row = gas_count * BIN_ROWS

    copies = [
        pltpu.make_async_copy(source, target, copied.at[place])
        for place, (source, target) in enumerate(
            (
                (absorb_hbm, absorb_ref),
                (scatter_hbm, albedo_ref),
                (order_hbm, order_ref),
                (cosine_hbm, cosine_ref),
                (ground_hbm, ground_ref),
                (bins_hbm, bins_ref),
                (gases_hbm, gases_ref),
                (mass_hbm, mass_ref),
            )
        )
    ]
    for copy in copies:
        copy.start()

    wide_buf[...] = jnp.zeros_like(wide_buf)
    for copy in copies[:3]:
        copy.wait()

    square = (columns, columns)
    order = jnp.broadcast_to(order_ref[...], square)
    match = one_hot(order == lax.broadcasted_iota(jnp.int32, square, 0))
    place = lax.broadcasted_iota(jnp.int32, (ROWS, columns), 1)
    group = (place // per_peer).astype(jnp.float32).astype(jnp.bfloat16)
    heat_ref[levels:] = lax.dot_general(group, match, (((1,), (1,)), ((), ())), preferred_element_type=jnp.float32)

    for gas in range(gas_count):
        wide_buf[gas * BIN_ROWS : gas * BIN_ROWS + bin_count, :points] = absorb_ref[gas].astype(jnp.float32)
    wide_buf[first_row : first_row + bin_count, :points] = 0.5 * albedo_ref[...].astype(jnp.float32)
    turned = [
        jnp.transpose(wide_buf[i * LANES : (i + 1) * LANES])[:points].astype(jnp.bfloat16)
        for i in range(wide_buf.shape[0] // LANES)
    ]
    whole = jnp.concatenate(turned, axis=1)
    table_ref[...] = whole[:, :first_row]
    scatter_ref[...] = whole[:, first_row : first_row + BIN_ROWS]
    for copy in copies[3:]:
        copy.wait()

    for block in range(blocks):
        cols = slice(block * LANES, (block + 1) * LANES)
        for gas in range(gas_count):
            block_ref[block, gas * levels : (gas + 1) * levels] = gases_ref[gas, :, cols].astype(jnp.float32)
        block_ref[block, bin_row:ray_row] = bins_ref[:, cols].astype(jnp.float32)
    wide = (1, columns)
    cosines = cosine_ref[...].astype(jnp.float32).reshape(wide)
    grounds = ground_ref[...].astype(jnp.float32).reshape(wide)
    for block in range(blocks):
        cols = slice(block * LANES, (block + 1) * LANES)
        block_ref[block, ray_row : ray_row + ROWS] = jnp.broadcast_to(cosines[:, cols], (ROWS, LANES))
        block_ref[block, ray_row + ROWS : ray_row + 2 * ROWS] = jnp.broadcast_to(grounds[:, cols], (ROWS, LANES))

    def optical(slot, layer):
        parts = []
        shape = (BIN_ROWS, LANES)
        rows = lax.broadcasted_iota(jnp.int32, shape, 0).astype(jnp.float32).astype(jnp.bfloat16)
        one = jnp.ones(shape, jnp.bfloat16)
        zero = jnp.zeros(shape, jnp.bfloat16)
        selectors = []
        for near in (layer, layer + 1):
            place = bin_row + near
            bins = jnp.broadcast_to(block_ref[slot, place : place + 1, :], (PACK, LANES)).astype(jnp.bfloat16)
            bins = jnp.concatenate([bins] * (BIN_ROWS // PACK), axis=0)
            selectors.append(jnp.where(bins == rows, one, zero))
        for gas in range(gas_count):
            pair = []
            for near, selector in zip((layer, layer + 1), selectors):
                place = gas * levels + near
                amount = jnp.broadcast_to(block_ref[slot, place : place + 1, :], (PACK, LANES)).astype(jnp.bfloat16)
                pair.append(jnp.concatenate([amount] * (BIN_ROWS // PACK), axis=0) * selector)
            parts.append(jnp.concatenate(pair, axis=1))
        weighted = jnp.concatenate(parts, axis=0)
        selected = jnp.concatenate(selectors, axis=1)
        tau = jnp.dot(table_ref[...], weighted, preferred_element_type=jnp.float32)
        albedo = jnp.dot(scatter_ref[...], selected, preferred_element_type=jnp.float32)
        for near in range(2):
            cols = slice(near * LANES, (near + 1) * LANES)
            optic_ref[layer + near, :points] = tau[:, cols]
            optic_ref[layer + near, points:] = albedo[:, cols]

    def advance(first, part, cosine, slope):
        rows = slice(edges[part], edges[part + 1])
        half_rows = slice(points + edges[part], points + edges[part + 1])
        size = edges[part + 1] - edges[part]
        shape = (size // ROWS, ROWS, LANES)
        if first > 0:
            refl = refl_buf[rows].reshape(shape)
            fall = fall_buf[rows].reshape(shape)
            direct = direct_buf[rows].reshape(shape)
        else:
            direct = jnp.broadcast_to(cosine[None], shape)
        for layer in range(first, first + STEP):
            tau = optic_ref[layer, rows].reshape(shape)
            half_albedo = optic_ref[layer, half_rows].reshape(shape)
            fading = jnp.exp2(tau * (-1.66 * LOG2E))
            passed = jnp.exp2(tau * slope)
            reflect = half_albedo * (1.0 - fading)
            transmit = fading + reflect
            below = direct * passed
            source = half_albedo * (direct - below)
            if layer == 0:
                up_buf[layer, rows] = transmit.reshape(size, LANES)
                rise_buf[layer, rows] = source.reshape(size, LANES)
                fall = source
                refl = reflect
            else:
                pass_buf[layer, rows] = (1.0 - refl).reshape(size, LANES)
                inverse = pl.reciprocal(1.0 - reflect * refl, approx=True)
                up = transmit * inverse
                rise = (reflect * fall + source) * inverse
                up_buf[layer, rows] = up.reshape(size, LANES)
                rise_buf[layer, rows] = rise.reshape(size, LANES)
                fall = source + transmit * (fall + refl * rise)
                refl = reflect + transmit * (refl * up)
            direct = below
            gain_buf[part, layer + 1] = jnp.sum(direct + fall, axis=0)
        refl_buf[rows] = refl.reshape(size, LANES)
        fall_buf[rows] = fall.reshape(size, LANES)
        direct_buf[rows] = direct.reshape(size, LANES)

    lead = range(0, STEP, 2)

    def column_block(block, carry):
        cosine = block_ref[block, ray_row : ray_row + ROWS]
        slope = (-LOG2E) / cosine
        for part in range(PARTS):
            gain_buf[part, 0] = cosine * float((edges[part + 1] - edges[part]) // ROWS)
        for first in range(0, levels, STEP):
            coming = [layer for layer in range(first + STEP, first + 2 * STEP, 2) if layer < levels]
            for part in range(PARTS):
                for layer in coming[part * len(coming) // PARTS : (part + 1) * len(coming) // PARTS]:
                    optical(block, layer)
                advance(first, part, cosine, slope)

        following = jnp.minimum(block + 1, blocks - 1)
        for layer in lead:
            optical(following, layer)

        albedo = block_ref[block, ray_row + ROWS : ray_row + 2 * ROWS]
        shape = (points // ROWS, ROWS, LANES)
        refl = refl_buf[...].reshape(shape)
        arriving = (fall_buf[...] + direct_buf[...]).reshape(shape)
        rising = albedo * arriving * pl.reciprocal(1.0 - albedo * refl, approx=True)

        def total(level):
            summed = gain_buf[0, level]
            for part in range(1, PARTS):
                summed = summed + gain_buf[part, level]
            return summed

        net_buf[levels] = total(levels) - jnp.sum(rising * (1.0 - refl), axis=0)
        for layer in range(levels - 1, -1, -1):
            rising = up_buf[layer].reshape(shape) * rising + rise_buf[layer].reshape(shape)
            taken = rising if layer == 0 else rising * pass_buf[layer].reshape(shape)
            net_buf[layer] = total(layer) - jnp.sum(taken, axis=0)
        warm_ref[block] = jnp.sum(net_buf[:levels] - net_buf[1:], axis=1)
        return carry

    for layer in lead:
        optical(0, layer)
    lax.fori_loop(0, blocks, column_block, 0)

    for block in range(blocks):
        cols = slice(block * LANES, (block + 1) * LANES)
        heat_ref[:levels, cols] = warm_ref[block] / mass_ref[:, cols].astype(jnp.float32)


def shade_kernel(heat_hbm, flags_ref, out_ref, heat_ref, copied):
    copy = pltpu.make_async_copy(heat_hbm, heat_ref, copied)
    copy.start()
    copy.wait()
    levels = out_ref.shape[0]
    owner = heat_ref[levels:]
    lit = jnp.zeros_like(owner)
    for group in range(flags_ref.shape[0]):
        flag = jnp.broadcast_to(flags_ref[group].astype(jnp.float32), owner.shape)
        lit = jnp.where(owner == float(group), flag, lit)
    out_ref[...] = heat_ref[:levels] * lit[:1]


def local(
    gases,
    pressure_bin,
    layer_mass,
    cos_zenith,
    surface_albedo,
    column_order,
    sunlit,
    absorption,
    scattering,
):
    group_size = lax.axis_size("span")
    gas_count, levels, columns = gases.shape
    points, _, bins = absorption.shape
    block_count = sunlit.shape[0]
    wanted = jnp.broadcast_to(sunlit[:, None], (block_count, group_size // block_count)).reshape(group_size, 1, 1)
    flags = lax.all_to_all(wanted, "span", split_axis=0, concat_axis=0, tiled=True)
    field = pltpu.VMEM((levels, points, LANES), jnp.float32)
    state = pltpu.VMEM((points, LANES), jnp.float32)
    rows = gas_count * levels + levels + PACK
    blocks = columns // LANES
    heat = pl.pallas_call(
        functools.partial(heating_kernel, columns // group_size),
        out_shape=jax.ShapeDtypeStruct((levels + ROWS, columns), jnp.float32),
        in_specs=[pl.BlockSpec(memory_space=pltpu.HBM)] * 8,
        out_specs=pl.BlockSpec(memory_space=pltpu.VMEM),
        scratch_shapes=[
            pltpu.VMEM(gases.shape, gases.dtype),
            pltpu.VMEM(pressure_bin.shape, pressure_bin.dtype),
            pltpu.VMEM(layer_mass.shape, layer_mass.dtype),
            pltpu.VMEM(cos_zenith.shape, cos_zenith.dtype),
            pltpu.VMEM(surface_albedo.shape, surface_albedo.dtype),
            pltpu.VMEM((1, columns), column_order.dtype),
            pltpu.VMEM((gas_count, bins, points), absorption.dtype),
            pltpu.VMEM((bins, points), scattering.dtype),
            pltpu.SemaphoreType.DMA((8,)),
            pltpu.VMEM((-(-(gas_count + 1) * BIN_ROWS // LANES) * LANES, LANES), jnp.float32),
            pltpu.VMEM((points, gas_count * BIN_ROWS), jnp.bfloat16),
            pltpu.VMEM((points, BIN_ROWS), jnp.bfloat16),
            pltpu.VMEM((blocks, rows, LANES), jnp.float32),
            pltpu.VMEM((levels, 2 * points, LANES), jnp.float32),
            field,
            field,
            field,
            state,
            state,
            state,
            pltpu.VMEM((PARTS, levels + 1, ROWS, LANES), jnp.float32),
            pltpu.VMEM((levels + 1, ROWS, LANES), jnp.float32),
            pltpu.VMEM((blocks, levels, LANES), jnp.float32),
        ],
        compiler_params=pltpu.CompilerParams(vmem_limit_bytes=VMEM_BYTES),
        cost_estimate=pl.CostEstimate(
            flops=40 * levels * points * columns, bytes_accessed=1 << 20, transcendentals=3 * levels * points * columns
        ),
    )(
        gases,
        pressure_bin,
        layer_mass,
        cos_zenith,
        surface_albedo,
        column_order.reshape(1, columns),
        jnp.transpose(absorption, (1, 2, 0)),
        jnp.transpose(scattering),
    )
    return pl.pallas_call(
        shade_kernel,
        out_shape=jax.ShapeDtypeStruct((levels, columns), heat.dtype),
        in_specs=[pl.BlockSpec(memory_space=pltpu.HBM), pl.BlockSpec(memory_space=pltpu.VMEM)],
        out_specs=pl.BlockSpec(memory_space=pltpu.VMEM),
        scratch_shapes=[
            pltpu.VMEM(heat.shape, heat.dtype),
            pltpu.SemaphoreType.DMA(()),
        ],
        compiler_params=pltpu.CompilerParams(vmem_limit_bytes=SHADE_BYTES),
    )(heat, flags)


def solution(mesh):
    placed = (
        P(None, None, ("band", "span")),
        P(None, ("band", "span")),
        P(None, ("band", "span")),
        P(("band", "span")),
        P(("band", "span")),
        P(("band", "span")),
        P(("band", "span")),
        P(),
        P(),
    )
    return jax.shard_map(
        local, mesh=mesh, in_specs=placed, out_specs=P(None, ("band", "span")), check_vma=False
    )
```

```python
import functools
import math

import jax
import jax.numpy as jnp
from jax import lax
from jax.experimental import pallas as pl
from jax.experimental.pallas import tpu as pltpu
from jax.sharding import PartitionSpec as P

LANES = 128
ROWS = 8
TILE = 256
PACK = 16
PAIR = 2
HALVES = 2
BIN_ROWS = 64
LOG2E = math.log2(math.e)
VMEM_BYTES = 63 * 1024 * 1024
SHADE_BYTES = 55200 * 1024


def one_hot(hit):
    return jnp.where(hit, 1.0, 0.0).astype(jnp.bfloat16)


def heating_kernel(
    per_peer,
    gases_hbm,
    bins_hbm,
    mass_hbm,
    cosine_hbm,
    ground_hbm,
    order_hbm,
    absorb_hbm,
    scatter_hbm,
    heat_ref,
    gases_ref,
    bins_ref,
    mass_ref,
    cosine_ref,
    ground_ref,
    order_ref,
    absorb_ref,
    albedo_ref,
    copied,
    wide_buf,
    table_ref,
    scatter_ref,
    block_ref,
    tau_ref,
    omega_ref,
    up_buf,
    rise_buf,
    pass_buf,
    refl_buf,
    fall_buf,
    gain_buf,
    net_buf,
    warm_ref,
):
    gas_count, levels, columns = gases_ref.shape
    points = table_ref.shape[0]
    bin_count = absorb_ref.shape[1]
    half = points // HALVES
    vregs = half // ROWS
    blocks = columns // LANES
    bin_row = gas_count * levels
    ray_row = bin_row + levels
    first_row = gas_count * BIN_ROWS

    copies = [
        pltpu.make_async_copy(source, target, copied.at[place])
        for place, (source, target) in enumerate(
            (
                (absorb_hbm, absorb_ref),
                (scatter_hbm, albedo_ref),
                (order_hbm, order_ref),
                (cosine_hbm, cosine_ref),
                (ground_hbm, ground_ref),
                (bins_hbm, bins_ref),
                (gases_hbm, gases_ref),
                (mass_hbm, mass_ref),
            )
        )
    ]
    for copy in copies:
        copy.start()

    wide_buf[...] = jnp.zeros_like(wide_buf)
    for copy in copies[:3]:
        copy.wait()

    square = (columns, columns)
    order = jnp.broadcast_to(order_ref[...], square)
    match = one_hot(order == lax.broadcasted_iota(jnp.int32, square, 0))
    place = lax.broadcasted_iota(jnp.int32, (ROWS, columns), 1)
    group = (place // per_peer).astype(jnp.float32).astype(jnp.bfloat16)
    heat_ref[levels:] = lax.dot_general(group, match, (((1,), (1,)), ((), ())), preferred_element_type=jnp.float32)

    for gas in range(gas_count):
        wide_buf[gas * BIN_ROWS : gas * BIN_ROWS + bin_count, :points] = absorb_ref[gas].astype(jnp.float32)
    wide_buf[first_row : first_row + bin_count, :points] = 0.5 * albedo_ref[...].astype(jnp.float32)
    turned = [
        jnp.transpose(wide_buf[i * LANES : (i + 1) * LANES])[:points].astype(jnp.bfloat16)
        for i in range(wide_buf.shape[0] // LANES)
    ]
    whole = jnp.concatenate(turned, axis=1)
    table_ref[...] = whole[:, :first_row]
    scatter_ref[...] = whole[:, first_row : first_row + BIN_ROWS]
    for copy in copies[3:]:
        copy.wait()

    for block in range(blocks):
        cols = slice(block * LANES, (block + 1) * LANES)
        for gas in range(gas_count):
            block_ref[block, gas * levels : (gas + 1) * levels] = gases_ref[gas, :, cols].astype(jnp.float32)
        block_ref[block, bin_row:ray_row] = bins_ref[:, cols].astype(jnp.float32)
    wide = (1, columns)
    cosines = cosine_ref[...].astype(jnp.float32).reshape(wide)
    grounds = ground_ref[...].astype(jnp.float32).reshape(wide)
    for block in range(blocks):
        cols = slice(block * LANES, (block + 1) * LANES)
        block_ref[block, ray_row : ray_row + ROWS] = jnp.broadcast_to(cosines[:, cols], (ROWS, LANES))
        block_ref[block, ray_row + ROWS : ray_row + 2 * ROWS] = jnp.broadcast_to(grounds[:, cols], (ROWS, LANES))

    def optical(slot, layer):
        parts = []
        shape = (BIN_ROWS, LANES)
        rows = lax.broadcasted_iota(jnp.int32, shape, 0).astype(jnp.float32).astype(jnp.bfloat16)
        one = jnp.ones(shape, jnp.bfloat16)
        zero = jnp.zeros(shape, jnp.bfloat16)
        selectors = []
        for near in (layer, layer + 1):
            place = bin_row + near
            bins = jnp.broadcast_to(block_ref[slot, place : place + 1, :], (PACK, LANES)).astype(jnp.bfloat16)
            bins = jnp.concatenate([bins] * (BIN_ROWS // PACK), axis=0)
            selectors.append(jnp.where(bins == rows, one, zero))
        for gas in range(gas_count):
            pair = []
            for near, selector in zip((layer, layer + 1), selectors):
                place = gas * levels + near
                amount = jnp.broadcast_to(block_ref[slot, place : place + 1, :], (PACK, LANES)).astype(jnp.bfloat16)
                pair.append(jnp.concatenate([amount] * (BIN_ROWS // PACK), axis=0) * selector)
            parts.append(jnp.concatenate(pair, axis=1))
        weighted = jnp.concatenate(parts, axis=0)
        selected = jnp.concatenate(selectors, axis=1)
        tau = jnp.dot(table_ref[...], weighted, preferred_element_type=jnp.float32)
        albedo = jnp.dot(scatter_ref[...], selected, preferred_element_type=jnp.float32)
        return tau, albedo

    def advance(first, part, state, optics, cosine, slope):
        rows = slice(part * half, (part + 1) * half)
        shape = (vregs, ROWS, LANES)
        if state is None:
            direct = jnp.broadcast_to(cosine[None], shape)
        else:
            refl, fall, direct = state
        for layer in range(first, first + PAIR):
            cols = slice((layer - first) * LANES, (layer - first + 1) * LANES)
            tau = optics[0][rows, cols].reshape(shape)
            half_albedo = optics[1][rows, cols].reshape(shape)
            fading = jnp.exp2(tau * (-1.66 * LOG2E))
            passed = jnp.exp2(tau * slope)
            reflect = half_albedo * (1.0 - fading)
            transmit = fading + reflect
            below = direct * passed
            source = half_albedo * (direct - below)
            if layer == 0:
                up_buf[layer, rows] = transmit.reshape(half, LANES)
                rise_buf[layer, rows] = source.reshape(half, LANES)
                fall = source
                refl = reflect
            else:
                pass_buf[layer, rows] = (1.0 - refl).reshape(half, LANES)
                inverse = pl.reciprocal(1.0 - reflect * refl, approx=True)
                up = transmit * inverse
                rise = (reflect * fall + source) * inverse
                up_buf[layer, rows] = up.reshape(half, LANES)
                rise_buf[layer, rows] = rise.reshape(half, LANES)
                fall = source + transmit * (fall + refl * rise)
                refl = reflect + transmit * (refl * up)
            direct = below
            gain_buf[part, layer + 1] = jnp.sum(direct + fall, axis=0)
        return refl, fall, direct

    def column_block(block, carry):
        cosine = block_ref[block, ray_row : ray_row + ROWS]
        slope = (-LOG2E) / cosine
        for part in range(HALVES):
            gain_buf[part, 0] = cosine * float(vregs)
        optics = (tau_ref[...], omega_ref[...])
        states = [None] * HALVES
        for first in range(0, levels, PAIR):
            coming = optical(block, first + PAIR) if first + PAIR < levels else None
            for part in range(HALVES):
                states[part] = advance(first, part, states[part], optics, cosine, slope)
            optics = coming
        for part in range(HALVES):
            rows = slice(part * half, (part + 1) * half)
            refl, fall, direct = states[part]
            refl_buf[rows] = refl.reshape(half, LANES)
            fall_buf[rows] = (fall + direct).reshape(half, LANES)

        following = jnp.minimum(block + 1, blocks - 1)
        tau_ref[...], omega_ref[...] = optical(following, 0)

        albedo = block_ref[block, ray_row + ROWS : ray_row + 2 * ROWS]
        shape = (points // ROWS, ROWS, LANES)
        refl = refl_buf[...].reshape(shape)
        arriving = fall_buf[...].reshape(shape)
        rising = albedo * arriving * pl.reciprocal(1.0 - albedo * refl, approx=True)

        def total(level):
            summed = gain_buf[0, level]
            for part in range(1, HALVES):
                summed = summed + gain_buf[part, level]
            return summed

        net_buf[levels] = total(levels) - jnp.sum(rising * (1.0 - refl), axis=0)
        for layer in range(levels - 1, -1, -1):
            rising = up_buf[layer].reshape(shape) * rising + rise_buf[layer].reshape(shape)
            taken = rising if layer == 0 else rising * pass_buf[layer].reshape(shape)
            net_buf[layer] = total(layer) - jnp.sum(taken, axis=0)
        warm_ref[block] = jnp.sum(net_buf[:levels] - net_buf[1:], axis=1)
        return carry

    tau_ref[...], omega_ref[...] = optical(0, 0)
    lax.fori_loop(0, blocks, column_block, 0)

    for block in range(blocks):
        cols = slice(block * LANES, (block + 1) * LANES)
        heat_ref[:levels, cols] = warm_ref[block] / mass_ref[:, cols].astype(jnp.float32)


def shade_kernel(heat_hbm, flags_ref, out_ref, heat_ref, copied):
    copy = pltpu.make_async_copy(heat_hbm, heat_ref, copied)
    copy.start()
    copy.wait()
    levels = out_ref.shape[0]
    owner = heat_ref[levels:]
    lit = jnp.zeros_like(owner)
    for group in range(flags_ref.shape[0]):
        flag = jnp.broadcast_to(flags_ref[group].astype(jnp.float32), owner.shape)
        lit = jnp.where(owner == float(group), flag, lit)
    out_ref[...] = heat_ref[:levels] * lit[:1]


def local(
    gases,
    pressure_bin,
    layer_mass,
    cos_zenith,
    surface_albedo,
    column_order,
    sunlit,
    absorption,
    scattering,
):
    group_size = lax.axis_size("span")
    gas_count, levels, columns = gases.shape
    points, _, bins = absorption.shape
    block_count = sunlit.shape[0]
    wanted = jnp.broadcast_to(sunlit[:, None], (block_count, group_size // block_count)).reshape(group_size, 1, 1)
    flags = lax.all_to_all(wanted, "span", split_axis=0, concat_axis=0, tiled=True)
    field = pltpu.VMEM((levels, points, LANES), jnp.float32)
    state = pltpu.VMEM((points, LANES), jnp.float32)
    rows = gas_count * levels + levels + PACK
    blocks = columns // LANES
    heat = pl.pallas_call(
        functools.partial(heating_kernel, columns // group_size),
        out_shape=jax.ShapeDtypeStruct((levels + ROWS, columns), jnp.float32),
        in_specs=[pl.BlockSpec(memory_space=pltpu.HBM)] * 8,
        out_specs=pl.BlockSpec(memory_space=pltpu.VMEM),
        scratch_shapes=[
            pltpu.VMEM(gases.shape, gases.dtype),
            pltpu.VMEM(pressure_bin.shape, pressure_bin.dtype),
            pltpu.VMEM(layer_mass.shape, layer_mass.dtype),
            pltpu.VMEM(cos_zenith.shape, cos_zenith.dtype),
            pltpu.VMEM(surface_albedo.shape, surface_albedo.dtype),
            pltpu.VMEM((1, columns), column_order.dtype),
            pltpu.VMEM((gas_count, bins, points), absorption.dtype),
            pltpu.VMEM((bins, points), scattering.dtype),
            pltpu.SemaphoreType.DMA((8,)),
            pltpu.VMEM((-(-(gas_count + 1) * BIN_ROWS // LANES) * LANES, LANES), jnp.float32),
            pltpu.VMEM((points, gas_count * BIN_ROWS), jnp.bfloat16),
            pltpu.VMEM((points, BIN_ROWS), jnp.bfloat16),
            pltpu.VMEM((blocks, rows, LANES), jnp.float32),
            pltpu.VMEM((points, TILE), jnp.float32),
            pltpu.VMEM((points, TILE), jnp.float32),
            field,
            field,
            field,
            state,
            state,
            pltpu.VMEM((HALVES, levels + 1, ROWS, LANES), jnp.float32),
            pltpu.VMEM((levels + 1, ROWS, LANES), jnp.float32),
            pltpu.VMEM((blocks, levels, LANES), jnp.float32),
        ],
        compiler_params=pltpu.CompilerParams(vmem_limit_bytes=VMEM_BYTES),
        cost_estimate=pl.CostEstimate(
            flops=40 * levels * points * columns, bytes_accessed=1 << 20, transcendentals=3 * levels * points * columns
        ),
    )(
        gases,
        pressure_bin,
        layer_mass,
        cos_zenith,
        surface_albedo,
        column_order.reshape(1, columns),
        jnp.transpose(absorption, (1, 2, 0)),
        jnp.transpose(scattering),
    )
    return pl.pallas_call(
        shade_kernel,
        out_shape=jax.ShapeDtypeStruct((levels, columns), heat.dtype),
        in_specs=[pl.BlockSpec(memory_space=pltpu.HBM), pl.BlockSpec(memory_space=pltpu.VMEM)],
        out_specs=pl.BlockSpec(memory_space=pltpu.VMEM),
        scratch_shapes=[
            pltpu.VMEM(heat.shape, heat.dtype),
            pltpu.SemaphoreType.DMA(()),
        ],
        compiler_params=pltpu.CompilerParams(vmem_limit_bytes=SHADE_BYTES),
    )(heat, flags)


def solution(mesh):
    placed = (
        P(None, None, ("band", "span")),
        P(None, ("band", "span")),
        P(None, ("band", "span")),
        P(("band", "span")),
        P(("band", "span")),
        P(("band", "span")),
        P(("band", "span")),
        P(),
        P(),
    )
    return jax.shard_map(
        local, mesh=mesh, in_specs=placed, out_specs=P(None, ("band", "span")), check_vma=False
    )
```

```python
import functools
import math

import jax
import jax.numpy as jnp
from jax import lax
from jax.experimental import pallas as pl
from jax.experimental.pallas import tpu as pltpu
from jax.sharding import PartitionSpec as P

LANES = 128
ROWS = 8
PACK = 16
STEP = 8
HALVES = 2
BIN_ROWS = 64
LOG2E = math.log2(math.e)
VMEM_BYTES = 24 * 1024 * 1024


def one_hot(hit):
    return jnp.where(hit, 1.0, 0.0).astype(jnp.bfloat16)


def heating_kernel(
    per_peer,
    gases_hbm,
    bins_hbm,
    mass_hbm,
    cosine_hbm,
    ground_hbm,
    order_hbm,
    absorb_hbm,
    scatter_hbm,
    heat_ref,
    gases_ref,
    bins_ref,
    mass_ref,
    cosine_ref,
    ground_ref,
    order_ref,
    absorb_ref,
    albedo_ref,
    copied,
    wide_buf,
    table_ref,
    scatter_ref,
    block_ref,
    optic_ref,
    up_buf,
    rise_buf,
    pass_buf,
    refl_buf,
    fall_buf,
    direct_buf,
    gain_buf,
    net_buf,
    warm_ref,
):
    gas_count, levels, columns = gases_ref.shape
    points = table_ref.shape[0]
    bin_count = absorb_ref.shape[1]
    half = points // HALVES
    vregs = half // ROWS
    blocks = columns // LANES
    bin_row = gas_count * levels
    ray_row = bin_row + levels
    first_row = gas_count * BIN_ROWS

    copies = [
        pltpu.make_async_copy(source, target, copied.at[place])
        for place, (source, target) in enumerate(
            (
                (absorb_hbm, absorb_ref),
                (scatter_hbm, albedo_ref),
                (order_hbm, order_ref),
                (cosine_hbm, cosine_ref),
                (ground_hbm, ground_ref),
                (bins_hbm, bins_ref),
                (gases_hbm, gases_ref),
                (mass_hbm, mass_ref),
            )
        )
    ]
    for copy in copies:
        copy.start()

    wide_buf[...] = jnp.zeros_like(wide_buf)
    for copy in copies[:3]:
        copy.wait()

    square = (columns, columns)
    order = jnp.broadcast_to(order_ref[...], square)
    match = one_hot(order == lax.broadcasted_iota(jnp.int32, square, 0))
    place = lax.broadcasted_iota(jnp.int32, (ROWS, columns), 1)
    group = (place // per_peer).astype(jnp.float32).astype(jnp.bfloat16)
    heat_ref[levels:] = lax.dot_general(group, match, (((1,), (1,)), ((), ())), preferred_element_type=jnp.float32)

    for gas in range(gas_count):
        wide_buf[gas * BIN_ROWS : gas * BIN_ROWS + bin_count, :points] = absorb_ref[gas].astype(jnp.float32)
    wide_buf[first_row : first_row + bin_count, :points] = 0.5 * albedo_ref[...].astype(jnp.float32)
    turned = [
        jnp.transpose(wide_buf[i * LANES : (i + 1) * LANES])[:points].astype(jnp.bfloat16)
        for i in range(wide_buf.shape[0] // LANES)
    ]
    whole = jnp.concatenate(turned, axis=1)
    table_ref[...] = whole[:, :first_row]
    scatter_ref[...] = whole[:, first_row : first_row + BIN_ROWS]
    for copy in copies[3:]:
        copy.wait()

    for block in range(blocks):
        cols = slice(block * LANES, (block + 1) * LANES)
        for gas in range(gas_count):
            block_ref[block, gas * levels : (gas + 1) * levels] = gases_ref[gas, :, cols].astype(jnp.float32)
        block_ref[block, bin_row:ray_row] = bins_ref[:, cols].astype(jnp.float32)
    wide = (1, columns)
    cosines = cosine_ref[...].astype(jnp.float32).reshape(wide)
    grounds = ground_ref[...].astype(jnp.float32).reshape(wide)
    for block in range(blocks):
        cols = slice(block * LANES, (block + 1) * LANES)
        block_ref[block, ray_row : ray_row + ROWS] = jnp.broadcast_to(cosines[:, cols], (ROWS, LANES))
        block_ref[block, ray_row + ROWS : ray_row + 2 * ROWS] = jnp.broadcast_to(grounds[:, cols], (ROWS, LANES))

    def optical(slot, layer):
        parts = []
        shape = (BIN_ROWS, LANES)
        rows = lax.broadcasted_iota(jnp.int32, shape, 0).astype(jnp.float32).astype(jnp.bfloat16)
        one = jnp.ones(shape, jnp.bfloat16)
        zero = jnp.zeros(shape, jnp.bfloat16)
        selectors = []
        for near in (layer, layer + 1):
            place = bin_row + near
            bins = jnp.broadcast_to(block_ref[slot, place : place + 1, :], (PACK, LANES)).astype(jnp.bfloat16)
            bins = jnp.concatenate([bins] * (BIN_ROWS // PACK), axis=0)
            selectors.append(jnp.where(bins == rows, one, zero))
        for gas in range(gas_count):
            pair = []
            for near, selector in zip((layer, layer + 1), selectors):
                place = gas * levels + near
                amount = jnp.broadcast_to(block_ref[slot, place : place + 1, :], (PACK, LANES)).astype(jnp.bfloat16)
                pair.append(jnp.concatenate([amount] * (BIN_ROWS // PACK), axis=0) * selector)
            parts.append(jnp.concatenate(pair, axis=1))
        weighted = jnp.concatenate(parts, axis=0)
        selected = jnp.concatenate(selectors, axis=1)
        tau = jnp.dot(table_ref[...], weighted, preferred_element_type=jnp.float32)
        albedo = jnp.dot(scatter_ref[...], selected, preferred_element_type=jnp.float32)
        for near in range(2):
            cols = slice(near * LANES, (near + 1) * LANES)
            optic_ref[layer + near, :points] = tau[:, cols]
            optic_ref[layer + near, points:] = albedo[:, cols]

    def advance(first, part, cosine, slope):
        rows = slice(part * half, (part + 1) * half)
        half_rows = slice(points + part * half, points + (part + 1) * half)
        shape = (vregs, ROWS, LANES)
        if first > 0:
            refl = refl_buf[rows].reshape(shape)
            fall = fall_buf[rows].reshape(shape)
            direct = direct_buf[rows].reshape(shape)
        else:
            direct = jnp.broadcast_to(cosine[None], shape)
        for layer in range(first, first + STEP):
            tau = optic_ref[layer, rows].reshape(shape)
            half_albedo = optic_ref[layer, half_rows].reshape(shape)
            fading = jnp.exp2(tau * (-1.66 * LOG2E))
            passed = jnp.exp2(tau * slope)
            reflect = half_albedo * (1.0 - fading)
            transmit = fading + reflect
            below = direct * passed
            source = half_albedo * (direct - below)
            if layer == 0:
                up_buf[layer, rows] = transmit.reshape(half, LANES)
                rise_buf[layer, rows] = source.reshape(half, LANES)
                fall = source
                refl = reflect
            else:
                pass_buf[layer, rows] = (1.0 - refl).reshape(half, LANES)
                inverse = pl.reciprocal(1.0 - reflect * refl, approx=True)
                up = transmit * inverse
                rise = (reflect * fall + source) * inverse
                up_buf[layer, rows] = up.reshape(half, LANES)
                rise_buf[layer, rows] = rise.reshape(half, LANES)
                fall = source + transmit * (fall + refl * rise)
                refl = reflect + transmit * (refl * up)
            direct = below
            gain_buf[part, layer + 1] = jnp.sum(direct + fall, axis=0)
        refl_buf[rows] = refl.reshape(half, LANES)
        fall_buf[rows] = fall.reshape(half, LANES)
        direct_buf[rows] = direct.reshape(half, LANES)

    lead = range(0, STEP, 2)

    def column_block(block, carry):
        cosine = block_ref[block, ray_row : ray_row + ROWS]
        slope = (-LOG2E) / cosine
        for part in range(HALVES):
            gain_buf[part, 0] = cosine * float(vregs)
        for first in range(0, levels, STEP):
            coming = [layer for layer in range(first + STEP, first + 2 * STEP, 2) if layer < levels]
            for part in range(HALVES):
                for layer in coming[part * len(coming) // HALVES : (part + 1) * len(coming) // HALVES]:
                    optical(block, layer)
                advance(first, part, cosine, slope)

        following = jnp.minimum(block + 1, blocks - 1)
        for layer in lead:
            optical(following, layer)

        albedo = block_ref[block, ray_row + ROWS : ray_row + 2 * ROWS]
        shape = (points // ROWS, ROWS, LANES)
        refl = refl_buf[...].reshape(shape)
        arriving = (fall_buf[...] + direct_buf[...]).reshape(shape)
        rising = albedo * arriving * pl.reciprocal(1.0 - albedo * refl, approx=True)

        def total(level):
            summed = gain_buf[0, level]
            for part in range(1, HALVES):
                summed = summed + gain_buf[part, level]
            return summed

        net_buf[levels] = total(levels) - jnp.sum(rising * (1.0 - refl), axis=0)
        for layer in range(levels - 1, -1, -1):
            rising = up_buf[layer].reshape(shape) * rising + rise_buf[layer].reshape(shape)
            taken = rising if layer == 0 else rising * pass_buf[layer].reshape(shape)
            net_buf[layer] = total(layer) - jnp.sum(taken, axis=0)
        warm_ref[block] = jnp.sum(net_buf[:levels] - net_buf[1:], axis=1)
        return carry

    for layer in lead:
        optical(0, layer)
    lax.fori_loop(0, blocks, column_block, 0)

    for block in range(blocks):
        cols = slice(block * LANES, (block + 1) * LANES)
        heat_ref[:levels, cols] = warm_ref[block] / mass_ref[:, cols].astype(jnp.float32)


def shade_kernel(heat_ref, flags_ref, out_ref):
    levels = out_ref.shape[0]
    owner = heat_ref[levels:]
    lit = jnp.zeros_like(owner)
    for group in range(flags_ref.shape[0]):
        flag = jnp.broadcast_to(flags_ref[group].astype(jnp.float32), owner.shape)
        lit = jnp.where(owner == float(group), flag, lit)
    out_ref[...] = heat_ref[:levels] * lit[:1]


def local(
    gases,
    pressure_bin,
    layer_mass,
    cos_zenith,
    surface_albedo,
    column_order,
    sunlit,
    absorption,
    scattering,
):
    group_size = lax.axis_size("span")
    gas_count, levels, columns = gases.shape
    points, _, bins = absorption.shape
    block_count = sunlit.shape[0]
    wanted = jnp.broadcast_to(sunlit[:, None], (block_count, group_size // block_count)).reshape(group_size, 1, 1)
    flags = lax.all_to_all(wanted, "span", split_axis=0, concat_axis=0, tiled=True)
    field = pltpu.VMEM((levels, points, LANES), jnp.float32)
    state = pltpu.VMEM((points, LANES), jnp.float32)
    rows = gas_count * levels + levels + PACK
    blocks = columns // LANES
    heat = pl.pallas_call(
        functools.partial(heating_kernel, columns // group_size),
        out_shape=jax.ShapeDtypeStruct((levels + ROWS, columns), jnp.float32),
        in_specs=[pl.BlockSpec(memory_space=pltpu.HBM)] * 8,
        out_specs=pl.BlockSpec(memory_space=pltpu.VMEM),
        scratch_shapes=[
            pltpu.VMEM(gases.shape, gases.dtype),
            pltpu.VMEM(pressure_bin.shape, pressure_bin.dtype),
            pltpu.VMEM(layer_mass.shape, layer_mass.dtype),
            pltpu.VMEM(cos_zenith.shape, cos_zenith.dtype),
            pltpu.VMEM(surface_albedo.shape, surface_albedo.dtype),
            pltpu.VMEM((1, columns), column_order.dtype),
            pltpu.VMEM((gas_count, bins, points), absorption.dtype),
            pltpu.VMEM((bins, points), scattering.dtype),
            pltpu.SemaphoreType.DMA((8,)),
            pltpu.VMEM((-(-(gas_count + 1) * BIN_ROWS // LANES) * LANES, LANES), jnp.float32),
            pltpu.VMEM((points, gas_count * BIN_ROWS), jnp.bfloat16),
            pltpu.VMEM((points, BIN_ROWS), jnp.bfloat16),
            pltpu.VMEM((blocks, rows, LANES), jnp.float32),
            pltpu.VMEM((levels, 2 * points, LANES), jnp.float32),
            field,
            field,
            field,
            state,
            state,
            state,
            pltpu.VMEM((HALVES, levels + 1, ROWS, LANES), jnp.float32),
            pltpu.VMEM((levels + 1, ROWS, LANES), jnp.float32),
            pltpu.VMEM((blocks, levels, LANES), jnp.float32),
        ],
        compiler_params=pltpu.CompilerParams(vmem_limit_bytes=VMEM_BYTES),
        cost_estimate=pl.CostEstimate(
            flops=40 * levels * points * columns, bytes_accessed=1 << 20, transcendentals=3 * levels * points * columns
        ),
    )(
        *[
            pltpu.with_memory_space_constraint(operand, pltpu.HBM)
            for operand in (
                gases,
                pressure_bin,
                layer_mass,
                cos_zenith,
                surface_albedo,
                column_order.reshape(1, columns),
                jnp.transpose(absorption, (1, 2, 0)),
                jnp.transpose(scattering),
            )
        ]
    )
    return pl.pallas_call(
        shade_kernel,
        out_shape=jax.ShapeDtypeStruct((levels, columns), heat.dtype),
        in_specs=[pl.BlockSpec(memory_space=pltpu.VMEM)] * 2,
        out_specs=pl.BlockSpec(memory_space=pltpu.VMEM),
        compiler_params=pltpu.CompilerParams(vmem_limit_bytes=VMEM_BYTES),
    )(heat, flags)


def solution(mesh):
    placed = (
        P(None, None, ("band", "span")),
        P(None, ("band", "span")),
        P(None, ("band", "span")),
        P(("band", "span")),
        P(("band", "span")),
        P(("band", "span")),
        P(("band", "span")),
        P(),
        P(),
    )
    return jax.shard_map(
        local, mesh=mesh, in_specs=placed, out_specs=P(None, ("band", "span")), check_vma=False
    )
```

```python
import functools
import math

import jax
import jax.numpy as jnp
from jax import lax
from jax.experimental import pallas as pl
from jax.experimental.pallas import tpu as pltpu
from jax.sharding import PartitionSpec as P

LANES = 128
ROWS = 8
PACK = 16
STEP = 8
HALVES = 2
BIN_ROWS = 64
LOG2E = math.log2(math.e)
VMEM_BYTES = 24 * 1024 * 1024


def one_hot(hit):
    return jnp.where(hit, 1.0, 0.0).astype(jnp.bfloat16)


def prepare_kernel(
    per_peer,
    sunlit_hbm,
    gases_hbm,
    bins_hbm,
    cosine_hbm,
    ground_hbm,
    order_hbm,
    absorb_hbm,
    scatter_hbm,
    wanted_hbm,
    table_ref,
    scatter_ref,
    block_ref,
    owner_ref,
    sunlit_ref,
    gases_ref,
    bins_ref,
    cosine_ref,
    ground_ref,
    order_ref,
    absorb_ref,
    albedo_ref,
    wanted_ref,
    copied,
    wide_buf,
):
    gas_count, levels, columns = gases_ref.shape
    points = table_ref.shape[0]
    bin_count = absorb_ref.shape[1]
    blocks = columns // LANES
    bin_row = gas_count * levels
    ray_row = bin_row + levels
    first_row = gas_count * BIN_ROWS
    peers = wanted_ref.shape[0]

    copies = [
        pltpu.make_async_copy(source, target, copied.at[place])
        for place, (source, target) in enumerate(
            (
                (sunlit_hbm, sunlit_ref),
                (order_hbm, order_ref),
                (absorb_hbm, absorb_ref),
                (scatter_hbm, albedo_ref),
                (cosine_hbm, cosine_ref),
                (ground_hbm, ground_ref),
                (bins_hbm, bins_ref),
                (gases_hbm, gases_ref),
            )
        )
    ]
    for copy in copies:
        copy.start()
    wide_buf[...] = jnp.zeros_like(wide_buf)
    copies[0].wait()
    for peer in range(peers):
        wanted_ref[peer] = jnp.full((1, 1), sunlit_ref[peer * sunlit_ref.shape[0] // peers], jnp.int32)
    sending = pltpu.make_async_copy(wanted_ref, wanted_hbm, copied.at[len(copies)])
    sending.start()
    for copy in copies[1:4]:
        copy.wait()

    square = (columns, columns)
    order = jnp.broadcast_to(order_ref[...], square)
    match = one_hot(order == lax.broadcasted_iota(jnp.int32, square, 0))
    place = lax.broadcasted_iota(jnp.int32, (ROWS, columns), 1)
    group = (place // per_peer).astype(jnp.float32).astype(jnp.bfloat16)
    owner_ref[...] = lax.dot_general(group, match, (((1,), (1,)), ((), ())), preferred_element_type=jnp.float32)

    for gas in range(gas_count):
        wide_buf[gas * BIN_ROWS : gas * BIN_ROWS + bin_count, :points] = absorb_ref[gas].astype(jnp.float32)
    wide_buf[first_row : first_row + bin_count, :points] = 0.5 * albedo_ref[...].astype(jnp.float32)
    turned = [
        jnp.transpose(wide_buf[i * LANES : (i + 1) * LANES])[:points].astype(jnp.bfloat16)
        for i in range(wide_buf.shape[0] // LANES)
    ]
    whole = jnp.concatenate(turned, axis=1)
    table_ref[...] = whole[:, :first_row]
    scatter_ref[...] = whole[:, first_row : first_row + BIN_ROWS]
    for copy in copies[4:]:
        copy.wait()

    for block in range(blocks):
        cols = slice(block * LANES, (block + 1) * LANES)
        for gas in range(gas_count):
            block_ref[block, gas * levels : (gas + 1) * levels] = gases_ref[gas, :, cols].astype(jnp.float32)
        block_ref[block, bin_row:ray_row] = bins_ref[:, cols].astype(jnp.float32)
    wide = (1, columns)
    cosines = cosine_ref[...].astype(jnp.float32).reshape(wide)
    grounds = ground_ref[...].astype(jnp.float32).reshape(wide)
    for block in range(blocks):
        cols = slice(block * LANES, (block + 1) * LANES)
        block_ref[block, ray_row : ray_row + ROWS] = jnp.broadcast_to(cosines[:, cols], (ROWS, LANES))
        block_ref[block, ray_row + ROWS : ray_row + 2 * ROWS] = jnp.broadcast_to(grounds[:, cols], (ROWS, LANES))
    sending.wait()


def heating_kernel(
    mass_hbm,
    table_ref,
    scatter_ref,
    block_ref,
    heat_ref,
    mass_ref,
    copied,
    optic_ref,
    up_buf,
    rise_buf,
    pass_buf,
    refl_buf,
    fall_buf,
    direct_buf,
    gain_buf,
    net_buf,
    warm_ref,
):
    levels, columns = heat_ref.shape
    points, gas_rows = table_ref.shape
    gas_count = gas_rows // BIN_ROWS
    half = points // HALVES
    vregs = half // ROWS
    blocks = columns // LANES
    bin_row = gas_count * levels
    ray_row = bin_row + levels
    mass_copy = pltpu.make_async_copy(mass_hbm, mass_ref, copied)
    mass_copy.start()

    def optical(slot, layer):
        parts = []
        shape = (BIN_ROWS, LANES)
        rows = lax.broadcasted_iota(jnp.int32, shape, 0).astype(jnp.float32).astype(jnp.bfloat16)
        one = jnp.ones(shape, jnp.bfloat16)
        zero = jnp.zeros(shape, jnp.bfloat16)
        selectors = []
        for near in (layer, layer + 1):
            place = bin_row + near
            bins = jnp.broadcast_to(block_ref[slot, place : place + 1, :], (PACK, LANES)).astype(jnp.bfloat16)
            bins = jnp.concatenate([bins] * (BIN_ROWS // PACK), axis=0)
            selectors.append(jnp.where(bins == rows, one, zero))
        for gas in range(gas_count):
            pair = []
            for near, selector in zip((layer, layer + 1), selectors):
                place = gas * levels + near
                amount = jnp.broadcast_to(block_ref[slot, place : place + 1, :], (PACK, LANES)).astype(jnp.bfloat16)
                pair.append(jnp.concatenate([amount] * (BIN_ROWS // PACK), axis=0) * selector)
            parts.append(jnp.concatenate(pair, axis=1))
        weighted = jnp.concatenate(parts, axis=0)
        selected = jnp.concatenate(selectors, axis=1)
        tau = jnp.dot(table_ref[...], weighted, preferred_element_type=jnp.float32)
        albedo = jnp.dot(scatter_ref[...], selected, preferred_element_type=jnp.float32)
        for near in range(2):
            cols = slice(near * LANES, (near + 1) * LANES)
            optic_ref[layer + near, :points] = tau[:, cols]
            optic_ref[layer + near, points:] = albedo[:, cols]

    def advance(first, part, cosine, slope):
        rows = slice(part * half, (part + 1) * half)
        half_rows = slice(points + part * half, points + (part + 1) * half)
        shape = (vregs, ROWS, LANES)
        if first > 0:
            refl = refl_buf[rows].reshape(shape)
            fall = fall_buf[rows].reshape(shape)
            direct = direct_buf[rows].reshape(shape)
        else:
            direct = jnp.broadcast_to(cosine[None], shape)
        for layer in range(first, first + STEP):
            tau = optic_ref[layer, rows].reshape(shape)
            half_albedo = optic_ref[layer, half_rows].reshape(shape)
            fading = jnp.exp2(tau * (-1.66 * LOG2E))
            passed = jnp.exp2(tau * slope)
            reflect = half_albedo * (1.0 - fading)
            transmit = fading + reflect
            below = direct * passed
            source = half_albedo * (direct - below)
            if layer == 0:
                up_buf[layer, rows] = transmit.reshape(half, LANES)
                rise_buf[layer, rows] = source.reshape(half, LANES)
                fall = source
                refl = reflect
            else:
                pass_buf[layer, rows] = (1.0 - refl).reshape(half, LANES)
                inverse = pl.reciprocal(1.0 - reflect * refl, approx=True)
                up = transmit * inverse
                rise = (reflect * fall + source) * inverse
                up_buf[layer, rows] = up.reshape(half, LANES)
                rise_buf[layer, rows] = rise.reshape(half, LANES)
                fall = source + transmit * (fall + refl * rise)
                refl = reflect + transmit * (refl * up)
            direct = below
            gain_buf[part, layer + 1] = jnp.sum(direct + fall, axis=0)
        refl_buf[rows] = refl.reshape(half, LANES)
        fall_buf[rows] = fall.reshape(half, LANES)
        direct_buf[rows] = direct.reshape(half, LANES)

    lead = range(0, STEP, 2)

    def column_block(block, carry):
        cosine = block_ref[block, ray_row : ray_row + ROWS]
        slope = (-LOG2E) / cosine
        for part in range(HALVES):
            gain_buf[part, 0] = cosine * float(vregs)
        for first in range(0, levels, STEP):
            coming = [layer for layer in range(first + STEP, first + 2 * STEP, 2) if layer < levels]
            for part in range(HALVES):
                for layer in coming[part * len(coming) // HALVES : (part + 1) * len(coming) // HALVES]:
                    optical(block, layer)
                advance(first, part, cosine, slope)

        following = jnp.minimum(block + 1, blocks - 1)
        for layer in lead:
            optical(following, layer)

        albedo = block_ref[block, ray_row + ROWS : ray_row + 2 * ROWS]
        shape = (points // ROWS, ROWS, LANES)
        refl = refl_buf[...].reshape(shape)
        arriving = (fall_buf[...] + direct_buf[...]).reshape(shape)
        rising = albedo * arriving * pl.reciprocal(1.0 - albedo * refl, approx=True)

        def total(level):
            summed = gain_buf[0, level]
            for part in range(1, HALVES):
                summed = summed + gain_buf[part, level]
            return summed

        net_buf[levels] = total(levels) - jnp.sum(rising * (1.0 - refl), axis=0)
        for layer in range(levels - 1, -1, -1):
            rising = up_buf[layer].reshape(shape) * rising + rise_buf[layer].reshape(shape)
            taken = rising if layer == 0 else rising * pass_buf[layer].reshape(shape)
            net_buf[layer] = total(layer) - jnp.sum(taken, axis=0)
        warm_ref[block] = jnp.sum(net_buf[:levels] - net_buf[1:], axis=1)
        return carry

    for layer in lead:
        optical(0, layer)
    lax.fori_loop(0, blocks, column_block, 0)
    mass_copy.wait()

    for block in range(blocks):
        cols = slice(block * LANES, (block + 1) * LANES)
        heat_ref[:, cols] = warm_ref[block] / mass_ref[:, cols].astype(jnp.float32)


def shade_kernel(heat_ref, owner_ref, flags_ref, out_ref):
    owner = owner_ref[...]
    lit = jnp.zeros_like(owner)
    for group in range(flags_ref.shape[0]):
        flag = jnp.broadcast_to(flags_ref[group].astype(jnp.float32), owner.shape)
        lit = jnp.where(owner == float(group), flag, lit)
    out_ref[...] = heat_ref[...] * lit[:1]


def local(
    gases,
    pressure_bin,
    layer_mass,
    cos_zenith,
    surface_albedo,
    column_order,
    sunlit,
    absorption,
    scattering,
):
    group_size = lax.axis_size("span")
    gas_count, levels, columns = gases.shape
    points, _, bins = absorption.shape
    rows = gas_count * levels + levels + PACK
    blocks = columns // LANES
    gas_rows = gas_count * BIN_ROWS
    hbm = pl.BlockSpec(memory_space=pltpu.HBM)
    vmem = pl.BlockSpec(memory_space=pltpu.VMEM)

    def pinned(*operands):
        return [pltpu.with_memory_space_constraint(operand, pltpu.HBM) for operand in operands]

    params = pltpu.CompilerParams(vmem_limit_bytes=VMEM_BYTES)
    wanted, table, scatter, block, owner = pl.pallas_call(
        functools.partial(prepare_kernel, columns // group_size),
        out_shape=(
            jax.ShapeDtypeStruct((group_size, 1, 1), sunlit.dtype),
            jax.ShapeDtypeStruct((points, gas_rows), jnp.bfloat16),
            jax.ShapeDtypeStruct((points, BIN_ROWS), jnp.bfloat16),
            jax.ShapeDtypeStruct((blocks, rows, LANES), jnp.float32),
            jax.ShapeDtypeStruct((ROWS, columns), jnp.float32),
        ),
        in_specs=[hbm] * 8,
        out_specs=(hbm, vmem, vmem, vmem, vmem),
        scratch_shapes=[
            pltpu.SMEM(sunlit.shape, sunlit.dtype),
            pltpu.VMEM(gases.shape, gases.dtype),
            pltpu.VMEM(pressure_bin.shape, pressure_bin.dtype),
            pltpu.VMEM(cos_zenith.shape, cos_zenith.dtype),
            pltpu.VMEM(surface_albedo.shape, surface_albedo.dtype),
            pltpu.VMEM((1, columns), column_order.dtype),
            pltpu.VMEM((gas_count, bins, points), absorption.dtype),
            pltpu.VMEM((bins, points), scattering.dtype),
            pltpu.VMEM((group_size, 1, 1), sunlit.dtype),
            pltpu.SemaphoreType.DMA((9,)),
            pltpu.VMEM((-(-(gas_rows + BIN_ROWS) // LANES) * LANES, LANES), jnp.float32),
        ],
        compiler_params=params,
    )(
        *pinned(
            sunlit,
            gases,
            pressure_bin,
            cos_zenith,
            surface_albedo,
            column_order.reshape(1, columns),
            jnp.transpose(absorption, (1, 2, 0)),
            jnp.transpose(scattering),
        )
    )
    flags = lax.all_to_all(wanted, "span", split_axis=0, concat_axis=0, tiled=True)
    field = pltpu.VMEM((levels, points, LANES), jnp.float32)
    state = pltpu.VMEM((points, LANES), jnp.float32)
    heat = pl.pallas_call(
        heating_kernel,
        out_shape=jax.ShapeDtypeStruct((levels, columns), jnp.float32),
        in_specs=[hbm, vmem, vmem, vmem],
        out_specs=vmem,
        scratch_shapes=[
            pltpu.VMEM(layer_mass.shape, layer_mass.dtype),
            pltpu.SemaphoreType.DMA(()),
            pltpu.VMEM((levels, 2 * points, LANES), jnp.float32),
            field,
            field,
            field,
            state,
            state,
            state,
            pltpu.VMEM((HALVES, levels + 1, ROWS, LANES), jnp.float32),
            pltpu.VMEM((levels + 1, ROWS, LANES), jnp.float32),
            pltpu.VMEM((blocks, levels, LANES), jnp.float32),
        ],
        compiler_params=params,
        cost_estimate=pl.CostEstimate(
            flops=40 * levels * points * columns, bytes_accessed=1 << 20, transcendentals=3 * levels * points * columns
        ),
    )(*pinned(layer_mass), table, scatter, block)
    return pl.pallas_call(
        shade_kernel,
        out_shape=jax.ShapeDtypeStruct((levels, columns), heat.dtype),
        in_specs=[vmem] * 3,
        out_specs=vmem,
        compiler_params=params,
    )(heat, owner, flags)


def solution(mesh):
    placed = (
        P(None, None, ("band", "span")),
        P(None, ("band", "span")),
        P(None, ("band", "span")),
        P(("band", "span")),
        P(("band", "span")),
        P(("band", "span")),
        P(("band", "span")),
        P(),
        P(),
    )
    return jax.shard_map(
        local, mesh=mesh, in_specs=placed, out_specs=P(None, ("band", "span")), check_vma=False
    )
```

```python
import functools
import math

import jax
import jax.numpy as jnp
from jax import lax
from jax.experimental import pallas as pl
from jax.experimental.pallas import tpu as pltpu
from jax.sharding import PartitionSpec as P

LANES = 128
ROWS = 8
PACK = 16
STEP = 8
HALVES = 2
BIN_ROWS = 64
LOG2E = math.log2(math.e)
VMEM_BYTES = 32 * 1024 * 1024


def one_hot(hit):
    return jnp.where(hit, 1.0, 0.0).astype(jnp.bfloat16)


def prepare_kernel(
    per_peer,
    sunlit_hbm,
    gases_hbm,
    bins_hbm,
    cosine_hbm,
    ground_hbm,
    order_hbm,
    absorb_hbm,
    scatter_hbm,
    wanted_hbm,
    table_ref,
    scatter_ref,
    block_ref,
    owner_ref,
    sunlit_ref,
    gases_ref,
    bins_ref,
    cosine_ref,
    ground_ref,
    order_ref,
    absorb_ref,
    albedo_ref,
    wanted_ref,
    copied,
    wide_buf,
):
    gas_count, levels, columns = gases_ref.shape
    points = table_ref.shape[0]
    bin_count = absorb_ref.shape[1]
    blocks = columns // LANES
    bin_row = gas_count * levels
    ray_row = bin_row + levels
    first_row = gas_count * BIN_ROWS
    peers = wanted_ref.shape[0]

    copies = [
        pltpu.make_async_copy(source, target, copied.at[place])
        for place, (source, target) in enumerate(
            (
                (sunlit_hbm, sunlit_ref),
                (order_hbm, order_ref),
                (absorb_hbm, absorb_ref),
                (scatter_hbm, albedo_ref),
                (cosine_hbm, cosine_ref),
                (ground_hbm, ground_ref),
                (bins_hbm, bins_ref),
                (gases_hbm, gases_ref),
            )
        )
    ]
    for copy in copies:
        copy.start()
    wide_buf[...] = jnp.zeros_like(wide_buf)
    copies[0].wait()
    for peer in range(peers):
        wanted_ref[peer] = jnp.full((1, 1), sunlit_ref[peer * sunlit_ref.shape[0] // peers], jnp.int32)
    sending = pltpu.make_async_copy(wanted_ref, wanted_hbm, copied.at[len(copies)])
    sending.start()
    for copy in copies[1:4]:
        copy.wait()

    square = (columns, columns)
    order = jnp.broadcast_to(order_ref[...], square)
    match = one_hot(order == lax.broadcasted_iota(jnp.int32, square, 0))
    place = lax.broadcasted_iota(jnp.int32, (ROWS, columns), 1)
    group = (place // per_peer).astype(jnp.float32).astype(jnp.bfloat16)
    owner_ref[...] = lax.dot_general(group, match, (((1,), (1,)), ((), ())), preferred_element_type=jnp.float32)

    for gas in range(gas_count):
        wide_buf[gas * BIN_ROWS : gas * BIN_ROWS + bin_count, :points] = absorb_ref[gas].astype(jnp.float32)
    wide_buf[first_row : first_row + bin_count, :points] = 0.5 * albedo_ref[...].astype(jnp.float32)
    turned = [
        jnp.transpose(wide_buf[i * LANES : (i + 1) * LANES])[:points].astype(jnp.bfloat16)
        for i in range(wide_buf.shape[0] // LANES)
    ]
    whole = jnp.concatenate(turned, axis=1)
    table_ref[...] = whole[:, :first_row]
    scatter_ref[...] = whole[:, first_row : first_row + BIN_ROWS]
    for copy in copies[4:]:
        copy.wait()

    for block in range(blocks):
        cols = slice(block * LANES, (block + 1) * LANES)
        for gas in range(gas_count):
            block_ref[block, gas * levels : (gas + 1) * levels] = gases_ref[gas, :, cols].astype(jnp.float32)
        block_ref[block, bin_row:ray_row] = bins_ref[:, cols].astype(jnp.float32)
    wide = (1, columns)
    cosines = cosine_ref[...].astype(jnp.float32).reshape(wide)
    grounds = ground_ref[...].astype(jnp.float32).reshape(wide)
    for block in range(blocks):
        cols = slice(block * LANES, (block + 1) * LANES)
        block_ref[block, ray_row : ray_row + ROWS] = jnp.broadcast_to(cosines[:, cols], (ROWS, LANES))
        block_ref[block, ray_row + ROWS : ray_row + 2 * ROWS] = jnp.broadcast_to(grounds[:, cols], (ROWS, LANES))
    sending.wait()


def heating_kernel(
    mass_hbm,
    table_ref,
    scatter_ref,
    block_ref,
    heat_ref,
    mass_ref,
    copied,
    optic_ref,
    even_up,
    even_rise,
    even_pass,
    even_start,
    even_gain,
    odd_up,
    odd_rise,
    odd_pass,
    odd_start,
    odd_gain,
    refl_buf,
    fall_buf,
    direct_buf,
    net_buf,
    warm_ref,
):
    levels, columns = heat_ref.shape
    points, gas_rows = table_ref.shape
    gas_count = gas_rows // BIN_ROWS
    half = points // HALVES
    vregs = half // ROWS
    blocks = columns // LANES
    bin_row = gas_count * levels
    ray_row = bin_row + levels
    mass_copy = pltpu.make_async_copy(mass_hbm, mass_ref, copied)
    mass_copy.start()

    def optical(slot, layer):
        parts = []
        shape = (BIN_ROWS, LANES)
        rows = lax.broadcasted_iota(jnp.int32, shape, 0).astype(jnp.float32).astype(jnp.bfloat16)
        one = jnp.ones(shape, jnp.bfloat16)
        zero = jnp.zeros(shape, jnp.bfloat16)
        selectors = []
        for near in (layer, layer + 1):
            place = bin_row + near
            bins = jnp.broadcast_to(block_ref[slot, place : place + 1, :], (PACK, LANES)).astype(jnp.bfloat16)
            bins = jnp.concatenate([bins] * (BIN_ROWS // PACK), axis=0)
            selectors.append(jnp.where(bins == rows, one, zero))
        for gas in range(gas_count):
            pair = []
            for near, selector in zip((layer, layer + 1), selectors):
                place = gas * levels + near
                amount = jnp.broadcast_to(block_ref[slot, place : place + 1, :], (PACK, LANES)).astype(jnp.bfloat16)
                pair.append(jnp.concatenate([amount] * (BIN_ROWS // PACK), axis=0) * selector)
            parts.append(jnp.concatenate(pair, axis=1))
        weighted = jnp.concatenate(parts, axis=0)
        selected = jnp.concatenate(selectors, axis=1)
        tau = jnp.dot(table_ref[...], weighted, preferred_element_type=jnp.float32)
        albedo = jnp.dot(scatter_ref[...], selected, preferred_element_type=jnp.float32)
        for near in range(2):
            cols = slice(near * LANES, (near + 1) * LANES)
            optic_ref[layer + near, :points] = tau[:, cols]
            optic_ref[layer + near, points:] = albedo[:, cols]

    def advance(first, part, cosine, slope, kept):
        up_buf, rise_buf, pass_buf, _, gain_buf = kept
        rows = slice(part * half, (part + 1) * half)
        half_rows = slice(points + part * half, points + (part + 1) * half)
        shape = (vregs, ROWS, LANES)
        if first > 0:
            refl = refl_buf[rows].reshape(shape)
            fall = fall_buf[rows].reshape(shape)
            direct = direct_buf[rows].reshape(shape)
        else:
            direct = jnp.broadcast_to(cosine[None], shape)
        for layer in range(first, first + STEP):
            tau = optic_ref[layer, rows].reshape(shape)
            half_albedo = optic_ref[layer, half_rows].reshape(shape)
            fading = jnp.exp2(tau * (-1.66 * LOG2E))
            passed = jnp.exp2(tau * slope)
            reflect = half_albedo * (1.0 - fading)
            transmit = fading + reflect
            below = direct * passed
            source = half_albedo * (direct - below)
            if layer == 0:
                up_buf[layer, rows] = transmit.reshape(half, LANES)
                rise_buf[layer, rows] = source.reshape(half, LANES)
                fall = source
                refl = reflect
            else:
                pass_buf[layer, rows] = (1.0 - refl).reshape(half, LANES)
                inverse = pl.reciprocal(1.0 - reflect * refl, approx=True)
                up = transmit * inverse
                rise = (reflect * fall + source) * inverse
                up_buf[layer, rows] = up.reshape(half, LANES)
                rise_buf[layer, rows] = rise.reshape(half, LANES)
                fall = source + transmit * (fall + refl * rise)
                refl = reflect + transmit * (refl * up)
            direct = below
            gain_buf[part, layer + 1] = jnp.sum(direct + fall, axis=0)
        refl_buf[rows] = refl.reshape(half, LANES)
        fall_buf[rows] = fall.reshape(half, LANES)
        direct_buf[rows] = direct.reshape(half, LANES)

    lead = range(0, STEP, 2)
    whole = (points // ROWS, ROWS, LANES)

    def total(gain_buf, level):
        summed = gain_buf[0, level]
        for part in range(1, HALVES):
            summed = summed + gain_buf[part, level]
        return summed

    def descend(block, kept, other):
        cosine = block_ref[block, ray_row : ray_row + ROWS]
        slope = (-LOG2E) / cosine
        gain_buf = kept[4]
        for part in range(HALVES):
            gain_buf[part, 0] = cosine * float(vregs)
        rising = other[3][...].reshape(whole)
        following = jnp.minimum(block + 1, blocks - 1)
        for first in range(0, levels, STEP):
            coming = [(block, layer) for layer in range(first + STEP, first + 2 * STEP, 2) if layer < levels]
            if not coming:
                coming = [(following, layer) for layer in lead]
            for part in range(HALVES):
                for where, layer in coming[part * len(coming) // HALVES : (part + 1) * len(coming) // HALVES]:
                    optical(where, layer)
                advance(first, part, cosine, slope, kept)
                if part == 0:
                    rising = ascend(levels - first, rising, other)
        albedo = block_ref[block, ray_row + ROWS : ray_row + 2 * ROWS]
        refl = refl_buf[...].reshape(whole)
        arriving = (fall_buf[...] + direct_buf[...]).reshape(whole)
        started = albedo * arriving * pl.reciprocal(1.0 - albedo * refl, approx=True)
        kept[3][...] = started.reshape(points, LANES)
        gain_buf[0, levels] = gain_buf[0, levels] - jnp.sum(started * (1.0 - refl), axis=0)

    def ascend(end, rising, kept):
        up_buf, rise_buf, pass_buf, _, gain_buf = kept
        if end == levels:
            net_buf[levels] = total(gain_buf, levels)
        for layer in range(end - 1, end - STEP - 1, -1):
            rising = up_buf[layer].reshape(whole) * rising + rise_buf[layer].reshape(whole)
            taken = rising if layer == 0 else rising * pass_buf[layer].reshape(whole)
            net_buf[layer] = total(gain_buf, layer) - jnp.sum(taken, axis=0)
        return rising

    def finish(block):
        warm_ref[block] = jnp.sum(net_buf[:levels] - net_buf[1:], axis=1)

    even = (even_up, even_rise, even_pass, even_start, even_gain)
    odd = (odd_up, odd_rise, odd_pass, odd_start, odd_gain)

    def block_pair(pair, carry):
        block = 2 * pair
        descend(block, even, odd)
        finish(jnp.where(pair == 0, blocks, block - 1))
        descend(block + 1, odd, even)
        finish(block)
        return carry

    for layer in lead:
        optical(0, layer)
    lax.fori_loop(0, blocks // 2, block_pair, 0)
    rising = odd_start[...].reshape(whole)
    for first in range(0, levels, STEP):
        rising = ascend(levels - first, rising, odd)
    finish(blocks - 1)
    mass_copy.wait()

    for block in range(blocks):
        cols = slice(block * LANES, (block + 1) * LANES)
        heat_ref[:, cols] = warm_ref[block] / mass_ref[:, cols].astype(jnp.float32)


def shade_kernel(heat_ref, owner_ref, flags_ref, out_ref):
    owner = owner_ref[...]
    lit = jnp.zeros_like(owner)
    for group in range(flags_ref.shape[0]):
        flag = jnp.broadcast_to(flags_ref[group].astype(jnp.float32), owner.shape)
        lit = jnp.where(owner == float(group), flag, lit)
    out_ref[...] = heat_ref[...] * lit[:1]


def local(
    gases,
    pressure_bin,
    layer_mass,
    cos_zenith,
    surface_albedo,
    column_order,
    sunlit,
    absorption,
    scattering,
):
    group_size = lax.axis_size("span")
    gas_count, levels, columns = gases.shape
    points, _, bins = absorption.shape
    rows = gas_count * levels + levels + PACK
    blocks = columns // LANES
    gas_rows = gas_count * BIN_ROWS
    hbm = pl.BlockSpec(memory_space=pltpu.HBM)
    vmem = pl.BlockSpec(memory_space=pltpu.VMEM)

    def pinned(*operands):
        return [pltpu.with_memory_space_constraint(operand, pltpu.HBM) for operand in operands]

    params = pltpu.CompilerParams(vmem_limit_bytes=VMEM_BYTES)
    wanted, table, scatter, block, owner = pl.pallas_call(
        functools.partial(prepare_kernel, columns // group_size),
        out_shape=(
            jax.ShapeDtypeStruct((group_size, 1, 1), sunlit.dtype),
            jax.ShapeDtypeStruct((points, gas_rows), jnp.bfloat16),
            jax.ShapeDtypeStruct((points, BIN_ROWS), jnp.bfloat16),
            jax.ShapeDtypeStruct((blocks, rows, LANES), jnp.float32),
            jax.ShapeDtypeStruct((ROWS, columns), jnp.float32),
        ),
        in_specs=[hbm] * 8,
        out_specs=(hbm, vmem, vmem, vmem, vmem),
        scratch_shapes=[
            pltpu.SMEM(sunlit.shape, sunlit.dtype),
            pltpu.VMEM(gases.shape, gases.dtype),
            pltpu.VMEM(pressure_bin.shape, pressure_bin.dtype),
            pltpu.VMEM(cos_zenith.shape, cos_zenith.dtype),
            pltpu.VMEM(surface_albedo.shape, surface_albedo.dtype),
            pltpu.VMEM((1, columns), column_order.dtype),
            pltpu.VMEM((gas_count, bins, points), absorption.dtype),
            pltpu.VMEM((bins, points), scattering.dtype),
            pltpu.VMEM((group_size, 1, 1), sunlit.dtype),
            pltpu.SemaphoreType.DMA((9,)),
            pltpu.VMEM((-(-(gas_rows + BIN_ROWS) // LANES) * LANES, LANES), jnp.float32),
        ],
        compiler_params=params,
    )(
        *pinned(
            sunlit,
            gases,
            pressure_bin,
            cos_zenith,
            surface_albedo,
            column_order.reshape(1, columns),
            jnp.transpose(absorption, (1, 2, 0)),
            jnp.transpose(scattering),
        )
    )
    flags = lax.all_to_all(wanted, "span", split_axis=0, concat_axis=0, tiled=True)
    field = pltpu.VMEM((levels, points, LANES), jnp.float32)
    state = pltpu.VMEM((points, LANES), jnp.float32)
    kept = (field, field, field, state, pltpu.VMEM((HALVES, levels + 1, ROWS, LANES), jnp.float32))
    heat = pl.pallas_call(
        heating_kernel,
        out_shape=jax.ShapeDtypeStruct((levels, columns), jnp.float32),
        in_specs=[hbm, vmem, vmem, vmem],
        out_specs=vmem,
        scratch_shapes=[
            pltpu.VMEM(layer_mass.shape, layer_mass.dtype),
            pltpu.SemaphoreType.DMA(()),
            pltpu.VMEM((levels, 2 * points, LANES), jnp.float32),
            *kept,
            *kept,
            state,
            state,
            state,
            pltpu.VMEM((levels + 1, ROWS, LANES), jnp.float32),
            pltpu.VMEM((blocks + 1, levels, LANES), jnp.float32),
        ],
        compiler_params=params,
        cost_estimate=pl.CostEstimate(
            flops=40 * levels * points * columns, bytes_accessed=1 << 20, transcendentals=3 * levels * points * columns
        ),
    )(*pinned(layer_mass), table, scatter, block)
    return pl.pallas_call(
        shade_kernel,
        out_shape=jax.ShapeDtypeStruct((levels, columns), heat.dtype),
        in_specs=[vmem] * 3,
        out_specs=vmem,
        compiler_params=params,
    )(heat, owner, flags)


def solution(mesh):
    placed = (
        P(None, None, ("band", "span")),
        P(None, ("band", "span")),
        P(None, ("band", "span")),
        P(("band", "span")),
        P(("band", "span")),
        P(("band", "span")),
        P(("band", "span")),
        P(),
        P(),
    )
    return jax.shard_map(
        local, mesh=mesh, in_specs=placed, out_specs=P(None, ("band", "span")), check_vma=False
    )
```

```python
import functools
import math

import jax
import jax.numpy as jnp
from jax import lax
from jax.experimental import pallas as pl
from jax.experimental.pallas import tpu as pltpu
from jax.sharding import PartitionSpec as P

LANES = 128
ROWS = 8
PACK = 16
STEP = 4
HALVES = 2
BIN_ROWS = 64
LOG2E = math.log2(math.e)
VMEM_BYTES = 24 * 1024 * 1024


def one_hot(hit):
    return jnp.where(hit, 1.0, 0.0).astype(jnp.bfloat16)


def prepare_kernel(
    per_peer,
    sunlit_hbm,
    gases_hbm,
    bins_hbm,
    cosine_hbm,
    ground_hbm,
    order_hbm,
    absorb_hbm,
    scatter_hbm,
    wanted_hbm,
    table_ref,
    scatter_ref,
    block_ref,
    owner_ref,
    sunlit_ref,
    gases_ref,
    bins_ref,
    cosine_ref,
    ground_ref,
    order_ref,
    absorb_ref,
    albedo_ref,
    wanted_ref,
    copied,
    wide_buf,
):
    gas_count, levels, columns = gases_ref.shape
    points = table_ref.shape[0]
    bin_count = absorb_ref.shape[1]
    blocks = columns // LANES
    bin_row = gas_count * levels
    ray_row = bin_row + levels
    first_row = gas_count * BIN_ROWS
    peers = wanted_ref.shape[0]

    copies = [
        pltpu.make_async_copy(source, target, copied.at[place])
        for place, (source, target) in enumerate(
            (
                (sunlit_hbm, sunlit_ref),
                (order_hbm, order_ref),
                (absorb_hbm, absorb_ref),
                (scatter_hbm, albedo_ref),
                (cosine_hbm, cosine_ref),
                (ground_hbm, ground_ref),
                (bins_hbm, bins_ref),
                (gases_hbm, gases_ref),
            )
        )
    ]
    for copy in copies:
        copy.start()
    wide_buf[...] = jnp.zeros_like(wide_buf)
    copies[0].wait()
    for peer in range(peers):
        wanted_ref[peer] = jnp.full((1, 1), sunlit_ref[peer * sunlit_ref.shape[0] // peers], jnp.int32)
    sending = pltpu.make_async_copy(wanted_ref, wanted_hbm, copied.at[len(copies)])
    sending.start()
    for copy in copies[1:4]:
        copy.wait()

    square = (columns, columns)
    order = jnp.broadcast_to(order_ref[...], square)
    match = one_hot(order == lax.broadcasted_iota(jnp.int32, square, 0))
    place = lax.broadcasted_iota(jnp.int32, (ROWS, columns), 1)
    group = (place // per_peer).astype(jnp.float32).astype(jnp.bfloat16)
    owner_ref[...] = lax.dot_general(group, match, (((1,), (1,)), ((), ())), preferred_element_type=jnp.float32)

    for gas in range(gas_count):
        wide_buf[gas * BIN_ROWS : gas * BIN_ROWS + bin_count, :points] = absorb_ref[gas].astype(jnp.float32)
    wide_buf[first_row : first_row + bin_count, :points] = 0.5 * albedo_ref[...].astype(jnp.float32)
    turned = [
        jnp.transpose(wide_buf[i * LANES : (i + 1) * LANES])[:points].astype(jnp.bfloat16)
        for i in range(wide_buf.shape[0] // LANES)
    ]
    whole = jnp.concatenate(turned, axis=1)
    table_ref[...] = whole[:, :first_row]
    scatter_ref[...] = whole[:, first_row : first_row + BIN_ROWS]
    for copy in copies[4:]:
        copy.wait()

    for block in range(blocks):
        cols = slice(block * LANES, (block + 1) * LANES)
        for gas in range(gas_count):
            block_ref[block, gas * levels : (gas + 1) * levels] = gases_ref[gas, :, cols].astype(jnp.float32)
        block_ref[block, bin_row:ray_row] = bins_ref[:, cols].astype(jnp.float32)
    wide = (1, columns)
    cosines = cosine_ref[...].astype(jnp.float32).reshape(wide)
    grounds = ground_ref[...].astype(jnp.float32).reshape(wide)
    for block in range(blocks):
        cols = slice(block * LANES, (block + 1) * LANES)
        block_ref[block, ray_row : ray_row + ROWS] = jnp.broadcast_to(cosines[:, cols], (ROWS, LANES))
        block_ref[block, ray_row + ROWS : ray_row + 2 * ROWS] = jnp.broadcast_to(grounds[:, cols], (ROWS, LANES))
    sending.wait()


def heating_kernel(
    mass_hbm,
    table_ref,
    scatter_ref,
    block_ref,
    heat_ref,
    mass_ref,
    copied,
    optic_even,
    optic_odd,
    up_buf,
    rise_buf,
    pass_buf,
    refl_buf,
    fall_buf,
    direct_buf,
    gain_buf,
    net_buf,
    warm_ref,
):
    levels, columns = heat_ref.shape
    points, gas_rows = table_ref.shape
    gas_count = gas_rows // BIN_ROWS
    half = points // HALVES
    vregs = half // ROWS
    blocks = columns // LANES
    bin_row = gas_count * levels
    ray_row = bin_row + levels
    mass_copy = pltpu.make_async_copy(mass_hbm, mass_ref, copied)
    mass_copy.start()

    def optical(slot, layer, place_at, optic_ref):
        parts = []
        shape = (BIN_ROWS, LANES)
        rows = lax.broadcasted_iota(jnp.int32, shape, 0).astype(jnp.float32).astype(jnp.bfloat16)
        one = jnp.ones(shape, jnp.bfloat16)
        zero = jnp.zeros(shape, jnp.bfloat16)
        selectors = []
        for near in (layer, layer + 1):
            place = bin_row + near
            bins = jnp.broadcast_to(block_ref[slot, pl.ds(place, 1), :], (PACK, LANES)).astype(jnp.bfloat16)
            bins = jnp.concatenate([bins] * (BIN_ROWS // PACK), axis=0)
            selectors.append(jnp.where(bins == rows, one, zero))
        for gas in range(gas_count):
            pair = []
            for near, selector in zip((layer, layer + 1), selectors):
                place = gas * levels + near
                amount = jnp.broadcast_to(block_ref[slot, pl.ds(place, 1), :], (PACK, LANES)).astype(jnp.bfloat16)
                pair.append(jnp.concatenate([amount] * (BIN_ROWS // PACK), axis=0) * selector)
            parts.append(jnp.concatenate(pair, axis=1))
        weighted = jnp.concatenate(parts, axis=0)
        selected = jnp.concatenate(selectors, axis=1)
        tau = jnp.dot(table_ref[...], weighted, preferred_element_type=jnp.float32)
        albedo = jnp.dot(scatter_ref[...], selected, preferred_element_type=jnp.float32)
        for near in range(2):
            cols = slice(near * LANES, (near + 1) * LANES)
            optic_ref[place_at + near, :points] = tau[:, cols]
            optic_ref[place_at + near, points:] = albedo[:, cols]

    def advance(first, part, slope, optic_ref):
        rows = slice(part * half, (part + 1) * half)
        half_rows = slice(points + part * half, points + (part + 1) * half)
        shape = (vregs, ROWS, LANES)
        refl = refl_buf[rows].reshape(shape)
        fall = fall_buf[rows].reshape(shape)
        direct = direct_buf[rows].reshape(shape)
        for slot in range(STEP):
            layer = first + slot
            tau = optic_ref[slot, rows].reshape(shape)
            half_albedo = optic_ref[slot, half_rows].reshape(shape)
            fading = jnp.exp2(tau * (-1.66 * LOG2E))
            passed = jnp.exp2(tau * slope)
            reflect = half_albedo * (1.0 - fading)
            transmit = fading + reflect
            below = direct * passed
            source = half_albedo * (direct - below)
            pass_buf[layer, rows] = (1.0 - refl).reshape(half, LANES)
            inverse = pl.reciprocal(1.0 - reflect * refl, approx=True)
            up = transmit * inverse
            rise = (reflect * fall + source) * inverse
            up_buf[layer, rows] = up.reshape(half, LANES)
            rise_buf[layer, rows] = rise.reshape(half, LANES)
            fall = source + transmit * (fall + refl * rise)
            refl = reflect + transmit * (refl * up)
            direct = below
            gain_buf[part, layer + 1] = jnp.sum(direct + fall, axis=0)
        refl_buf[rows] = refl.reshape(half, LANES)
        fall_buf[rows] = fall.reshape(half, LANES)
        direct_buf[rows] = direct.reshape(half, LANES)

    pairs = range(0, STEP, 2)
    whole = (points // ROWS, ROWS, LANES)

    def column_block(block, carry):
        cosine = block_ref[block, ray_row : ray_row + ROWS]
        albedo = block_ref[block, ray_row + ROWS : ray_row + 2 * ROWS]
        slope = (-LOG2E) / cosine
        refl_buf[...] = jnp.zeros_like(refl_buf)
        fall_buf[...] = jnp.zeros_like(fall_buf)
        direct_buf[...] = jnp.broadcast_to(cosine[:1], direct_buf.shape)
        for part in range(HALVES):
            gain_buf[part, 0] = cosine * float(vregs)

        def down(turn, inner):
            first = turn * (2 * STEP)
            wraps = first + 2 * STEP >= levels
            next_block = jnp.where(wraps, jnp.minimum(block + 1, blocks - 1), block)
            next_first = jnp.where(wraps, 0, first + 2 * STEP)
            for part in range(HALVES):
                for near in pairs[part * len(pairs) // HALVES : (part + 1) * len(pairs) // HALVES]:
                    optical(block, first + STEP + near, near, optic_odd)
                advance(first, part, slope, optic_even)
            for part in range(HALVES):
                for near in pairs[part * len(pairs) // HALVES : (part + 1) * len(pairs) // HALVES]:
                    optical(next_block, next_first + near, near, optic_even)
                advance(first + STEP, part, slope, optic_odd)
            return inner

        lax.fori_loop(0, levels // (2 * STEP), down, 0)

        def total(level):
            summed = gain_buf[0, level]
            for part in range(1, HALVES):
                summed = summed + gain_buf[part, level]
            return summed

        refl = refl_buf[...].reshape(whole)
        arriving = (fall_buf[...] + direct_buf[...]).reshape(whole)
        started = albedo * arriving * pl.reciprocal(1.0 - albedo * refl, approx=True)
        fall_buf[...] = started.reshape(points, LANES)
        net_buf[levels] = total(levels) - jnp.sum(started * (1.0 - refl), axis=0)

        def ascend(turn, inner):
            last = levels - 1 - turn * (2 * STEP)
            rising = fall_buf[...].reshape(whole)
            for slot in range(2 * STEP):
                layer = last - slot
                rising = up_buf[layer].reshape(whole) * rising + rise_buf[layer].reshape(whole)
                net_buf[layer] = total(layer) - jnp.sum(rising * pass_buf[layer].reshape(whole), axis=0)
            fall_buf[...] = rising.reshape(points, LANES)
            return inner

        lax.fori_loop(0, levels // (2 * STEP), ascend, 0)
        warm_ref[block] = jnp.sum(net_buf[:levels] - net_buf[1:], axis=1)
        return carry

    for near in pairs:
        optical(0, near, near, optic_even)
    lax.fori_loop(0, blocks, column_block, 0)
    mass_copy.wait()

    for block in range(blocks):
        cols = slice(block * LANES, (block + 1) * LANES)
        heat_ref[:, cols] = warm_ref[block] / mass_ref[:, cols].astype(jnp.float32)


def shade_kernel(heat_ref, owner_ref, flags_ref, out_ref):
    owner = owner_ref[...]
    lit = jnp.zeros_like(owner)
    for group in range(flags_ref.shape[0]):
        flag = jnp.broadcast_to(flags_ref[group].astype(jnp.float32), owner.shape)
        lit = jnp.where(owner == float(group), flag, lit)
    out_ref[...] = heat_ref[...] * lit[:1]


def local(
    gases,
    pressure_bin,
    layer_mass,
    cos_zenith,
    surface_albedo,
    column_order,
    sunlit,
    absorption,
    scattering,
):
    group_size = lax.axis_size("span")
    gas_count, levels, columns = gases.shape
    points, _, bins = absorption.shape
    rows = gas_count * levels + levels + PACK
    blocks = columns // LANES
    gas_rows = gas_count * BIN_ROWS
    hbm = pl.BlockSpec(memory_space=pltpu.HBM)
    vmem = pl.BlockSpec(memory_space=pltpu.VMEM)

    def pinned(*operands):
        return [pltpu.with_memory_space_constraint(operand, pltpu.HBM) for operand in operands]

    params = pltpu.CompilerParams(vmem_limit_bytes=VMEM_BYTES)
    wanted, table, scatter, block, owner = pl.pallas_call(
        functools.partial(prepare_kernel, columns // group_size),
        out_shape=(
            jax.ShapeDtypeStruct((group_size, 1, 1), sunlit.dtype),
            jax.ShapeDtypeStruct((points, gas_rows), jnp.bfloat16),
            jax.ShapeDtypeStruct((points, BIN_ROWS), jnp.bfloat16),
            jax.ShapeDtypeStruct((blocks, rows, LANES), jnp.float32),
            jax.ShapeDtypeStruct((ROWS, columns), jnp.float32),
        ),
        in_specs=[hbm] * 8,
        out_specs=(hbm, vmem, vmem, vmem, vmem),
        scratch_shapes=[
            pltpu.SMEM(sunlit.shape, sunlit.dtype),
            pltpu.VMEM(gases.shape, gases.dtype),
            pltpu.VMEM(pressure_bin.shape, pressure_bin.dtype),
            pltpu.VMEM(cos_zenith.shape, cos_zenith.dtype),
            pltpu.VMEM(surface_albedo.shape, surface_albedo.dtype),
            pltpu.VMEM((1, columns), column_order.dtype),
            pltpu.VMEM((gas_count, bins, points), absorption.dtype),
            pltpu.VMEM((bins, points), scattering.dtype),
            pltpu.VMEM((group_size, 1, 1), sunlit.dtype),
            pltpu.SemaphoreType.DMA((9,)),
            pltpu.VMEM((-(-(gas_rows + BIN_ROWS) // LANES) * LANES, LANES), jnp.float32),
        ],
        compiler_params=params,
    )(
        *pinned(
            sunlit,
            gases,
            pressure_bin,
            cos_zenith,
            surface_albedo,
            column_order.reshape(1, columns),
            jnp.transpose(absorption, (1, 2, 0)),
            jnp.transpose(scattering),
        )
    )
    flags = lax.all_to_all(wanted, "span", split_axis=0, concat_axis=0, tiled=True)
    field = pltpu.VMEM((levels, points, LANES), jnp.float32)
    state = pltpu.VMEM((points, LANES), jnp.float32)
    heat = pl.pallas_call(
        heating_kernel,
        out_shape=jax.ShapeDtypeStruct((levels, columns), jnp.float32),
        in_specs=[hbm, vmem, vmem, vmem],
        out_specs=vmem,
        scratch_shapes=[
            pltpu.VMEM(layer_mass.shape, layer_mass.dtype),
            pltpu.SemaphoreType.DMA(()),
            pltpu.VMEM((STEP, 2 * points, LANES), jnp.float32),
            pltpu.VMEM((STEP, 2 * points, LANES), jnp.float32),
            field,
            field,
            field,
            state,
            state,
            state,
            pltpu.VMEM((HALVES, levels + 1, ROWS, LANES), jnp.float32),
            pltpu.VMEM((levels + 1, ROWS, LANES), jnp.float32),
            pltpu.VMEM((blocks, levels, LANES), jnp.float32),
        ],
        compiler_params=params,
        cost_estimate=pl.CostEstimate(
            flops=40 * levels * points * columns, bytes_accessed=1 << 20, transcendentals=3 * levels * points * columns
        ),
    )(*pinned(layer_mass), table, scatter, block)
    return pl.pallas_call(
        shade_kernel,
        out_shape=jax.ShapeDtypeStruct((levels, columns), heat.dtype),
        in_specs=[vmem] * 3,
        out_specs=vmem,
        compiler_params=params,
    )(heat, owner, flags)


def solution(mesh):
    placed = (
        P(None, None, ("band", "span")),
        P(None, ("band", "span")),
        P(None, ("band", "span")),
        P(("band", "span")),
        P(("band", "span")),
        P(("band", "span")),
        P(("band", "span")),
        P(),
        P(),
    )
    return jax.shard_map(
        local, mesh=mesh, in_specs=placed, out_specs=P(None, ("band", "span")), check_vma=False
    )
```

```python
import functools
import math

import jax
import jax.numpy as jnp
from jax import lax
from jax.experimental import pallas as pl
from jax.experimental.pallas import tpu as pltpu
from jax.sharding import PartitionSpec as P

LANES = 128
ROWS = 8
PACK = 16
STEP = 8
HALVES = 1
BIN_ROWS = 64
LOG2E = math.log2(math.e)
VMEM_BYTES = 24 * 1024 * 1024


def one_hot(hit):
    return jnp.where(hit, 1.0, 0.0).astype(jnp.bfloat16)


def prepare_kernel(
    per_peer,
    sunlit_hbm,
    gases_hbm,
    bins_hbm,
    cosine_hbm,
    ground_hbm,
    order_hbm,
    absorb_hbm,
    scatter_hbm,
    wanted_hbm,
    table_ref,
    scatter_ref,
    block_ref,
    owner_ref,
    sunlit_ref,
    gases_ref,
    bins_ref,
    cosine_ref,
    ground_ref,
    order_ref,
    absorb_ref,
    albedo_ref,
    wanted_ref,
    copied,
    wide_buf,
):
    gas_count, levels, columns = gases_ref.shape
    points = table_ref.shape[0]
    bin_count = absorb_ref.shape[1]
    blocks = columns // LANES
    bin_row = gas_count * levels
    ray_row = bin_row + levels
    first_row = gas_count * BIN_ROWS
    peers = wanted_ref.shape[0]

    copies = [
        pltpu.make_async_copy(source, target, copied.at[place])
        for place, (source, target) in enumerate(
            (
                (sunlit_hbm, sunlit_ref),
                (order_hbm, order_ref),
                (absorb_hbm, absorb_ref),
                (scatter_hbm, albedo_ref),
                (cosine_hbm, cosine_ref),
                (ground_hbm, ground_ref),
                (bins_hbm, bins_ref),
                (gases_hbm, gases_ref),
            )
        )
    ]
    for copy in copies:
        copy.start()
    wide_buf[...] = jnp.zeros_like(wide_buf)
    copies[0].wait()
    for peer in range(peers):
        wanted_ref[peer] = jnp.full((1, 1), sunlit_ref[peer * sunlit_ref.shape[0] // peers], jnp.int32)
    sending = pltpu.make_async_copy(wanted_ref, wanted_hbm, copied.at[len(copies)])
    sending.start()
    for copy in copies[1:4]:
        copy.wait()

    square = (columns, columns)
    order = jnp.broadcast_to(order_ref[...], square)
    match = one_hot(order == lax.broadcasted_iota(jnp.int32, square, 0))
    place = lax.broadcasted_iota(jnp.int32, (ROWS, columns), 1)
    group = (place // per_peer).astype(jnp.float32).astype(jnp.bfloat16)
    owner_ref[...] = lax.dot_general(group, match, (((1,), (1,)), ((), ())), preferred_element_type=jnp.float32)

    for gas in range(gas_count):
        wide_buf[gas * BIN_ROWS : gas * BIN_ROWS + bin_count, :points] = absorb_ref[gas].astype(jnp.float32)
    wide_buf[first_row : first_row + bin_count, :points] = 0.5 * albedo_ref[...].astype(jnp.float32)
    turned = [
        jnp.transpose(wide_buf[i * LANES : (i + 1) * LANES])[:points].astype(jnp.bfloat16)
        for i in range(wide_buf.shape[0] // LANES)
    ]
    whole = jnp.concatenate(turned, axis=1)
    table_ref[...] = whole[:, :first_row]
    scatter_ref[...] = whole[:, first_row : first_row + BIN_ROWS]
    for copy in copies[4:]:
        copy.wait()

    for block in range(blocks):
        cols = slice(block * LANES, (block + 1) * LANES)
        for gas in range(gas_count):
            block_ref[block, gas * levels : (gas + 1) * levels] = gases_ref[gas, :, cols].astype(jnp.float32)
        block_ref[block, bin_row:ray_row] = bins_ref[:, cols].astype(jnp.float32)
    wide = (1, columns)
    cosines = cosine_ref[...].astype(jnp.float32).reshape(wide)
    grounds = ground_ref[...].astype(jnp.float32).reshape(wide)
    for block in range(blocks):
        cols = slice(block * LANES, (block + 1) * LANES)
        block_ref[block, ray_row : ray_row + ROWS] = jnp.broadcast_to(cosines[:, cols], (ROWS, LANES))
        block_ref[block, ray_row + ROWS : ray_row + 2 * ROWS] = jnp.broadcast_to(grounds[:, cols], (ROWS, LANES))
    sending.wait()


def heating_kernel(
    mass_hbm,
    table_ref,
    scatter_ref,
    block_ref,
    heat_ref,
    mass_ref,
    copied,
    optic_ref,
    up_buf,
    rise_buf,
    pass_buf,
    refl_buf,
    fall_buf,
    direct_buf,
    gain_buf,
    net_buf,
    warm_ref,
):
    levels, columns = heat_ref.shape
    points, gas_rows = table_ref.shape
    gas_count = gas_rows // BIN_ROWS
    half = points // HALVES
    vregs = half // ROWS
    blocks = columns // LANES
    bin_row = gas_count * levels
    ray_row = bin_row + levels
    mass_copy = pltpu.make_async_copy(mass_hbm, mass_ref, copied)
    mass_copy.start()

    def optical(slot, layer):
        parts = []
        shape = (BIN_ROWS, LANES)
        rows = lax.broadcasted_iota(jnp.int32, shape, 0).astype(jnp.float32).astype(jnp.bfloat16)
        one = jnp.ones(shape, jnp.bfloat16)
        zero = jnp.zeros(shape, jnp.bfloat16)
        selectors = []
        for near in (layer, layer + 1):
            place = bin_row + near
            bins = jnp.broadcast_to(block_ref[slot, place : place + 1, :], (PACK, LANES)).astype(jnp.bfloat16)
            bins = jnp.concatenate([bins] * (BIN_ROWS // PACK), axis=0)
            selectors.append(jnp.where(bins == rows, one, zero))
        for gas in range(gas_count):
            pair = []
            for near, selector in zip((layer, layer + 1), selectors):
                place = gas * levels + near
                amount = jnp.broadcast_to(block_ref[slot, place : place + 1, :], (PACK, LANES)).astype(jnp.bfloat16)
                pair.append(jnp.concatenate([amount] * (BIN_ROWS // PACK), axis=0) * selector)
            parts.append(jnp.concatenate(pair, axis=1))
        weighted = jnp.concatenate(parts, axis=0)
        selected = jnp.concatenate(selectors, axis=1)
        tau = jnp.dot(table_ref[...], weighted, preferred_element_type=jnp.float32)
        albedo = jnp.dot(scatter_ref[...], selected, preferred_element_type=jnp.float32)
        for near in range(2):
            cols = slice(near * LANES, (near + 1) * LANES)
            optic_ref[layer + near, :points] = tau[:, cols]
            optic_ref[layer + near, points:] = albedo[:, cols]

    def advance(first, part, cosine, slope):
        rows = slice(part * half, (part + 1) * half)
        half_rows = slice(points + part * half, points + (part + 1) * half)
        shape = (vregs, ROWS, LANES)
        if first > 0:
            refl = refl_buf[rows].reshape(shape)
            fall = fall_buf[rows].reshape(shape)
            direct = direct_buf[rows].reshape(shape)
        else:
            direct = jnp.broadcast_to(cosine[None], shape)
        for layer in range(first, first + STEP):
            tau = optic_ref[layer, rows].reshape(shape)
            half_albedo = optic_ref[layer, half_rows].reshape(shape)
            fading = jnp.exp2(tau * (-1.66 * LOG2E))
            passed = jnp.exp2(tau * slope)
            reflect = half_albedo * (1.0 - fading)
            transmit = fading + reflect
            below = direct * passed
            source = half_albedo * (direct - below)
            if layer == 0:
                up_buf[layer, rows] = transmit.reshape(half, LANES)
                rise_buf[layer, rows] = source.reshape(half, LANES)
                fall = source
                refl = reflect
            else:
                pass_buf[layer, rows] = (1.0 - refl).reshape(half, LANES)
                inverse = pl.reciprocal(1.0 - reflect * refl, approx=True)
                up = transmit * inverse
                rise = (reflect * fall + source) * inverse
                up_buf[layer, rows] = up.reshape(half, LANES)
                rise_buf[layer, rows] = rise.reshape(half, LANES)
                fall = source + transmit * (fall + refl * rise)
                refl = reflect + transmit * (refl * up)
            direct = below
            gain_buf[part, layer + 1] = jnp.sum(direct + fall, axis=0)
        refl_buf[rows] = refl.reshape(half, LANES)
        fall_buf[rows] = fall.reshape(half, LANES)
        direct_buf[rows] = direct.reshape(half, LANES)

    lead = range(0, STEP, 2)

    def column_block(block, carry):
        cosine = block_ref[block, ray_row : ray_row + ROWS]
        slope = (-LOG2E) / cosine
        for part in range(HALVES):
            gain_buf[part, 0] = cosine * float(vregs)
        for first in range(0, levels, STEP):
            coming = [layer for layer in range(first + STEP, first + 2 * STEP, 2) if layer < levels]
            for part in range(HALVES):
                for layer in coming[part * len(coming) // HALVES : (part + 1) * len(coming) // HALVES]:
                    optical(block, layer)
                advance(first, part, cosine, slope)

        following = jnp.minimum(block + 1, blocks - 1)
        for layer in lead:
            optical(following, layer)

        albedo = block_ref[block, ray_row + ROWS : ray_row + 2 * ROWS]
        shape = (points // ROWS, ROWS, LANES)
        refl = refl_buf[...].reshape(shape)
        arriving = (fall_buf[...] + direct_buf[...]).reshape(shape)
        rising = albedo * arriving * pl.reciprocal(1.0 - albedo * refl, approx=True)

        def total(level):
            summed = gain_buf[0, level]
            for part in range(1, HALVES):
                summed = summed + gain_buf[part, level]
            return summed

        net_buf[levels] = total(levels) - jnp.sum(rising * (1.0 - refl), axis=0)
        for layer in range(levels - 1, -1, -1):
            rising = up_buf[layer].reshape(shape) * rising + rise_buf[layer].reshape(shape)
            taken = rising if layer == 0 else rising * pass_buf[layer].reshape(shape)
            net_buf[layer] = total(layer) - jnp.sum(taken, axis=0)
        warm_ref[block] = jnp.sum(net_buf[:levels] - net_buf[1:], axis=1)
        return carry

    for layer in lead:
        optical(0, layer)
    lax.fori_loop(0, blocks, column_block, 0)
    mass_copy.wait()

    for block in range(blocks):
        cols = slice(block * LANES, (block + 1) * LANES)
        heat_ref[:, cols] = warm_ref[block] / mass_ref[:, cols].astype(jnp.float32)


def shade_kernel(heat_ref, owner_ref, flags_ref, out_ref):
    owner = owner_ref[...]
    lit = jnp.zeros_like(owner)
    for group in range(flags_ref.shape[0]):
        flag = jnp.broadcast_to(flags_ref[group].astype(jnp.float32), owner.shape)
        lit = jnp.where(owner == float(group), flag, lit)
    out_ref[...] = heat_ref[...] * lit[:1]


def local(
    gases,
    pressure_bin,
    layer_mass,
    cos_zenith,
    surface_albedo,
    column_order,
    sunlit,
    absorption,
    scattering,
):
    group_size = lax.axis_size("span")
    gas_count, levels, columns = gases.shape
    points, _, bins = absorption.shape
    rows = gas_count * levels + levels + PACK
    blocks = columns // LANES
    gas_rows = gas_count * BIN_ROWS
    hbm = pl.BlockSpec(memory_space=pltpu.HBM)
    vmem = pl.BlockSpec(memory_space=pltpu.VMEM)

    def pinned(*operands):
        return [pltpu.with_memory_space_constraint(operand, pltpu.HBM) for operand in operands]

    params = pltpu.CompilerParams(vmem_limit_bytes=VMEM_BYTES)
    wanted, table, scatter, block, owner = pl.pallas_call(
        functools.partial(prepare_kernel, columns // group_size),
        out_shape=(
            jax.ShapeDtypeStruct((group_size, 1, 1), sunlit.dtype),
            jax.ShapeDtypeStruct((points, gas_rows), jnp.bfloat16),
            jax.ShapeDtypeStruct((points, BIN_ROWS), jnp.bfloat16),
            jax.ShapeDtypeStruct((blocks, rows, LANES), jnp.float32),
            jax.ShapeDtypeStruct((ROWS, columns), jnp.float32),
        ),
        in_specs=[hbm] * 8,
        out_specs=(hbm, vmem, vmem, vmem, vmem),
        scratch_shapes=[
            pltpu.SMEM(sunlit.shape, sunlit.dtype),
            pltpu.VMEM(gases.shape, gases.dtype),
            pltpu.VMEM(pressure_bin.shape, pressure_bin.dtype),
            pltpu.VMEM(cos_zenith.shape, cos_zenith.dtype),
            pltpu.VMEM(surface_albedo.shape, surface_albedo.dtype),
            pltpu.VMEM((1, columns), column_order.dtype),
            pltpu.VMEM((gas_count, bins, points), absorption.dtype),
            pltpu.VMEM((bins, points), scattering.dtype),
            pltpu.VMEM((group_size, 1, 1), sunlit.dtype),
            pltpu.SemaphoreType.DMA((9,)),
            pltpu.VMEM((-(-(gas_rows + BIN_ROWS) // LANES) * LANES, LANES), jnp.float32),
        ],
        compiler_params=params,
    )(
        *pinned(
            sunlit,
            gases,
            pressure_bin,
            cos_zenith,
            surface_albedo,
            column_order.reshape(1, columns),
            jnp.transpose(absorption, (1, 2, 0)),
            jnp.transpose(scattering),
        )
    )
    flags = lax.all_to_all(wanted, "span", split_axis=0, concat_axis=0, tiled=True)
    field = pltpu.VMEM((levels, points, LANES), jnp.float32)
    state = pltpu.VMEM((points, LANES), jnp.float32)
    heat = pl.pallas_call(
        heating_kernel,
        out_shape=jax.ShapeDtypeStruct((levels, columns), jnp.float32),
        in_specs=[hbm, vmem, vmem, vmem],
        out_specs=vmem,
        scratch_shapes=[
            pltpu.VMEM(layer_mass.shape, layer_mass.dtype),
            pltpu.SemaphoreType.DMA(()),
            pltpu.VMEM((levels, 2 * points, LANES), jnp.float32),
            field,
            field,
            field,
            state,
            state,
            state,
            pltpu.VMEM((HALVES, levels + 1, ROWS, LANES), jnp.float32),
            pltpu.VMEM((levels + 1, ROWS, LANES), jnp.float32),
            pltpu.VMEM((blocks, levels, LANES), jnp.float32),
        ],
        compiler_params=params,
        cost_estimate=pl.CostEstimate(
            flops=40 * levels * points * columns, bytes_accessed=1 << 20, transcendentals=3 * levels * points * columns
        ),
    )(*pinned(layer_mass), table, scatter, block)
    return pl.pallas_call(
        shade_kernel,
        out_shape=jax.ShapeDtypeStruct((levels, columns), heat.dtype),
        in_specs=[vmem] * 3,
        out_specs=vmem,
        compiler_params=params,
    )(heat, owner, flags)


def solution(mesh):
    placed = (
        P(None, None, ("band", "span")),
        P(None, ("band", "span")),
        P(None, ("band", "span")),
        P(("band", "span")),
        P(("band", "span")),
        P(("band", "span")),
        P(("band", "span")),
        P(),
        P(),
    )
    return jax.shard_map(
        local, mesh=mesh, in_specs=placed, out_specs=P(None, ("band", "span")), check_vma=False
    )
```

```python
import functools
import math

import jax
import jax.numpy as jnp
from jax import lax
from jax.experimental import pallas as pl
from jax.experimental.pallas import tpu as pltpu
from jax.sharding import PartitionSpec as P

LANES = 128
ROWS = 8
PACK = 16
STEP = 8
HALVES = 2
BIN_ROWS = 64
LOG2E = math.log2(math.e)
VMEM_BYTES = 24 * 1024 * 1024


def one_hot(hit):
    return jnp.where(hit, 1.0, 0.0).astype(jnp.bfloat16)


def prepare_kernel(
    per_peer,
    sunlit_hbm,
    gases_hbm,
    bins_hbm,
    cosine_hbm,
    ground_hbm,
    order_hbm,
    absorb_hbm,
    scatter_hbm,
    wanted_hbm,
    table_ref,
    scatter_ref,
    block_ref,
    owner_ref,
    sunlit_ref,
    gases_ref,
    bins_ref,
    cosine_ref,
    ground_ref,
    order_ref,
    absorb_ref,
    albedo_ref,
    wanted_ref,
    copied,
    wide_buf,
):
    gas_count, levels, columns = gases_ref.shape
    points = table_ref.shape[0]
    bin_count = absorb_ref.shape[1]
    blocks = columns // LANES
    bin_row = gas_count * levels
    ray_row = bin_row + levels
    first_row = gas_count * BIN_ROWS
    peers = wanted_ref.shape[0]

    copies = [
        pltpu.make_async_copy(source, target, copied.at[place])
        for place, (source, target) in enumerate(
            (
                (sunlit_hbm, sunlit_ref),
                (order_hbm, order_ref),
                (absorb_hbm, absorb_ref),
                (scatter_hbm, albedo_ref),
                (cosine_hbm, cosine_ref),
                (ground_hbm, ground_ref),
                (bins_hbm, bins_ref),
                (gases_hbm, gases_ref),
            )
        )
    ]
    for copy in copies:
        copy.start()
    wide_buf[...] = jnp.zeros_like(wide_buf)
    copies[0].wait()
    for peer in range(peers):
        wanted_ref[peer] = jnp.full((1, 1), sunlit_ref[peer * sunlit_ref.shape[0] // peers], jnp.int32)
    sending = pltpu.make_async_copy(wanted_ref, wanted_hbm, copied.at[len(copies)])
    sending.start()
    for copy in copies[1:4]:
        copy.wait()

    square = (columns, columns)
    order = jnp.broadcast_to(order_ref[...], square)
    match = one_hot(order == lax.broadcasted_iota(jnp.int32, square, 0))
    place = lax.broadcasted_iota(jnp.int32, (ROWS, columns), 1)
    group = (place // per_peer).astype(jnp.float32).astype(jnp.bfloat16)
    owner_ref[...] = lax.dot_general(group, match, (((1,), (1,)), ((), ())), preferred_element_type=jnp.float32)

    for gas in range(gas_count):
        wide_buf[gas * BIN_ROWS : gas * BIN_ROWS + bin_count, :points] = absorb_ref[gas].astype(jnp.float32)
    wide_buf[first_row : first_row + bin_count, :points] = 0.5 * albedo_ref[...].astype(jnp.float32)
    turned = [
        jnp.transpose(wide_buf[i * LANES : (i + 1) * LANES])[:points].astype(jnp.bfloat16)
        for i in range(wide_buf.shape[0] // LANES)
    ]
    whole = jnp.concatenate(turned, axis=1)
    table_ref[...] = whole[:, :first_row]
    scatter_ref[...] = whole[:, first_row : first_row + BIN_ROWS]
    for copy in copies[4:]:
        copy.wait()

    for block in range(blocks):
        cols = slice(block * LANES, (block + 1) * LANES)
        for gas in range(gas_count):
            block_ref[block, gas * levels : (gas + 1) * levels] = gases_ref[gas, :, cols].astype(jnp.float32)
        block_ref[block, bin_row:ray_row] = bins_ref[:, cols].astype(jnp.float32)
    wide = (1, columns)
    cosines = cosine_ref[...].astype(jnp.float32).reshape(wide)
    grounds = ground_ref[...].astype(jnp.float32).reshape(wide)
    for block in range(blocks):
        cols = slice(block * LANES, (block + 1) * LANES)
        block_ref[block, ray_row : ray_row + ROWS] = jnp.broadcast_to(cosines[:, cols], (ROWS, LANES))
        block_ref[block, ray_row + ROWS : ray_row + 2 * ROWS] = jnp.broadcast_to(grounds[:, cols], (ROWS, LANES))
    sending.wait()


def heating_kernel(
    mass_hbm,
    table_ref,
    scatter_ref,
    block_ref,
    heat_ref,
    mass_ref,
    copied,
    optic_ref,
    up_buf,
    rise_buf,
    pass_buf,
    refl_buf,
    fall_buf,
    direct_buf,
    gain_buf,
    net_buf,
    warm_ref,
):
    levels, columns = heat_ref.shape
    points, gas_rows = table_ref.shape
    gas_count = gas_rows // BIN_ROWS
    half = points // HALVES
    vregs = half // ROWS
    blocks = columns // LANES
    bin_row = gas_count * levels
    ray_row = bin_row + levels
    mass_copy = pltpu.make_async_copy(mass_hbm, mass_ref, copied)
    mass_copy.start()

    def optical(slot, layer):
        parts = []
        shape = (BIN_ROWS, LANES)
        rows = lax.broadcasted_iota(jnp.int32, shape, 0).astype(jnp.float32).astype(jnp.bfloat16)
        one = jnp.ones(shape, jnp.bfloat16)
        zero = jnp.zeros(shape, jnp.bfloat16)
        selectors = []
        for near in (layer, layer + 1):
            place = bin_row + near
            bins = jnp.broadcast_to(block_ref[slot, place : place + 1, :], (PACK, LANES)).astype(jnp.bfloat16)
            bins = jnp.concatenate([bins] * (BIN_ROWS // PACK), axis=0)
            selectors.append(jnp.where(bins == rows, one, zero))
        for gas in range(gas_count):
            pair = []
            for near, selector in zip((layer, layer + 1), selectors):
                place = gas * levels + near
                amount = jnp.broadcast_to(block_ref[slot, place : place + 1, :], (PACK, LANES)).astype(jnp.bfloat16)
                pair.append(jnp.concatenate([amount] * (BIN_ROWS // PACK), axis=0) * selector)
            parts.append(jnp.concatenate(pair, axis=1))
        weighted = jnp.concatenate(parts, axis=0)
        selected = jnp.concatenate(selectors, axis=1)
        tau = jnp.dot(table_ref[...], weighted, preferred_element_type=jnp.float32)
        albedo = jnp.dot(scatter_ref[...], selected, preferred_element_type=jnp.float32)
        for near in range(2):
            cols = slice(near * LANES, (near + 1) * LANES)
            optic_ref[layer + near, :points] = tau[:, cols]
            optic_ref[layer + near, points:] = albedo[:, cols]

    def advance(first, part, cosine, slope):
        rows = slice(part * half, (part + 1) * half)
        half_rows = slice(points + part * half, points + (part + 1) * half)
        shape = (vregs, ROWS, LANES)
        if first > 0:
            refl = refl_buf[rows].reshape(shape)
            fall = fall_buf[rows].reshape(shape)
            direct = direct_buf[rows].reshape(shape)
        else:
            direct = jnp.broadcast_to(cosine[None], shape)
        for layer in range(first, first + STEP):
            tau = optic_ref[layer, rows].reshape(shape)
            half_albedo = optic_ref[layer, half_rows].reshape(shape)
            fading = jnp.exp2(tau * (-1.66 * LOG2E))
            passed = jnp.exp2(tau * slope)
            reflect = half_albedo * (1.0 - fading)
            transmit = fading + reflect
            below = direct * passed
            source = half_albedo * (direct - below)
            if layer == 0:
                up_buf[layer, rows] = transmit.reshape(half, LANES)
                rise_buf[layer, rows] = source.reshape(half, LANES)
                fall = source
                refl = reflect
            else:
                pass_buf[layer, rows] = (1.0 - refl).reshape(half, LANES)
                inverse = pl.reciprocal(1.0 - reflect * refl, approx=True)
                up = transmit * inverse
                rise = (reflect * fall + source) * inverse
                up_buf[layer, rows] = up.reshape(half, LANES)
                rise_buf[layer, rows] = rise.reshape(half, LANES)
                fall = source + transmit * (fall + refl * rise)
                refl = reflect + transmit * (refl * up)
            direct = below
            gain_buf[part, layer + 1] = jnp.sum(direct + fall, axis=0)
        refl_buf[rows] = refl.reshape(half, LANES)
        fall_buf[rows] = fall.reshape(half, LANES)
        direct_buf[rows] = direct.reshape(half, LANES)

    lead = range(0, STEP, 2)

    def column_block(block, carry):
        cosine = block_ref[block, ray_row : ray_row + ROWS]
        slope = (-LOG2E) / cosine
        for part in range(HALVES):
            gain_buf[part, 0] = cosine * float(vregs)
        for first in range(0, levels, STEP):
            coming = [layer for layer in range(first + STEP, first + 2 * STEP, 2) if layer < levels]
            for part in range(HALVES):
                advance(first, part, cosine, slope)
                for layer in coming[part * len(coming) // HALVES : (part + 1) * len(coming) // HALVES]:
                    optical(block, layer)

        following = jnp.minimum(block + 1, blocks - 1)
        for layer in lead:
            optical(following, layer)

        albedo = block_ref[block, ray_row + ROWS : ray_row + 2 * ROWS]
        shape = (points // ROWS, ROWS, LANES)
        refl = refl_buf[...].reshape(shape)
        arriving = (fall_buf[...] + direct_buf[...]).reshape(shape)
        rising = albedo * arriving * pl.reciprocal(1.0 - albedo * refl, approx=True)

        def total(level):
            summed = gain_buf[0, level]
            for part in range(1, HALVES):
                summed = summed + gain_buf[part, level]
            return summed

        net_buf[levels] = total(levels) - jnp.sum(rising * (1.0 - refl), axis=0)
        for layer in range(levels - 1, -1, -1):
            rising = up_buf[layer].reshape(shape) * rising + rise_buf[layer].reshape(shape)
            taken = rising if layer == 0 else rising * pass_buf[layer].reshape(shape)
            net_buf[layer] = total(layer) - jnp.sum(taken, axis=0)
        warm_ref[block] = jnp.sum(net_buf[:levels] - net_buf[1:], axis=1)
        return carry

    for layer in lead:
        optical(0, layer)
    lax.fori_loop(0, blocks, column_block, 0)
    mass_copy.wait()

    for block in range(blocks):
        cols = slice(block * LANES, (block + 1) * LANES)
        heat_ref[:, cols] = warm_ref[block] / mass_ref[:, cols].astype(jnp.float32)


def shade_kernel(heat_ref, owner_ref, flags_ref, out_ref):
    owner = owner_ref[...]
    lit = jnp.zeros_like(owner)
    for group in range(flags_ref.shape[0]):
        flag = jnp.broadcast_to(flags_ref[group].astype(jnp.float32), owner.shape)
        lit = jnp.where(owner == float(group), flag, lit)
    out_ref[...] = heat_ref[...] * lit[:1]


def local(
    gases,
    pressure_bin,
    layer_mass,
    cos_zenith,
    surface_albedo,
    column_order,
    sunlit,
    absorption,
    scattering,
):
    group_size = lax.axis_size("span")
    gas_count, levels, columns = gases.shape
    points, _, bins = absorption.shape
    rows = gas_count * levels + levels + PACK
    blocks = columns // LANES
    gas_rows = gas_count * BIN_ROWS
    hbm = pl.BlockSpec(memory_space=pltpu.HBM)
    vmem = pl.BlockSpec(memory_space=pltpu.VMEM)

    def pinned(*operands):
        return [pltpu.with_memory_space_constraint(operand, pltpu.HBM) for operand in operands]

    params = pltpu.CompilerParams(vmem_limit_bytes=VMEM_BYTES)
    wanted, table, scatter, block, owner = pl.pallas_call(
        functools.partial(prepare_kernel, columns // group_size),
        out_shape=(
            jax.ShapeDtypeStruct((group_size, 1, 1), sunlit.dtype),
            jax.ShapeDtypeStruct((points, gas_rows), jnp.bfloat16),
            jax.ShapeDtypeStruct((points, BIN_ROWS), jnp.bfloat16),
            jax.ShapeDtypeStruct((blocks, rows, LANES), jnp.float32),
            jax.ShapeDtypeStruct((ROWS, columns), jnp.float32),
        ),
        in_specs=[hbm] * 8,
        out_specs=(hbm, vmem, vmem, vmem, vmem),
        scratch_shapes=[
            pltpu.SMEM(sunlit.shape, sunlit.dtype),
            pltpu.VMEM(gases.shape, gases.dtype),
            pltpu.VMEM(pressure_bin.shape, pressure_bin.dtype),
            pltpu.VMEM(cos_zenith.shape, cos_zenith.dtype),
            pltpu.VMEM(surface_albedo.shape, surface_albedo.dtype),
            pltpu.VMEM((1, columns), column_order.dtype),
            pltpu.VMEM((gas_count, bins, points), absorption.dtype),
            pltpu.VMEM((bins, points), scattering.dtype),
            pltpu.VMEM((group_size, 1, 1), sunlit.dtype),
            pltpu.SemaphoreType.DMA((9,)),
            pltpu.VMEM((-(-(gas_rows + BIN_ROWS) // LANES) * LANES, LANES), jnp.float32),
        ],
        compiler_params=params,
    )(
        *pinned(
            sunlit,
            gases,
            pressure_bin,
            cos_zenith,
            surface_albedo,
            column_order.reshape(1, columns),
            jnp.transpose(absorption, (1, 2, 0)),
            jnp.transpose(scattering),
        )
    )
    flags = lax.all_to_all(wanted, "span", split_axis=0, concat_axis=0, tiled=True)
    field = pltpu.VMEM((levels, points, LANES), jnp.float32)
    state = pltpu.VMEM((points, LANES), jnp.float32)
    heat = pl.pallas_call(
        heating_kernel,
        out_shape=jax.ShapeDtypeStruct((levels, columns), jnp.float32),
        in_specs=[hbm, vmem, vmem, vmem],
        out_specs=vmem,
        scratch_shapes=[
            pltpu.VMEM(layer_mass.shape, layer_mass.dtype),
            pltpu.SemaphoreType.DMA(()),
            pltpu.VMEM((levels, 2 * points, LANES), jnp.float32),
            field,
            field,
            field,
            state,
            state,
            state,
            pltpu.VMEM((HALVES, levels + 1, ROWS, LANES), jnp.float32),
            pltpu.VMEM((levels + 1, ROWS, LANES), jnp.float32),
            pltpu.VMEM((blocks, levels, LANES), jnp.float32),
        ],
        compiler_params=params,
        cost_estimate=pl.CostEstimate(
            flops=40 * levels * points * columns, bytes_accessed=1 << 20, transcendentals=3 * levels * points * columns
        ),
    )(*pinned(layer_mass), table, scatter, block)
    return pl.pallas_call(
        shade_kernel,
        out_shape=jax.ShapeDtypeStruct((levels, columns), heat.dtype),
        in_specs=[vmem] * 3,
        out_specs=vmem,
        compiler_params=params,
    )(heat, owner, flags)


def solution(mesh):
    placed = (
        P(None, None, ("band", "span")),
        P(None, ("band", "span")),
        P(None, ("band", "span")),
        P(("band", "span")),
        P(("band", "span")),
        P(("band", "span")),
        P(("band", "span")),
        P(),
        P(),
    )
    return jax.shard_map(
        local, mesh=mesh, in_specs=placed, out_specs=P(None, ("band", "span")), check_vma=False
    )
```

```python
import functools
import math

import jax
import jax.numpy as jnp
from jax import lax
from jax.experimental import pallas as pl
from jax.experimental.pallas import tpu as pltpu
from jax.sharding import PartitionSpec as P

LANES = 128
ROWS = 8
PACK = 16
STEP = 4
HALVES = 2
BIN_ROWS = 64
LOG2E = math.log2(math.e)
VMEM_BYTES = 24 * 1024 * 1024


def one_hot(hit):
    return jnp.where(hit, 1.0, 0.0).astype(jnp.bfloat16)


def prepare_kernel(
    per_peer,
    sunlit_hbm,
    gases_hbm,
    bins_hbm,
    cosine_hbm,
    ground_hbm,
    order_hbm,
    absorb_hbm,
    scatter_hbm,
    wanted_hbm,
    table_ref,
    scatter_ref,
    block_ref,
    owner_ref,
    sunlit_ref,
    gases_ref,
    bins_ref,
    cosine_ref,
    ground_ref,
    order_ref,
    absorb_ref,
    albedo_ref,
    wanted_ref,
    copied,
    wide_buf,
):
    gas_count, levels, columns = gases_ref.shape
    points = table_ref.shape[0]
    bin_count = absorb_ref.shape[1]
    blocks = columns // LANES
    bin_row = gas_count * levels
    ray_row = bin_row + levels
    first_row = gas_count * BIN_ROWS
    peers = wanted_ref.shape[0]

    copies = [
        pltpu.make_async_copy(source, target, copied.at[place])
        for place, (source, target) in enumerate(
            (
                (sunlit_hbm, sunlit_ref),
                (order_hbm, order_ref),
                (absorb_hbm, absorb_ref),
                (scatter_hbm, albedo_ref),
                (cosine_hbm, cosine_ref),
                (ground_hbm, ground_ref),
                (bins_hbm, bins_ref),
                (gases_hbm, gases_ref),
            )
        )
    ]
    for copy in copies:
        copy.start()
    wide_buf[...] = jnp.zeros_like(wide_buf)
    copies[0].wait()
    for peer in range(peers):
        wanted_ref[peer] = jnp.full((1, 1), sunlit_ref[peer * sunlit_ref.shape[0] // peers], jnp.int32)
    sending = pltpu.make_async_copy(wanted_ref, wanted_hbm, copied.at[len(copies)])
    sending.start()
    for copy in copies[1:4]:
        copy.wait()

    square = (columns, columns)
    order = jnp.broadcast_to(order_ref[...], square)
    match = one_hot(order == lax.broadcasted_iota(jnp.int32, square, 0))
    place = lax.broadcasted_iota(jnp.int32, (ROWS, columns), 1)
    group = (place // per_peer).astype(jnp.float32).astype(jnp.bfloat16)
    owner_ref[...] = lax.dot_general(group, match, (((1,), (1,)), ((), ())), preferred_element_type=jnp.float32)

    for gas in range(gas_count):
        wide_buf[gas * BIN_ROWS : gas * BIN_ROWS + bin_count, :points] = absorb_ref[gas].astype(jnp.float32)
    wide_buf[first_row : first_row + bin_count, :points] = 0.5 * albedo_ref[...].astype(jnp.float32)
    turned = [
        jnp.transpose(wide_buf[i * LANES : (i + 1) * LANES])[:points].astype(jnp.bfloat16)
        for i in range(wide_buf.shape[0] // LANES)
    ]
    whole = jnp.concatenate(turned, axis=1)
    table_ref[...] = whole[:, :first_row]
    scatter_ref[...] = whole[:, first_row : first_row + BIN_ROWS]
    for copy in copies[4:]:
        copy.wait()

    for block in range(blocks):
        cols = slice(block * LANES, (block + 1) * LANES)
        for gas in range(gas_count):
            block_ref[block, gas * levels : (gas + 1) * levels] = gases_ref[gas, :, cols].astype(jnp.float32)
        block_ref[block, bin_row:ray_row] = bins_ref[:, cols].astype(jnp.float32)
    wide = (1, columns)
    cosines = cosine_ref[...].astype(jnp.float32).reshape(wide)
    grounds = ground_ref[...].astype(jnp.float32).reshape(wide)
    for block in range(blocks):
        cols = slice(block * LANES, (block + 1) * LANES)
        block_ref[block, ray_row : ray_row + ROWS] = jnp.broadcast_to(cosines[:, cols], (ROWS, LANES))
        block_ref[block, ray_row + ROWS : ray_row + 2 * ROWS] = jnp.broadcast_to(grounds[:, cols], (ROWS, LANES))
    sending.wait()


def heating_kernel(
    mass_hbm,
    table_ref,
    scatter_ref,
    block_ref,
    heat_ref,
    mass_ref,
    copied,
    optic_ref,
    up_buf,
    rise_buf,
    pass_buf,
    refl_buf,
    fall_buf,
    direct_buf,
    gain_buf,
    net_buf,
    warm_ref,
):
    levels, columns = heat_ref.shape
    points, gas_rows = table_ref.shape
    gas_count = gas_rows // BIN_ROWS
    half = points // HALVES
    vregs = half // ROWS
    blocks = columns // LANES
    bin_row = gas_count * levels
    ray_row = bin_row + levels
    mass_copy = pltpu.make_async_copy(mass_hbm, mass_ref, copied)
    mass_copy.start()

    def optical(slot, layer):
        parts = []
        shape = (BIN_ROWS, LANES)
        rows = lax.broadcasted_iota(jnp.int32, shape, 0).astype(jnp.float32).astype(jnp.bfloat16)
        one = jnp.ones(shape, jnp.bfloat16)
        zero = jnp.zeros(shape, jnp.bfloat16)
        selectors = []
        for near in (layer, layer + 1):
            place = bin_row + near
            bins = jnp.broadcast_to(block_ref[slot, place : place + 1, :], (PACK, LANES)).astype(jnp.bfloat16)
            bins = jnp.concatenate([bins] * (BIN_ROWS // PACK), axis=0)
            selectors.append(jnp.where(bins == rows, one, zero))
        for gas in range(gas_count):
            pair = []
            for near, selector in zip((layer, layer + 1), selectors):
                place = gas * levels + near
                amount = jnp.broadcast_to(block_ref[slot, place : place + 1, :], (PACK, LANES)).astype(jnp.bfloat16)
                pair.append(jnp.concatenate([amount] * (BIN_ROWS // PACK), axis=0) * selector)
            parts.append(jnp.concatenate(pair, axis=1))
        weighted = jnp.concatenate(parts, axis=0)
        selected = jnp.concatenate(selectors, axis=1)
        tau = jnp.dot(table_ref[...], weighted, preferred_element_type=jnp.float32)
        albedo = jnp.dot(scatter_ref[...], selected, preferred_element_type=jnp.float32)
        for near in range(2):
            cols = slice(near * LANES, (near + 1) * LANES)
            optic_ref[layer + near, :points] = tau[:, cols]
            optic_ref[layer + near, points:] = albedo[:, cols]

    def advance(first, part, cosine, slope):
        rows = slice(part * half, (part + 1) * half)
        half_rows = slice(points + part * half, points + (part + 1) * half)
        shape = (vregs, ROWS, LANES)
        if first > 0:
            refl = refl_buf[rows].reshape(shape)
            fall = fall_buf[rows].reshape(shape)
            direct = direct_buf[rows].reshape(shape)
        else:
            direct = jnp.broadcast_to(cosine[None], shape)
        for layer in range(first, first + STEP):
            tau = optic_ref[layer, rows].reshape(shape)
            half_albedo = optic_ref[layer, half_rows].reshape(shape)
            fading = jnp.exp2(tau * (-1.66 * LOG2E))
            passed = jnp.exp2(tau * slope)
            reflect = half_albedo * (1.0 - fading)
            transmit = fading + reflect
            below = direct * passed
            source = half_albedo * (direct - below)
            if layer == 0:
                up_buf[layer, rows] = transmit.reshape(half, LANES)
                rise_buf[layer, rows] = source.reshape(half, LANES)
                fall = source
                refl = reflect
            else:
                pass_buf[layer, rows] = (1.0 - refl).reshape(half, LANES)
                inverse = pl.reciprocal(1.0 - reflect * refl, approx=True)
                up = transmit * inverse
                rise = (reflect * fall + source) * inverse
                up_buf[layer, rows] = up.reshape(half, LANES)
                rise_buf[layer, rows] = rise.reshape(half, LANES)
                fall = source + transmit * (fall + refl * rise)
                refl = reflect + transmit * (refl * up)
            direct = below
            gain_buf[part, layer + 1] = jnp.sum(direct + fall, axis=0)
        refl_buf[rows] = refl.reshape(half, LANES)
        fall_buf[rows] = fall.reshape(half, LANES)
        direct_buf[rows] = direct.reshape(half, LANES)

    lead = range(0, STEP, 2)

    def column_block(block, carry):
        cosine = block_ref[block, ray_row : ray_row + ROWS]
        slope = (-LOG2E) / cosine
        for part in range(HALVES):
            gain_buf[part, 0] = cosine * float(vregs)
        for first in range(0, levels, STEP):
            coming = [layer for layer in range(first + STEP, first + 2 * STEP, 2) if layer < levels]
            for part in range(HALVES):
                advance(first, part, cosine, slope)
                for layer in coming[part * len(coming) // HALVES : (part + 1) * len(coming) // HALVES]:
                    optical(block, layer)

        following = jnp.minimum(block + 1, blocks - 1)
        for layer in lead:
            optical(following, layer)

        albedo = block_ref[block, ray_row + ROWS : ray_row + 2 * ROWS]
        shape = (points // ROWS, ROWS, LANES)
        refl = refl_buf[...].reshape(shape)
        arriving = (fall_buf[...] + direct_buf[...]).reshape(shape)
        rising = albedo * arriving * pl.reciprocal(1.0 - albedo * refl, approx=True)

        def total(level):
            summed = gain_buf[0, level]
            for part in range(1, HALVES):
                summed = summed + gain_buf[part, level]
            return summed

        net_buf[levels] = total(levels) - jnp.sum(rising * (1.0 - refl), axis=0)
        for layer in range(levels - 1, -1, -1):
            rising = up_buf[layer].reshape(shape) * rising + rise_buf[layer].reshape(shape)
            taken = rising if layer == 0 else rising * pass_buf[layer].reshape(shape)
            net_buf[layer] = total(layer) - jnp.sum(taken, axis=0)
        warm_ref[block] = jnp.sum(net_buf[:levels] - net_buf[1:], axis=1)
        return carry

    for layer in lead:
        optical(0, layer)
    lax.fori_loop(0, blocks, column_block, 0)
    mass_copy.wait()

    for block in range(blocks):
        cols = slice(block * LANES, (block + 1) * LANES)
        heat_ref[:, cols] = warm_ref[block] / mass_ref[:, cols].astype(jnp.float32)


def shade_kernel(heat_ref, owner_ref, flags_ref, out_ref):
    owner = owner_ref[...]
    lit = jnp.zeros_like(owner)
    for group in range(flags_ref.shape[0]):
        flag = jnp.broadcast_to(flags_ref[group].astype(jnp.float32), owner.shape)
        lit = jnp.where(owner == float(group), flag, lit)
    out_ref[...] = heat_ref[...] * lit[:1]


def local(
    gases,
    pressure_bin,
    layer_mass,
    cos_zenith,
    surface_albedo,
    column_order,
    sunlit,
    absorption,
    scattering,
):
    group_size = lax.axis_size("span")
    gas_count, levels, columns = gases.shape
    points, _, bins = absorption.shape
    rows = gas_count * levels + levels + PACK
    blocks = columns // LANES
    gas_rows = gas_count * BIN_ROWS
    hbm = pl.BlockSpec(memory_space=pltpu.HBM)
    vmem = pl.BlockSpec(memory_space=pltpu.VMEM)

    def pinned(*operands):
        return [pltpu.with_memory_space_constraint(operand, pltpu.HBM) for operand in operands]

    params = pltpu.CompilerParams(vmem_limit_bytes=VMEM_BYTES)
    wanted, table, scatter, block, owner = pl.pallas_call(
        functools.partial(prepare_kernel, columns // group_size),
        out_shape=(
            jax.ShapeDtypeStruct((group_size, 1, 1), sunlit.dtype),
            jax.ShapeDtypeStruct((points, gas_rows), jnp.bfloat16),
            jax.ShapeDtypeStruct((points, BIN_ROWS), jnp.bfloat16),
            jax.ShapeDtypeStruct((blocks, rows, LANES), jnp.float32),
            jax.ShapeDtypeStruct((ROWS, columns), jnp.float32),
        ),
        in_specs=[hbm] * 8,
        out_specs=(hbm, vmem, vmem, vmem, vmem),
        scratch_shapes=[
            pltpu.SMEM(sunlit.shape, sunlit.dtype),
            pltpu.VMEM(gases.shape, gases.dtype),
            pltpu.VMEM(pressure_bin.shape, pressure_bin.dtype),
            pltpu.VMEM(cos_zenith.shape, cos_zenith.dtype),
            pltpu.VMEM(surface_albedo.shape, surface_albedo.dtype),
            pltpu.VMEM((1, columns), column_order.dtype),
            pltpu.VMEM((gas_count, bins, points), absorption.dtype),
            pltpu.VMEM((bins, points), scattering.dtype),
            pltpu.VMEM((group_size, 1, 1), sunlit.dtype),
            pltpu.SemaphoreType.DMA((9,)),
            pltpu.VMEM((-(-(gas_rows + BIN_ROWS) // LANES) * LANES, LANES), jnp.float32),
        ],
        compiler_params=params,
    )(
        *pinned(
            sunlit,
            gases,
            pressure_bin,
            cos_zenith,
            surface_albedo,
            column_order.reshape(1, columns),
            jnp.transpose(absorption, (1, 2, 0)),
            jnp.transpose(scattering),
        )
    )
    flags = lax.all_to_all(wanted, "span", split_axis=0, concat_axis=0, tiled=True)
    field = pltpu.VMEM((levels, points, LANES), jnp.float32)
    state = pltpu.VMEM((points, LANES), jnp.float32)
    heat = pl.pallas_call(
        heating_kernel,
        out_shape=jax.ShapeDtypeStruct((levels, columns), jnp.float32),
        in_specs=[hbm, vmem, vmem, vmem],
        out_specs=vmem,
        scratch_shapes=[
            pltpu.VMEM(layer_mass.shape, layer_mass.dtype),
            pltpu.SemaphoreType.DMA(()),
            pltpu.VMEM((levels, 2 * points, LANES), jnp.float32),
            field,
            field,
            field,
            state,
            state,
            state,
            pltpu.VMEM((HALVES, levels + 1, ROWS, LANES), jnp.float32),
            pltpu.VMEM((levels + 1, ROWS, LANES), jnp.float32),
            pltpu.VMEM((blocks, levels, LANES), jnp.float32),
        ],
        compiler_params=params,
        cost_estimate=pl.CostEstimate(
            flops=40 * levels * points * columns, bytes_accessed=1 << 20, transcendentals=3 * levels * points * columns
        ),
    )(*pinned(layer_mass), table, scatter, block)
    return pl.pallas_call(
        shade_kernel,
        out_shape=jax.ShapeDtypeStruct((levels, columns), heat.dtype),
        in_specs=[vmem] * 3,
        out_specs=vmem,
        compiler_params=params,
    )(heat, owner, flags)


def solution(mesh):
    placed = (
        P(None, None, ("band", "span")),
        P(None, ("band", "span")),
        P(None, ("band", "span")),
        P(("band", "span")),
        P(("band", "span")),
        P(("band", "span")),
        P(("band", "span")),
        P(),
        P(),
    )
    return jax.shard_map(
        local, mesh=mesh, in_specs=placed, out_specs=P(None, ("band", "span")), check_vma=False
    )
```

```python
import functools
import math

import jax
import jax.numpy as jnp
from jax import lax
from jax.experimental import pallas as pl
from jax.experimental.pallas import tpu as pltpu
from jax.sharding import PartitionSpec as P

LANES = 128
ROWS = 8
PACK = 16
STEP = 8
HALVES = 1
BIN_ROWS = 64
LOG2E = math.log2(math.e)
VMEM_BYTES = 24 * 1024 * 1024


def one_hot(hit):
    return jnp.where(hit, 1.0, 0.0).astype(jnp.bfloat16)


def prepare_kernel(
    per_peer,
    sunlit_hbm,
    gases_hbm,
    bins_hbm,
    cosine_hbm,
    ground_hbm,
    order_hbm,
    absorb_hbm,
    scatter_hbm,
    wanted_hbm,
    table_ref,
    scatter_ref,
    block_ref,
    owner_ref,
    sunlit_ref,
    gases_ref,
    bins_ref,
    cosine_ref,
    ground_ref,
    order_ref,
    absorb_ref,
    albedo_ref,
    wanted_ref,
    copied,
    wide_buf,
):
    gas_count, levels, columns = gases_ref.shape
    points = table_ref.shape[0]
    bin_count = absorb_ref.shape[1]
    blocks = columns // LANES
    bin_row = gas_count * levels
    ray_row = bin_row + levels
    first_row = gas_count * BIN_ROWS
    peers = wanted_ref.shape[0]

    copies = [
        pltpu.make_async_copy(source, target, copied.at[place])
        for place, (source, target) in enumerate(
            (
                (sunlit_hbm, sunlit_ref),
                (order_hbm, order_ref),
                (absorb_hbm, absorb_ref),
                (scatter_hbm, albedo_ref),
                (cosine_hbm, cosine_ref),
                (ground_hbm, ground_ref),
                (bins_hbm, bins_ref),
                (gases_hbm, gases_ref),
            )
        )
    ]
    for copy in copies:
        copy.start()
    wide_buf[...] = jnp.zeros_like(wide_buf)
    copies[0].wait()
    for peer in range(peers):
        wanted_ref[peer] = jnp.full((1, 1), sunlit_ref[peer * sunlit_ref.shape[0] // peers], jnp.int32)
    sending = pltpu.make_async_copy(wanted_ref, wanted_hbm, copied.at[len(copies)])
    sending.start()
    for copy in copies[1:4]:
        copy.wait()

    square = (columns, columns)
    order = jnp.broadcast_to(order_ref[...], square)
    match = one_hot(order == lax.broadcasted_iota(jnp.int32, square, 0))
    place = lax.broadcasted_iota(jnp.int32, (ROWS, columns), 1)
    group = (place // per_peer).astype(jnp.float32).astype(jnp.bfloat16)
    owner_ref[...] = lax.dot_general(group, match, (((1,), (1,)), ((), ())), preferred_element_type=jnp.float32)

    for gas in range(gas_count):
        wide_buf[gas * BIN_ROWS : gas * BIN_ROWS + bin_count, :points] = absorb_ref[gas].astype(jnp.float32)
    wide_buf[first_row : first_row + bin_count, :points] = 0.5 * albedo_ref[...].astype(jnp.float32)
    turned = [
        jnp.transpose(wide_buf[i * LANES : (i + 1) * LANES])[:points].astype(jnp.bfloat16)
        for i in range(wide_buf.shape[0] // LANES)
    ]
    whole = jnp.concatenate(turned, axis=1)
    table_ref[...] = whole[:, :first_row]
    scatter_ref[...] = whole[:, first_row : first_row + BIN_ROWS]
    for copy in copies[4:]:
        copy.wait()

    for block in range(blocks):
        cols = slice(block * LANES, (block + 1) * LANES)
        for gas in range(gas_count):
            block_ref[block, gas * levels : (gas + 1) * levels] = gases_ref[gas, :, cols].astype(jnp.float32)
        block_ref[block, bin_row:ray_row] = bins_ref[:, cols].astype(jnp.float32)
    wide = (1, columns)
    cosines = cosine_ref[...].astype(jnp.float32).reshape(wide)
    grounds = ground_ref[...].astype(jnp.float32).reshape(wide)
    for block in range(blocks):
        cols = slice(block * LANES, (block + 1) * LANES)
        block_ref[block, ray_row : ray_row + ROWS] = jnp.broadcast_to(cosines[:, cols], (ROWS, LANES))
        block_ref[block, ray_row + ROWS : ray_row + 2 * ROWS] = jnp.broadcast_to(grounds[:, cols], (ROWS, LANES))
    sending.wait()


def heating_kernel(
    mass_hbm,
    table_ref,
    scatter_ref,
    block_ref,
    heat_ref,
    mass_ref,
    copied,
    optic_ref,
    up_buf,
    rise_buf,
    pass_buf,
    refl_buf,
    fall_buf,
    direct_buf,
    gain_buf,
    net_buf,
    warm_ref,
):
    levels, columns = heat_ref.shape
    points, gas_rows = table_ref.shape
    gas_count = gas_rows // BIN_ROWS
    half = points // HALVES
    vregs = half // ROWS
    blocks = columns // LANES
    bin_row = gas_count * levels
    ray_row = bin_row + levels
    mass_copy = pltpu.make_async_copy(mass_hbm, mass_ref, copied)
    mass_copy.start()

    def optical(slot, layer):
        parts = []
        shape = (BIN_ROWS, LANES)
        rows = lax.broadcasted_iota(jnp.int32, shape, 0).astype(jnp.float32).astype(jnp.bfloat16)
        one = jnp.ones(shape, jnp.bfloat16)
        zero = jnp.zeros(shape, jnp.bfloat16)
        selectors = []
        for near in (layer, layer + 1):
            place = bin_row + near
            bins = jnp.broadcast_to(block_ref[slot, place : place + 1, :], (PACK, LANES)).astype(jnp.bfloat16)
            bins = jnp.concatenate([bins] * (BIN_ROWS // PACK), axis=0)
            selectors.append(jnp.where(bins == rows, one, zero))
        for gas in range(gas_count):
            pair = []
            for near, selector in zip((layer, layer + 1), selectors):
                place = gas * levels + near
                amount = jnp.broadcast_to(block_ref[slot, place : place + 1, :], (PACK, LANES)).astype(jnp.bfloat16)
                pair.append(jnp.concatenate([amount] * (BIN_ROWS // PACK), axis=0) * selector)
            parts.append(jnp.concatenate(pair, axis=1))
        weighted = jnp.concatenate(parts, axis=0)
        selected = jnp.concatenate(selectors, axis=1)
        tau = jnp.dot(table_ref[...], weighted, preferred_element_type=jnp.float32)
        albedo = jnp.dot(scatter_ref[...], selected, preferred_element_type=jnp.float32)
        for near in range(2):
            cols = slice(near * LANES, (near + 1) * LANES)
            optic_ref[layer + near, :points] = tau[:, cols]
            optic_ref[layer + near, points:] = albedo[:, cols]

    def advance(first, part, cosine, slope):
        rows = slice(part * half, (part + 1) * half)
        half_rows = slice(points + part * half, points + (part + 1) * half)
        shape = (vregs, ROWS, LANES)
        if first > 0:
            refl = refl_buf[rows].reshape(shape)
            fall = fall_buf[rows].reshape(shape)
            direct = direct_buf[rows].reshape(shape)
        else:
            direct = jnp.broadcast_to(cosine[None], shape)
        for layer in range(first, first + STEP):
            tau = optic_ref[layer, rows].reshape(shape)
            half_albedo = optic_ref[layer, half_rows].reshape(shape)
            fading = jnp.exp2(tau * (-1.66 * LOG2E))
            passed = jnp.exp2(tau * slope)
            reflect = half_albedo * (1.0 - fading)
            transmit = fading + reflect
            below = direct * passed
            source = half_albedo * (direct - below)
            if layer == 0:
                up_buf[layer, rows] = transmit.reshape(half, LANES)
                rise_buf[layer, rows] = source.reshape(half, LANES)
                fall = source
                refl = reflect
            else:
                pass_buf[layer, rows] = (1.0 - refl).reshape(half, LANES)
                inverse = pl.reciprocal(1.0 - reflect * refl, approx=True)
                up = transmit * inverse
                rise = (reflect * fall + source) * inverse
                up_buf[layer, rows] = up.reshape(half, LANES)
                rise_buf[layer, rows] = rise.reshape(half, LANES)
                fall = source + transmit * (fall + refl * rise)
                refl = reflect + transmit * (refl * up)
            direct = below
            gain_buf[part, layer + 1] = jnp.sum(direct + fall, axis=0)
        refl_buf[rows] = refl.reshape(half, LANES)
        fall_buf[rows] = fall.reshape(half, LANES)
        direct_buf[rows] = direct.reshape(half, LANES)

    lead = range(0, STEP, 2)

    def column_block(block, carry):
        cosine = block_ref[block, ray_row : ray_row + ROWS]
        slope = (-LOG2E) / cosine
        for part in range(HALVES):
            gain_buf[part, 0] = cosine * float(vregs)
        for first in range(0, levels, STEP):
            coming = [layer for layer in range(first + STEP, first + 2 * STEP, 2) if layer < levels]
            for part in range(HALVES):
                advance(first, part, cosine, slope)
                for layer in coming[part * len(coming) // HALVES : (part + 1) * len(coming) // HALVES]:
                    optical(block, layer)

        following = jnp.minimum(block + 1, blocks - 1)
        for layer in lead:
            optical(following, layer)

        albedo = block_ref[block, ray_row + ROWS : ray_row + 2 * ROWS]
        shape = (points // ROWS, ROWS, LANES)
        refl = refl_buf[...].reshape(shape)
        arriving = (fall_buf[...] + direct_buf[...]).reshape(shape)
        rising = albedo * arriving * pl.reciprocal(1.0 - albedo * refl, approx=True)

        def total(level):
            summed = gain_buf[0, level]
            for part in range(1, HALVES):
                summed = summed + gain_buf[part, level]
            return summed

        net_buf[levels] = total(levels) - jnp.sum(rising * (1.0 - refl), axis=0)
        for layer in range(levels - 1, -1, -1):
            rising = up_buf[layer].reshape(shape) * rising + rise_buf[layer].reshape(shape)
            taken = rising if layer == 0 else rising * pass_buf[layer].reshape(shape)
            net_buf[layer] = total(layer) - jnp.sum(taken, axis=0)
        warm_ref[block] = jnp.sum(net_buf[:levels] - net_buf[1:], axis=1)
        return carry

    for layer in lead:
        optical(0, layer)
    lax.fori_loop(0, blocks, column_block, 0)
    mass_copy.wait()

    for block in range(blocks):
        cols = slice(block * LANES, (block + 1) * LANES)
        heat_ref[:, cols] = warm_ref[block] / mass_ref[:, cols].astype(jnp.float32)


def shade_kernel(heat_ref, owner_ref, flags_ref, out_ref):
    owner = owner_ref[...]
    lit = jnp.zeros_like(owner)
    for group in range(flags_ref.shape[0]):
        flag = jnp.broadcast_to(flags_ref[group].astype(jnp.float32), owner.shape)
        lit = jnp.where(owner == float(group), flag, lit)
    out_ref[...] = heat_ref[...] * lit[:1]


def local(
    gases,
    pressure_bin,
    layer_mass,
    cos_zenith,
    surface_albedo,
    column_order,
    sunlit,
    absorption,
    scattering,
):
    group_size = lax.axis_size("span")
    gas_count, levels, columns = gases.shape
    points, _, bins = absorption.shape
    rows = gas_count * levels + levels + PACK
    blocks = columns // LANES
    gas_rows = gas_count * BIN_ROWS
    hbm = pl.BlockSpec(memory_space=pltpu.HBM)
    vmem = pl.BlockSpec(memory_space=pltpu.VMEM)

    def pinned(*operands):
        return [pltpu.with_memory_space_constraint(operand, pltpu.HBM) for operand in operands]

    params = pltpu.CompilerParams(vmem_limit_bytes=VMEM_BYTES)
    wanted, table, scatter, block, owner = pl.pallas_call(
        functools.partial(prepare_kernel, columns // group_size),
        out_shape=(
            jax.ShapeDtypeStruct((group_size, 1, 1), sunlit.dtype),
            jax.ShapeDtypeStruct((points, gas_rows), jnp.bfloat16),
            jax.ShapeDtypeStruct((points, BIN_ROWS), jnp.bfloat16),
            jax.ShapeDtypeStruct((blocks, rows, LANES), jnp.float32),
            jax.ShapeDtypeStruct((ROWS, columns), jnp.float32),
        ),
        in_specs=[hbm] * 8,
        out_specs=(hbm, vmem, vmem, vmem, vmem),
        scratch_shapes=[
            pltpu.SMEM(sunlit.shape, sunlit.dtype),
            pltpu.VMEM(gases.shape, gases.dtype),
            pltpu.VMEM(pressure_bin.shape, pressure_bin.dtype),
            pltpu.VMEM(cos_zenith.shape, cos_zenith.dtype),
            pltpu.VMEM(surface_albedo.shape, surface_albedo.dtype),
            pltpu.VMEM((1, columns), column_order.dtype),
            pltpu.VMEM((gas_count, bins, points), absorption.dtype),
            pltpu.VMEM((bins, points), scattering.dtype),
            pltpu.VMEM((group_size, 1, 1), sunlit.dtype),
            pltpu.SemaphoreType.DMA((9,)),
            pltpu.VMEM((-(-(gas_rows + BIN_ROWS) // LANES) * LANES, LANES), jnp.float32),
        ],
        compiler_params=params,
    )(
        *pinned(
            sunlit,
            gases,
            pressure_bin,
            cos_zenith,
            surface_albedo,
            column_order.reshape(1, columns),
            jnp.transpose(absorption, (1, 2, 0)),
            jnp.transpose(scattering),
        )
    )
    flags = lax.all_to_all(wanted, "span", split_axis=0, concat_axis=0, tiled=True)
    field = pltpu.VMEM((levels, points, LANES), jnp.float32)
    state = pltpu.VMEM((points, LANES), jnp.float32)
    heat = pl.pallas_call(
        heating_kernel,
        out_shape=jax.ShapeDtypeStruct((levels, columns), jnp.float32),
        in_specs=[hbm, vmem, vmem, vmem],
        out_specs=vmem,
        scratch_shapes=[
            pltpu.VMEM(layer_mass.shape, layer_mass.dtype),
            pltpu.SemaphoreType.DMA(()),
            pltpu.VMEM((levels, 2 * points, LANES), jnp.float32),
            field,
            field,
            field,
            state,
            state,
            state,
            pltpu.VMEM((HALVES, levels + 1, ROWS, LANES), jnp.float32),
            pltpu.VMEM((levels + 1, ROWS, LANES), jnp.float32),
            pltpu.VMEM((blocks, levels, LANES), jnp.float32),
        ],
        compiler_params=params,
        cost_estimate=pl.CostEstimate(
            flops=40 * levels * points * columns, bytes_accessed=1 << 20, transcendentals=3 * levels * points * columns
        ),
    )(*pinned(layer_mass), table, scatter, block)
    return pl.pallas_call(
        shade_kernel,
        out_shape=jax.ShapeDtypeStruct((levels, columns), heat.dtype),
        in_specs=[vmem] * 3,
        out_specs=vmem,
        compiler_params=params,
    )(heat, owner, flags)


def solution(mesh):
    placed = (
        P(None, None, ("band", "span")),
        P(None, ("band", "span")),
        P(None, ("band", "span")),
        P(("band", "span")),
        P(("band", "span")),
        P(("band", "span")),
        P(("band", "span")),
        P(),
        P(),
    )
    return jax.shard_map(
        local, mesh=mesh, in_specs=placed, out_specs=P(None, ("band", "span")), check_vma=False
    )
```
